512 devices in a mesh: wide: 16 (over y, core), narrow: 32 (over x, z).
Axes of the slice: x: 4, y: 8, z: 8, core: 2. Of those that a mesh axis runs over, the one named last changes fastest.
Arguments:
- modes: float32 [2, 512, 512, 128], P(None, 'narrow', 'wide'), may hold values from -6 to 6
- to_eigen: float32 [128, 128], replicated, may hold values from -0.2 to 1.4
- from_eigen: float32 [128, 128], replicated, may hold values from -0.2 to 1.4
- eigenvalues: float32 [128], replicated, may hold values from 1 to 20000
- bins_owned: int32 [16, 32], P('wide'), may hold values from 1 to 54, 576 in all within a row
- bed_planes: int32 [9216], P('wide'), may hold values from 1 to 4
- particle_position: float32 [16, 32, 2, 54, 128], P('wide', 'narrow'), may hold values from 0 to 8
- particle_velocity: float32 [16, 32, 2, 54, 128], P('wide', 'narrow'), may hold values from -5 to 5
- particle_size: float32 [16, 32, 54, 128], P('wide', 'narrow'), may hold values from 0.5 to 2
Outputs:
- new_modes: float32 [2, 512, 512, 128], P(None, 'narrow', 'wide')
- lifted: float32 [16, 32, 54, 128], P('wide', 'narrow')
- particle_push: float32 [16, 32, 2, 54, 128], P('wide', 'narrow')
The draws below stay inside these ranges and needn't reach their ends.
Inputs may be any that keep to these rules, and one draw needn't show every extreme that they name: `bins_owned`: row w lists, for each narrow index in order, how many consecutive bins of column w it owns; each row sums to 576 and its largest entry is 54.
All inputs are finite; a program needn't handle non-finite values.
Results may differ from the reference program's by a relative error of at most 0.0003.
Values sent between devices are 32-bit elements; how exact they have to be, the bound alone decides.
No kernel may reach another device: no remote copies, remote signals or barrier semaphores. Data moves between devices by JAX's collectives and lax.ppermute only.
A program may use at most 128 MiB of HBM per device.

```python
import math
import jax
import jax.numpy as jnp
import numpy as np
from jax import lax

NX = 768
NZ = 768
NY = 128
KX = 512
KZ = 512
COMPS = 2
BED = 4
BIN = 8
PPB = 128
BINS_COL = 576
MOST = 54
N_WIDE = 16
N_NARROW = 32


def dominant(key, noise_part):
    diagonal = jax.random.uniform(key, (NY,), jnp.float32, 0.8, 1.2)
    return jnp.eye(NY, dtype=jnp.float32) * diagonal[None, :] + noise_part * (0.3 / math.sqrt(NY))


def draw_to_eigen(key, part):
    key = jax.random.fold_in(key, 11)
    key_diag, key_noise = jax.random.split(key)
    noise_part = jnp.clip(jax.random.normal(key_noise, (NY, NY), jnp.float32), -4.0, 4.0)
    return dominant(key_diag, noise_part)


def draw_from_eigen(key, part):
    key = jax.random.fold_in(key, 23)
    key_diag, key_noise = jax.random.split(key)
    noise_part = jnp.clip(jax.random.normal(key_noise, (NY, NY), jnp.float32), -4.0, 4.0)
    return dominant(key_diag, noise_part)


def touch_ends(entries, key, least, high):
    dims = entries.shape
    spot = [jax.random.randint(jax.random.fold_in(key, axis), (), 0, dims[axis]) for axis in range(len(dims))]
    entries = entries.at[tuple(spot)].set(least)
    longest = dims.index(max(dims))
    spot[longest] = (spot[longest] + 1) % dims[longest]
    return entries.at[tuple(spot)].set(high)


def level_of(own_key, extent, shards, smallest, largest):
    level, own = 1.0, jax.random.fold_in(own_key, 6)
    for position, blocks in shards:
        heights = jnp.exp(jax.random.uniform(jax.random.fold_in(own, position), (blocks,), jnp.float32, smallest / len(shards), largest / len(shards)))
        level = level * jnp.repeat(heights, extent[position] // blocks).reshape([-1 if axis == position else 1 for axis in range(len(extent))])
    return level


def length_profile(count, total, limit, lean):
    portions = [(1 << 20) // math.isqrt(standing ** lean) + 1 for standing in range(2, count + 1)]
    surplus, given = total - limit - (count - 1), [1] * (count - 1)
    while surplus > 0:
        movable = [i for i in range(count - 1) if given[i] < limit]
        pool, left = sum([portions[i] for i in movable]), surplus
        for i in movable:
            addition = min(limit - given[i], max(1, left * portions[i] // pool), surplus)
            given[i] = given[i] + addition
            surplus = surplus - addition
    return np.array([limit] + given)


def ragged(key, amount, total, most, lean):
    if amount == 2:
        one = jax.random.randint(key, (), max(1, total - most), min(most, total - 1) + 1)
        return jnp.stack([one, total - one])
    tallies = jnp.asarray(length_profile(amount, total, most, lean), jnp.int32)
    twos = (amount - 1) // 2
    giver, sink = tallies[1:1 + 2 * twos:2], tallies[2:2 + 2 * twos:2]
    margin = jnp.minimum(giver - 1, most - sink)
    moved = jax.random.randint(jax.random.fold_in(key, 1), (twos,), 0, 1 << 20) % (margin + 1)
    tallies = tallies.at[1:1 + 2 * twos:2].set(giver - moved).at[2:2 + 2 * twos:2].set(sink + moved)
    return tallies[jax.random.permutation(jax.random.fold_in(key, 2), amount)]


def scatter_about(key, dims, deviation, reach, cuts=(), held_as=jnp.bfloat16):
    values = jax.random.normal(key, dims, jnp.float32) * deviation
    if len(cuts) > 0:
        values = level_of(key, dims, cuts, -0.22, 0.18) * values
    return jnp.clip(values, min=-reach, max=reach).astype(held_as)


def setup_inputs(seed: int = 0) -> dict:
    keys = jax.random.split(jax.random.key(seed), 10)
    modes = scatter_about(keys[0], (COMPS, KX, KZ, NY), 1.0, 6.0, ((1, 32), (2, 16)), jnp.float32)
    to_eigen = draw_to_eigen(jax.random.fold_in(keys[9], 71), 0)
    from_eigen = draw_from_eigen(jax.random.fold_in(keys[9], 71), 0)
    eigenvalues = jnp.clip(jnp.exp(jax.random.uniform(keys[3], (NY,), jnp.float32, math.log(1.0), math.log(20000.0))), 1.0, 20000.0)
    bins_owned = jax.vmap(lambda own: ragged(own, N_NARROW, BINS_COL, MOST, 2))(jax.random.split(keys[4], N_WIDE)).reshape((N_WIDE, N_NARROW)).astype(jnp.int32)
    bed_planes = touch_ends(jax.random.randint(keys[5], (N_WIDE * BINS_COL,), 1, BED + 1), jax.random.fold_in(keys[5], 1), 1, BED).astype(jnp.int32)
    particle_position = jnp.clip(8.0 * jax.random.uniform(keys[6], (N_WIDE, N_NARROW, 2, MOST, PPB), jnp.float32) ** level_of(keys[6], (N_WIDE, N_NARROW, 2, MOST, PPB), ((0, 16), (1, 32)), -0.2, 0.2), 0.0, 8.0)
    particle_velocity = scatter_about(keys[7], (N_WIDE, N_NARROW, COMPS, MOST, PPB), 1.0, 5.0, ((0, 16), (1, 32)), jnp.float32)
    particle_size = jnp.clip(jnp.exp(math.log(2.0) - 1.3862944 * jax.random.uniform(keys[8], (N_WIDE, N_NARROW, MOST, PPB), jnp.float32) ** level_of(keys[8], (N_WIDE, N_NARROW, MOST, PPB), ((0, 16), (1, 32)), -0.2, 0.2)), 0.5, 2.0)
    return {"modes": modes, "to_eigen": to_eigen, "from_eigen": from_eigen, "eigenvalues": eigenvalues, "bins_owned": bins_owned, "bed_planes": bed_planes, "particle_position": particle_position, "particle_velocity": particle_velocity, "particle_size": particle_size}


highest = lax.Precision.HIGHEST
time_step = 0.003
viscous = 0.0001
reaction = 0.25

def basis_table(mode_count, points):
    mode_index = jnp.arange(mode_count, dtype=jnp.int32)[:, None]
    point_index = jnp.arange(points, dtype=jnp.int32)[None, :]
    wavenumber = (mode_index + 1) // 2
    phases = (wavenumber * point_index % points).astype(jnp.float32) * (2.0 * math.pi / points)
    factor = math.sqrt(2.0 / points)
    result = jnp.where(mode_index % 2 == 1, factor * jnp.cos(phases), factor * jnp.sin(phases))
    return jnp.where(mode_index == 0, 1.0 / math.sqrt(points), result).astype(jnp.float32)

def slope_table(points, mode_count):
    point_index = jnp.arange(points, dtype=jnp.int32)[:, None]
    mode_index = jnp.arange(mode_count, dtype=jnp.int32)[None, :]
    wavenumber = (mode_index + 1) // 2
    phases = (wavenumber * point_index % points).astype(jnp.float32) * (2.0 * math.pi / points)
    slopes = wavenumber.astype(jnp.float32) * math.sqrt(2.0 / points)
    result = jnp.where(mode_index % 2 == 1, slopes * jnp.sin(phases), -slopes * jnp.cos(phases))
    return jnp.where(mode_index == 0, 0.0, result).astype(jnp.float32)

def forward_table(points, mode_count):
    return jnp.concatenate([-time_step * slope_table(points, mode_count), basis_table(mode_count, points).T], axis=0)

def plane_mean(block, depths):
    inside = jnp.arange(block.shape[2], dtype=jnp.int32)[None, :] < depths[:, None]
    summed = lax.optimization_barrier(jnp.sum(jnp.where(inside[:, None, :, None], block, 0.0), axis=2))
    return summed / depths.astype(jnp.float32)[:, None, None]

def particle_terms(positions, velocities, diameters, cell_grid, active):
    centre = jnp.arange(cell_grid.shape[2], dtype=jnp.int32).astype(jnp.float32) + 0.5
    weight_x = jnp.exp(-0.5 * (positions[0][..., None] - centre) ** 2)
    weight_z = jnp.exp(-0.5 * (positions[1][..., None] - centre) ** 2)
    totals = lax.optimization_barrier(jnp.sum(weight_x, axis=-1)) * lax.optimization_barrier(jnp.sum(weight_z, axis=-1))
    partial_value = jnp.einsum('spi,scik->cspk', weight_x, cell_grid, precision=highest)
    felt_velocity = lax.optimization_barrier(jnp.sum(partial_value * weight_z[None], axis=-1)) / totals[None]
    relative = felt_velocity - velocities
    magnitude = jnp.sqrt(relative[0] ** 2 + relative[1] ** 2 + 0.1)
    squared = diameters * diameters
    drag_force = 0.5 * squared[None] * relative * magnitude[None]
    lift_force = 0.5 * squared * (felt_velocity[0] ** 2 + felt_velocity[1] ** 2)
    alive_mask = active[:, None]
    lifted = jnp.where(alive_mask, jax.nn.sigmoid((lift_force - 0.5 * squared * diameters) / 0.25), 0.0)
    particle_push = jnp.where(alive_mask[None], drag_force * (1.0 + lifted[None]), 0.0)
    share_part = -reaction * particle_push / totals[None]
    cell_force = jnp.einsum('spi,cspk->csik', weight_x, weight_z[None] * share_part[..., None], precision=highest)
    owned_rows = cell_force.transpose(1, 0, 2, 3).reshape(cell_force.shape[1], -1)
    return (lifted, particle_push, owned_rows)

def reference(modes, to_eigen, from_eigen, eigenvalues, bins_owned, bed_planes, particle_position, particle_velocity, particle_size):
    along_x = basis_table(KX, NX)
    along_z = basis_table(KZ, NZ)
    forward_z = forward_table(NZ, KZ)
    x_bins = NX // N_WIDE // BIN
    z_bins = NZ // BIN
    cell_count = BIN * BIN

    def plane_velocity(plane_at):
        mode_sheet = lax.dynamic_index_in_dim(modes, plane_at, 3, keepdims=False)
        partial_value = jnp.einsum('cab,ax->cxb', mode_sheet, along_x, precision=highest)
        return jnp.einsum('cxb,bz->cxz', partial_value, along_z, precision=highest)
    bottom = lax.map(plane_velocity, jnp.arange(BED, dtype=jnp.int32))
    bottom_slab = bottom.reshape(BED, COMPS, N_WIDE, x_bins, BIN, z_bins, BIN).transpose(2, 3, 5, 1, 0, 4, 6)
    bottom_slab = bottom_slab.reshape(N_WIDE * BINS_COL, COMPS, BED, cell_count)
    near_mean = plane_mean(bottom_slab, bed_planes).reshape(N_WIDE, BINS_COL, COMPS, cell_count)
    first_bins = jnp.cumsum(bins_owned, axis=1) - bins_owned
    slot_index = jnp.arange(MOST, dtype=jnp.int32)
    bin_index = first_bins[:, :, None] + slot_index
    active = slot_index < bins_owned[:, :, None]
    safe_index = jnp.minimum(bin_index, BINS_COL - 1)
    column_index = jnp.arange(N_WIDE, dtype=jnp.int32)[:, None, None]
    cell_grid = near_mean[column_index, safe_index].reshape(N_WIDE, N_NARROW, MOST, COMPS, BIN, BIN)
    lifted, particle_push, owned_rows = jax.vmap(jax.vmap(particle_terms))(particle_position, particle_velocity, particle_size, cell_grid, active)
    bed_force = jnp.zeros((N_WIDE, BINS_COL, COMPS * cell_count), jnp.float32)
    bed_force = bed_force.at[column_index, safe_index].add(owned_rows)
    depths = bed_planes.reshape(N_WIDE, BINS_COL)
    inside = jnp.arange(BED, dtype=jnp.int32)[None, None, :] < depths[:, :, None]
    spread_force = bed_force.reshape(N_WIDE, BINS_COL, COMPS, 1, cell_count) / depths.astype(jnp.float32)[:, :, None, None, None]
    forcing = jnp.where(inside[:, :, None, :, None], spread_force, 0.0)
    forcing = forcing.reshape(N_WIDE, x_bins, z_bins, COMPS, BED, BIN, BIN).transpose(4, 3, 0, 1, 5, 2, 6)
    forcing = forcing.reshape(BED, COMPS, NX, NZ)

    def plane_terms(plane_at):
        velocity = plane_velocity(plane_at)
        product = velocity[1][None] * velocity
        near_force = lax.dynamic_index_in_dim(forcing, jnp.minimum(plane_at, BED - 1), 0, keepdims=False)
        pushed = jnp.where(plane_at < BED, near_force, 0.0)
        joined = jnp.concatenate([product, pushed], axis=2)
        inner_sum = jnp.einsum('cxz,zb->cxb', joined, forward_z, precision=highest)
        return jnp.einsum('cxb,ax->cab', inner_sum, along_x, precision=highest)
    spectral_terms = lax.map(plane_terms, jnp.arange(NY, dtype=jnp.int32))
    right_side = modes + spectral_terms.transpose(1, 2, 3, 0)
    wave_x = ((jnp.arange(KX, dtype=jnp.int32) + 1) // 2).astype(jnp.float32)
    wave_z = ((jnp.arange(KZ, dtype=jnp.int32) + 1) // 2).astype(jnp.float32)
    divisor = 1.0 + viscous * (wave_x[:, None, None] ** 2 + wave_z[None, :, None] ** 2 + eigenvalues[None, None, :])
    eigen_part = jnp.einsum('caby,jy->cabj', right_side, from_eigen, precision=highest)
    new_modes = jnp.einsum('cabj,yj->caby', eigen_part / divisor, to_eigen, precision=highest)
    return (new_modes, lifted, particle_push)
```

```python
import math

import jax
import jax.numpy as jnp
import ml_dtypes
import numpy as np
from jax import lax
from jax.experimental import pallas as pl
from jax.experimental.pallas import tpu as pltpu
from jax.sharding import PartitionSpec as P

NX = 768
NZ = 768
KX = 512
KZ = 512
BED = 4
BIN = 8
COL = 48
ZB = NZ // BIN
LANES = 128

highest = lax.Precision.HIGHEST
time_step = 0.003
viscous = 0.0001
reaction = 0.25
f32 = jnp.float32
bf16 = jnp.bfloat16


def basis_np(mode_count, points):
    m = np.arange(mode_count)[:, None]
    j = np.arange(points)[None, :]
    k = (m + 1) // 2
    angle = (k * j % points) * (2.0 * math.pi / points)
    table = math.sqrt(2.0 / points) * np.where(m % 2 == 1, np.cos(angle), np.sin(angle))
    return np.where(m == 0, 1.0 / math.sqrt(points), table)


def slope_np(points, mode_count):
    j = np.arange(points)[:, None]
    m = np.arange(mode_count)[None, :]
    k = (m + 1) // 2
    angle = (k * j % points) * (2.0 * math.pi / points)
    return k * math.sqrt(2.0 / points) * np.where(m % 2 == 1, np.sin(angle), -np.cos(angle))


def split_np(table):
    table = np.ascontiguousarray(table).astype(np.float32)
    high = table.astype(ml_dtypes.bfloat16)
    low = (table - high.astype(np.float32)).astype(ml_dtypes.bfloat16)
    return high, low


def tables():
    basis = basis_np(KX, NX)
    n, kxh, g = np.meshgrid(np.arange(32), np.arange(2), np.arange(4), indexing="ij")
    even = (n * 16 + g * 4 + kxh * 2).reshape(-1)
    half = (np.arange(16)[:, None] * COL + np.arange(24)[None, :]).reshape(-1)
    nx, w, k8 = np.meshgrid(np.arange(4), np.arange(16), np.arange(8), indexing="ij")
    span = (w * 32 + nx * 8 + k8).reshape(-1)
    return {
        "x": split_np(basis.T),
        "x_bed": split_np(np.concatenate([basis.T[:, even], basis.T[:, even + 1]], axis=0)),
        "z": split_np(basis),
        "slope": split_np(-time_step * slope_np(NZ, KZ)),
        "z_bed": split_np(basis.T[:, span]),
        "z_bed_back": split_np(basis[span, :]),
        "x_bed_back": split_np(
            np.concatenate(
                [basis[np.ix_(even + bit, half + 24 * part)] for bit in (0, 1) for part in (0, 1)],
                axis=0,
            )
        ),
    }


def halves(value):
    high = value.astype(bf16)
    return high, (value - high.astype(f32)).astype(bf16)


def mul(a, b, dims=(((1,), (0,)), ((), ()))):
    def one(p, q):
        return lax.dot_general(p, q, dims, preferred_element_type=f32)

    return one(a[0], b[0]) + (one(a[0], b[1]) + one(a[1], b[0]))


def lane_bit(shape, bit):
    return (lax.broadcasted_iota(jnp.int32, shape, len(shape) - 1) & bit) != 0


def turn(value, shift):
    return pltpu.roll(value, shift % LANES, value.ndim - 1)


def swap(rows, bits):
    rows = list(rows)
    step = len(rows) // 2
    for bit in bits:
        upper = lane_bit(rows[0].shape, bit)
        for i in range(len(rows)):
            if i & step:
                continue
            a, b = rows[i], rows[i + step]
            rows[i] = jnp.where(upper, turn(b, bit), a)
            rows[i + step] = jnp.where(upper, b, turn(a, -bit))
        step //= 2
    return rows


def cross(value):
    row = lax.broadcasted_iota(jnp.int32, value.shape, 0) >= 4
    return jnp.where(row == lane_bit(value.shape, 64), value, turn(pltpu.roll(value, 4, 0), 64))


def open_kernel(modes, out, flat):
    for c in range(2):
        for g in range(4):
            at = c * 4 + g
            flat[at] = modes[c, 4 * g : 4 * g + 4].reshape(LANES, LANES).T
            rows = [flat[at, pl.ds(y, 32, stride=4), :] for y in range(4)]
            for k, row in enumerate(swap(rows, (64, 32))):
                out[:, c * 16 + 4 * g + k, :] = row
    bed = swap([cross(flat[:, p, :]) for p in range(BED)], (16, 8))
    for nx in range(4):
        out[nx * 8 : nx * 8 + 8, 32:40, :] = jnp.broadcast_to(bed[nx][None], (8, 8, LANES))


def spread_kernel(got, xh, xl, bh, bl, out):
    block = jnp.concatenate(
        [got[:, c * 16 : c * 16 + 16, :].reshape(KX, LANES) for c in range(2)], axis=1
    )
    grid = mul((xh[...], xl[...]), halves(block))
    for w in range(16):
        for c in range(2):
            out[w, c * COL : c * COL + COL, :] = grid[
                w * COL : w * COL + COL, c * LANES : c * LANES + LANES
            ]
    bed = mul((bh[...], bl[...]), halves(got[:, 32:40, :].reshape(256, LANES)))
    bed = bed[:NX] + turn(bed[NX:], -32)
    upper = lane_bit((24, LANES), 32)
    for w in range(16):
        first = bed[w * COL : w * COL + 24]
        second = bed[w * COL + 24 : w * COL + COL]
        out[w, 96:120, :] = jnp.where(upper, turn(second, 32), first)


def pick_kernel(blocks, got, out):
    upper = lane_bit((LANES, LANES), 32)
    for o in range(4):
        low, high = blocks[0, o], blocks[1, o]
        a = got[:, pl.ds(pl.multiple_of(96 + 8 * lax.rem(low, 3), 8), 8), :].reshape(LANES, LANES)
        b = got[:, pl.ds(pl.multiple_of(96 + 8 * lax.rem(high, 3), 8), 8), :].reshape(LANES, LANES)
        a = jnp.where(low >= 3, turn(a, -32), a)
        b = jnp.where(high >= 3, b, turn(b, 32))
        out[o] = jnp.where(upper, b, a)


def product_kernel(got, zh, zl, sh, sl, out, held):
    for wh in range(4):
        rows = swap([got[4 * wh + wl, 0:96, :] for wl in range(4)], (64, 32))
        for y in range(4):
            held[y * 96 : y * 96 + 96, wh * LANES : wh * LANES + LANES] = rows[y]
    speed = mul(halves(held[...]), (zh[...], zl[...])).reshape(4, 2, COL, NZ)
    product = (speed[:, 1:2] * speed).reshape(384, NZ)
    inner = mul(halves(product), (sh[...], sl[...]))
    for wh in range(4):
        part = inner[:, wh * LANES : wh * LANES + LANES]
        rows = swap([part[y * 96 : y * 96 + 96] for y in range(4)], (64, 32))
        for wl in range(4):
            out[4 * wh + wl] = rows[wl]


def near_kernel(got, share, zh, zl, out, held):
    for nx in range(4):
        flat = got[nx].T
        rows = swap([flat[q * 8 : q * 8 + 8] for q in range(16)], (64, 32, 16, 8))
        for w in range(16):
            held[nx * LANES + w * 8 : nx * LANES + w * 8 + 8, :] = rows[w]
    speed = mul((zh[...], zl[...]), halves(held[...])).reshape(ZB, BIN, LANES)
    speed = speed * share[...][:, None, :]
    speed = speed + turn(speed, -8)
    out[...] = speed + turn(speed, -16)


def force_kernel(force, zh, zl, out):
    inner = mul((zh[...], zl[...]), halves(force[...].reshape(NZ, LANES)))
    for nx in range(4):
        part = inner[nx * LANES : nx * LANES + LANES]
        rows = swap([part[w * 8 : w * 8 + 8] for w in range(16)], (64, 32, 16, 8))
        out[nx] = jnp.concatenate(rows, axis=0).T


def place_kernel(blocks, got, main, out):
    out[:, 0:96, :] = main[...]
    out[:, 96:120, :] = jnp.zeros((16, 24, LANES), f32)
    upper = lane_bit((LANES, LANES), 32)
    for o in range(4):
        low, high = blocks[0, o], blocks[1, o]
        value = got[o]
        a = jnp.where(upper, 0.0, value)
        b = jnp.where(upper, value, 0.0)
        a = jnp.where(low >= 3, turn(a, 32), a).reshape(16, 8, LANES)
        b = jnp.where(high >= 3, b, turn(b, -32)).reshape(16, 8, LANES)
        rows = pl.ds(pl.multiple_of(96 + 8 * lax.rem(low, 3), 8), 8)
        out[:, rows, :] = out[:, rows, :] + a
        rows = pl.ds(pl.multiple_of(96 + 8 * lax.rem(high, 3), 8), 8)
        out[:, rows, :] = out[:, rows, :] + b


def gather_kernel(got, xh, xl, bh, bl, out):
    block = jnp.concatenate(
        [got[:, c * COL : c * COL + COL, :].reshape(NX, LANES) for c in range(2)], axis=1
    )
    terms = mul((xh[...], xl[...]), halves(block))
    for n in range(32):
        for c in range(2):
            out[n, c * 16 : c * 16 + 16, :] = terms[
                n * 16 : n * 16 + 16, c * LANES : c * LANES + LANES
            ]
    bed = mul((bh[...], bl[...]), halves(got[:, 96:120, :].reshape(384, LANES)))
    low = bed[0:256] + turn(bed[256:512], -32)
    high = turn(bed[512:768], 32) + bed[768:1024]
    bed = jnp.where(lane_bit((256, LANES), 32), high, low)
    out[:, 32:40, :] = bed.reshape(32, 8, LANES)


def close_kernel(place, got, modes, to_eigen, from_eigen, eigenvalues, out, flat, right):
    bed = [jnp.sum(got[nx * 8 : nx * 8 + 8, 32:40, :], axis=0) for nx in range(4)]
    bed = [cross(value) for value in swap(bed, (16, 8))]
    for c in range(2):
        for g in range(4):
            rows = swap([got[:, c * 16 + 4 * g + k, :] for k in range(4)], (64, 32))
            for y in range(4):
                flat[c * 4 + g, pl.ds(y, 32, stride=4), :] = rows[y]
    for p in range(BED):
        flat[:, p, :] = flat[:, p, :] + bed[p]
    for c in range(2):
        for g in range(4):
            at = c * 4 + g
            right[at * LANES : at * LANES + LANES, :] = flat[at].T + modes[
                c, 4 * g : 4 * g + 4
            ].reshape(LANES, LANES)
    across = (((1,), (1,)), ((), ()))
    part = mul(halves(right[...]), halves(from_eigen[...]), across)
    shape = (1024, LANES)
    row = lax.broadcasted_iota(jnp.int32, shape, 0)
    wave_x = ((place[0] * 16 + ((row >> 5) & 15) + 1) >> 1).astype(f32)
    wave_z = ((place[1] * 32 + (row & 31) + 1) >> 1).astype(f32)
    divisor = 1.0 + viscous * (wave_x * wave_x + wave_z * wave_z + eigenvalues[...])
    result = mul(halves(part / divisor), halves(to_eigen[...]), across)
    out[...] = result.reshape(2, 16, 32, LANES)


def call(body, shape, *operands, scalars=0, scratch=()):
    memory = [pl.BlockSpec(memory_space=pltpu.SMEM)] * scalars
    memory += [pl.BlockSpec(memory_space=pltpu.VMEM)] * (len(operands) - scalars)
    return pl.pallas_call(
        body,
        out_shape=jax.ShapeDtypeStruct(shape, f32),
        in_specs=memory,
        out_specs=pl.BlockSpec(memory_space=pltpu.VMEM),
        scratch_shapes=[pltpu.VMEM(size, f32) for size in scratch],
        compiler_params=pltpu.CompilerParams(vmem_limit_bytes=48 << 20),
        name=body.__name__,
    )(*operands)


def exchange(value, axis, groups=None):
    return lax.all_to_all(value, axis, 0, 0, axis_index_groups=groups, tiled=True)


def particle_terms(positions, velocities, diameters, cell_grid, active):
    centre = jnp.arange(cell_grid.shape[2], dtype=jnp.int32).astype(f32) + 0.5
    weight_x = jnp.exp(-0.5 * (positions[0][..., None] - centre) ** 2)
    weight_z = jnp.exp(-0.5 * (positions[1][..., None] - centre) ** 2)
    totals = jnp.sum(weight_x, axis=-1) * jnp.sum(weight_z, axis=-1)
    partial_value = jnp.einsum("spi,scik->cspk", weight_x, cell_grid, precision=highest)
    felt_velocity = jnp.sum(partial_value * weight_z[None], axis=-1) / totals[None]
    relative = felt_velocity - velocities
    magnitude = jnp.sqrt(relative[0] ** 2 + relative[1] ** 2 + 0.1)
    squared = diameters * diameters
    drag_force = 0.5 * squared[None] * relative * magnitude[None]
    lift_force = 0.5 * squared * (felt_velocity[0] ** 2 + felt_velocity[1] ** 2)
    alive_mask = active[:, None]
    lifted = jnp.where(
        alive_mask, jax.nn.sigmoid((lift_force - 0.5 * squared * diameters) / 0.25), 0.0
    )
    particle_push = jnp.where(alive_mask[None], drag_force * (1.0 + lifted[None]), 0.0)
    share_part = -reaction * particle_push / totals[None]
    cell_force = jnp.einsum(
        "spi,cspk->scik", weight_x, weight_z[None] * share_part[..., None], precision=highest
    )
    return (lifted, particle_push, cell_force)


def shards(
    modes,
    to_eigen,
    from_eigen,
    eigenvalues,
    bins_owned,
    bed_planes,
    particle_position,
    particle_velocity,
    particle_size,
):
    table = tables()
    narrow_at = lax.axis_index("narrow")
    wide_at = lax.axis_index("wide")
    most_bins = particle_size.shape[2]
    groups = [[nz + 8 * nx for nx in range(4)] for nz in range(8)]

    counts = bins_owned[0]
    rank = jnp.arange(32, dtype=jnp.int32)
    firsts = jnp.sum(jnp.where(rank[None, :] < rank[:, None], counts[None, :], 0), axis=1)
    first_bin = jnp.sum(jnp.where(rank < narrow_at, counts, 0))
    owned_count = jnp.sum(jnp.where(rank == narrow_at, counts, 0))
    active = jnp.arange(most_bins, dtype=jnp.int32) < owned_count
    row_low = first_bin // ZB
    row_high = jnp.minimum(row_low + 1, 5)
    nz_at = narrow_at % 8
    group_low = jnp.sum(
        jnp.where(rank.reshape(4, 8) % 8 == nz_at, firsts.reshape(4, 8), 0), axis=1
    ) // ZB
    blocks = jnp.stack([group_low, jnp.minimum(group_low + 1, 5)])
    planes = bed_planes.reshape(6, ZB)
    planes = jnp.stack(
        [
            lax.dynamic_index_in_dim(planes, row_low, 0, keepdims=False),
            lax.dynamic_index_in_dim(planes, row_high, 0, keepdims=False),
        ],
        axis=1,
    )
    inside = jnp.arange(BED, dtype=jnp.int32)[None, None, :] < planes[:, :, None]
    share = jnp.where(inside, 1.0 / planes.astype(f32)[:, :, None], 0.0)
    share = jnp.broadcast_to(share[:, None, :, :, None], (ZB, 2, 2, BED, BIN)).reshape(ZB, LANES)

    sent = call(open_kernel, (32, 40, LANES), modes, scratch=[(8, LANES, LANES)])
    got = exchange(sent, "narrow")
    sent = call(spread_kernel, (16, 120, LANES), got, *table["x"], *table["x_bed"])
    grid = exchange(sent, "wide")

    sent = call(pick_kernel, (4, LANES, LANES), blocks, grid, scalars=1)
    got = exchange(sent, "narrow", groups)
    inner = call(
        product_kernel, (16, 96, LANES), grid, *table["z"], *table["slope"], scratch=[(384, KZ)]
    )
    near = call(
        near_kernel, (ZB, BIN, LANES), got, share, *table["z_bed"], scratch=[(KZ, LANES)]
    )
    near = near.reshape(ZB, BIN, 2, 2, BED, BIN)[:, :, :, :, 0, :].transpose(3, 0, 2, 4, 1)
    cell_grid = lax.dynamic_slice_in_dim(
        near.reshape(2 * ZB, 2, BIN, BIN), first_bin - row_low * ZB, most_bins, 0
    )
    lifted, particle_push, cell_force = particle_terms(
        particle_position[0, 0], particle_velocity[0, 0], particle_size[0, 0], cell_grid, active
    )

    force = lax.dynamic_update_slice_in_dim(
        jnp.zeros((2 * ZB, 2, BIN, BIN), f32), cell_force, first_bin - row_low * ZB, 0
    )
    force = force.reshape(2, ZB, 2, BIN, BIN).transpose(1, 4, 2, 0, 3)
    force = jnp.broadcast_to(force[:, :, :, :, None, :], (ZB, BIN, 2, 2, BED, BIN))
    force = force.reshape(ZB, BIN, LANES) * share[:, None, :]
    sent = call(force_kernel, (4, LANES, LANES), force, *table["z_bed_back"])
    got = exchange(sent, "narrow", groups)
    sent = call(place_kernel, (16, 120, LANES), blocks, got, inner, scalars=1)

    got = exchange(sent, "wide")
    sent = call(gather_kernel, (32, 40, LANES), got, *table["z"], *table["x_bed_back"])
    got = exchange(sent, "narrow")
    new_modes = call(
        close_kernel,
        modes.shape,
        jnp.stack([narrow_at, wide_at]),
        got,
        modes,
        to_eigen,
        from_eigen,
        eigenvalues[None],
        scalars=1,
        scratch=[(8, LANES, LANES), (1024, LANES)],
    )
    return (new_modes, lifted[None, None], particle_push[None, None])


def solution(mesh):
    in_specs = (
        P(None, "narrow", "wide", None),
        P(),
        P(),
        P(),
        P("wide", None),
        P("wide"),
        P("wide", "narrow", None, None, None),
        P("wide", "narrow", None, None, None),
        P("wide", "narrow", None, None),
    )
    out_specs = (
        P(None, "narrow", "wide", None),
        P("wide", "narrow", None, None),
        P("wide", "narrow", None, None, None),
    )
    return jax.shard_map(shards, mesh=mesh, in_specs=in_specs, out_specs=out_specs, check_vma=False)
```

```python
import math

import jax
import jax.numpy as jnp
import ml_dtypes
import numpy as np
from jax import lax
from jax.experimental import pallas as pl
from jax.experimental.pallas import tpu as pltpu
from jax.sharding import PartitionSpec as P

NX = 768
NZ = 768
KX = 512
KZ = 512
BED = 4
BIN = 8
COL = 48
ZB = NZ // BIN
LANES = 128

time_step = 0.003
viscous = 0.0001
reaction = 0.25
f32 = jnp.float32
bf16 = jnp.bfloat16


def basis_np(mode_count, points):
    m = np.arange(mode_count)[:, None]
    j = np.arange(points)[None, :]
    k = (m + 1) // 2
    angle = (k * j % points) * (2.0 * math.pi / points)
    table = math.sqrt(2.0 / points) * np.where(m % 2 == 1, np.cos(angle), np.sin(angle))
    return np.where(m == 0, 1.0 / math.sqrt(points), table)


def slope_np(points, mode_count):
    j = np.arange(points)[:, None]
    m = np.arange(mode_count)[None, :]
    k = (m + 1) // 2
    angle = (k * j % points) * (2.0 * math.pi / points)
    return k * math.sqrt(2.0 / points) * np.where(m % 2 == 1, np.sin(angle), -np.cos(angle))


def split_np(table):
    table = np.ascontiguousarray(table).astype(np.float32)
    high = table.astype(ml_dtypes.bfloat16)
    low = (table - high.astype(np.float32)).astype(ml_dtypes.bfloat16)
    return np.stack([high, low])


def tables():
    basis = basis_np(KX, NX)
    return split_np(basis.T), split_np(basis), split_np(-time_step * slope_np(NZ, KZ))


def halves(value):
    high = value.astype(bf16)
    return high, (value - high.astype(f32)).astype(bf16)


def mul(a, b, dims=(((1,), (0,)), ((), ()))):
    def one(p, q):
        return lax.dot_general(p, q, dims, preferred_element_type=f32)

    return one(a[0], b[0]) + (one(a[0], b[1]) + one(a[1], b[0]))


def start(copies):
    for copy in copies:
        copy.start()
    return copies


def finish(copies):
    for copy in copies:
        copy.wait()


def lane_bit(shape, bit):
    return (lax.broadcasted_iota(jnp.int32, shape, len(shape) - 1) & bit) != 0


def turn(value, shift):
    return pltpu.roll(value, shift % LANES, value.ndim - 1)


def swap(rows, bits):
    rows = list(rows)
    step = len(rows) // 2
    for bit in bits:
        upper = lane_bit(rows[0].shape, bit)
        for i in range(len(rows)):
            if i & step:
                continue
            a, b = rows[i], rows[i + step]
            rows[i] = jnp.where(upper, turn(b, bit), a)
            rows[i + step] = jnp.where(upper, b, turn(a, -bit))
        step //= 2
    return rows


def cross(value):
    row = lax.broadcasted_iota(jnp.int32, value.shape, 0)
    for sub, bit in ((4, 64), (2, 32)):
        below, right = (row & sub) != 0, lane_bit(value.shape, bit)
        down = turn(pltpu.roll(value, sub, 0), -bit)
        up = turn(pltpu.roll(value, 8 - sub, 0), bit)
        value = jnp.where(below == right, value, jnp.where(below, down, up))
    return value


def modes_of(g):
    return [(g // 2) * 8 + g % 2 + 2 * k for k in range(4)]


def open_kernel(modes, out, flat):
    for c in range(2):
        for g in range(4):
            at = c * 4 + g
            flat[at] = jnp.concatenate([modes[c, k] for k in modes_of(g)], axis=0).T
            rows = [flat[at, pl.ds(y, 32, stride=4), :] for y in range(4)]
            for k, row in zip(modes_of(g), swap(rows, (64, 32))):
                out[:, c * 16 + k, :] = row
    bed = swap([cross(flat[:, p, :]) for p in range(BED)], (16, 8))
    for nx in range(4):
        out[nx * 8 : nx * 8 + 8, 32:40, :] = jnp.broadcast_to(bed[nx][None], (8, 8, LANES))


def spread_bed_kernel(got, table, out):
    block = got[:, 32:40, :]
    block = jnp.concatenate([block, turn(block, -32)], axis=1).reshape(KX, LANES)
    bed = mul((table[0], table[1]), halves(block))
    upper = lane_bit((24, LANES), 32)
    for w in range(16):
        first = bed[w * COL : w * COL + 24]
        second = bed[w * COL + 24 : w * COL + COL]
        out[w] = jnp.where(upper, turn(second, 32), first)


def spread_kernel(got, table, out):
    block = jnp.concatenate(
        [got[:, c * 16 : c * 16 + 16, :].reshape(KX, LANES) for c in range(2)], axis=1
    )
    grid = mul((table[0], table[1]), halves(block))
    for w in range(16):
        for c in range(2):
            out[w, c * COL : c * COL + COL, :] = grid[
                w * COL : w * COL + COL, c * LANES : c * LANES + LANES
            ]


def pick(blocks, o, got):
    low, high = blocks[0, o], blocks[1, o]
    a = got[:, pl.ds(pl.multiple_of(8 * lax.rem(low, 3), 8), 8), :].reshape(LANES, LANES)
    b = got[:, pl.ds(pl.multiple_of(8 * lax.rem(high, 3), 8), 8), :].reshape(LANES, LANES)
    a = jnp.where(low >= 3, turn(a, -32), a)
    b = jnp.where(high >= 3, b, turn(b, 32))
    return jnp.where(lane_bit((LANES, LANES), 32), b, a)


def pick_kernel(blocks, where, got, out1, out2, out3):
    for k, out in enumerate((out1, out2, out3)):
        out[...] = pick(blocks, (where[2] + k + 1) & 3, got)


def product_kernel(got, basis, slope, out, held):
    for wh in range(4):
        rows = swap([got[4 * wh + wl] for wl in range(4)], (64, 32))
        for y in range(4):
            held[y * 96 : y * 96 + 96, wh * LANES : wh * LANES + LANES] = rows[y]
    speed = mul(halves(held[...]), (basis[0], basis[1])).reshape(4, 2, COL, NZ)
    product = (speed[:, 1:2] * speed).reshape(384, NZ)
    inner = mul(halves(product), (slope[0], slope[1]))
    for wh in range(4):
        part = inner[:, wh * LANES : wh * LANES + LANES]
        rows = swap([part[y * 96 : y * 96 + 96] for y in range(4)], (64, 32))
        for wl in range(4):
            out[4 * wh + wl] = rows[wl]


def bed_kernel(
    blocks, where, own, got1, got2, got3, share, basis, basis_back, position, velocity, size,
    out, lifted, push,
    held, near, force, grid, built, lifted_held, push_held, sems,
):
    for k, got in enumerate((None, got1, got2, got3)):
        nx = (where[2] - k) & 3
        flat = (pick(blocks, nx, own) if k == 0 else got[...]).T
        rows = swap([flat[q * 8 : q * 8 + 8] for q in range(16)], (64, 32, 16, 8))
        for w in range(16):
            held[pl.ds(pl.multiple_of(w * 32 + nx * 8, 8), 8), :] = rows[w]
    speed = mul((basis[0], basis[1]), halves(held[...])).reshape(ZB, BIN, LANES)
    speed = speed * share[...][:, None, :]
    speed = speed + turn(speed, -8)
    near[...] = speed + turn(speed, -16)
    force[...] = jnp.zeros(force.shape, f32)

    offset, owned = where[0], where[1]
    lane = lax.broadcasted_iota(jnp.int32, (BIN, LANES), 1)
    slots = position.shape[1]
    for base in (0, 16, 32, slots - 16):
        span = slice(base, base + 16)
        spot = []
        for s in range(16):
            index = offset + (base + s)
            row = (index >= ZB).astype(jnp.int32)
            spot.append((index - ZB * row, row))
            cells = near[index - ZB * row]
            for c in range(2):
                cell = pltpu.roll(cells, (s * 8 - c * 64 - row * 32) & (LANES - 1), 1)
                grid[s * 16 + c * 8 : s * 16 + c * 8 + 8, :] = jnp.where(lane >> 3 == s, cell, 0.0)
        centre = lax.broadcasted_iota(jnp.int32, (16, BIN, LANES), 1).astype(f32) + 0.5
        weight_x = jnp.exp(-0.5 * (position[0, span][:, None, :] - centre) ** 2)
        weight_z = jnp.exp(-0.5 * (position[1, span][:, None, :] - centre) ** 2)
        totals = jnp.sum(weight_x, axis=1) * jnp.sum(weight_z, axis=1)
        flat_x = halves(weight_x.reshape(LANES, LANES))
        part = mul(halves(grid[...]), flat_x).reshape(16, 2, BIN, LANES)
        felt = [jnp.sum(part[:, c] * weight_z, axis=1) / totals for c in range(2)]
        relative = [felt[c] - velocity[c, span] for c in range(2)]
        magnitude = jnp.sqrt(relative[0] * relative[0] + relative[1] * relative[1] + 0.1)
        diameter = size[span]
        squared = diameter * diameter
        lift = 0.5 * squared * (felt[0] * felt[0] + felt[1] * felt[1])
        active = lax.broadcasted_iota(jnp.int32, (16, LANES), 0) + base < owned
        chance = jnp.where(
            active, jax.nn.sigmoid((lift - 0.5 * squared * diameter) / 0.25), 0.0
        )
        lifted_held[span] = chance
        pulls = []
        for c in range(2):
            pushed = jnp.where(
                active, 0.5 * squared * relative[c] * magnitude * (1.0 + chance), 0.0
            )
            push_held[c, span] = pushed
            pulls.append((-reaction * pushed / totals)[:, None, :] * weight_z)
        pull = jnp.stack(pulls, axis=1).reshape(2 * LANES, LANES)
        cells = mul(halves(pull), flat_x, (((1,), (1,)), ((), ())))
        shape = (2 * LANES, LANES)
        mine = lax.broadcasted_iota(jnp.int32, shape, 1) >> 3 == (
            lax.broadcasted_iota(jnp.int32, shape, 0) >> 4
        )
        cells = jnp.where(mine, cells, 0.0)
        for bit in (8, 16, 32, 64):
            cells = cells + turn(cells, bit)
        for s in range(16):
            value = jnp.where(
                lane_bit((BIN, LANES), 64),
                cells[s * 16 + 8 : s * 16 + 16],
                cells[s * 16 : s * 16 + 8],
            )
            value = jnp.where((lane >> 5) & 1 == spot[s][1], value, 0.0)
            force[spot[s][0]] = value * share[pl.ds(spot[s][0], 1), :]

    sent = start(
        [
            pltpu.make_async_copy(lifted_held, lifted, sems.at[0]),
            pltpu.make_async_copy(push_held, push, sems.at[1]),
        ]
    )
    inner = mul((basis_back[0], basis_back[1]), halves(force[...].reshape(NZ, LANES)))
    for nx in range(4):
        rows = [inner[w * 32 + nx * 8 : w * 32 + nx * 8 + 8] for w in range(16)]
        built[nx] = jnp.concatenate(swap(rows, (64, 32, 16, 8)), axis=0).T
        sent += start([pltpu.make_async_copy(built.at[nx], out.at[nx], sems.at[2 + nx])])
    finish(sent)


def place_kernel(blocks, got, main, out):
    out[:, 0:96, :] = main[...]
    out[:, 96:120, :] = jnp.zeros((16, 24, LANES), f32)
    upper = lane_bit((LANES, LANES), 32)
    for o in range(4):
        low, high = blocks[0, o], blocks[1, o]
        value = got[o]
        a = jnp.where(upper, 0.0, value)
        b = jnp.where(upper, value, 0.0)
        a = jnp.where(low >= 3, turn(a, 32), a).reshape(16, 8, LANES)
        b = jnp.where(high >= 3, b, turn(b, -32)).reshape(16, 8, LANES)
        rows = pl.ds(pl.multiple_of(96 + 8 * lax.rem(low, 3), 8), 8)
        out[:, rows, :] = out[:, rows, :] + a
        rows = pl.ds(pl.multiple_of(96 + 8 * lax.rem(high, 3), 8), 8)
        out[:, rows, :] = out[:, rows, :] + b


def gather_kernel(got, table, out):
    block = [got[:, c * COL : c * COL + COL, :].reshape(NX, LANES) for c in range(2)]
    bed = got[:, 96:120, :]
    block.append(jnp.concatenate([bed, turn(bed, -32)], axis=1).reshape(NX, LANES))
    terms = mul((table[0], table[1]), halves(jnp.concatenate(block, axis=1)))
    upper = lane_bit((8, LANES), 32)
    for n in range(32):
        part = terms[n * 16 : n * 16 + 16]
        for c in range(2):
            out[n, c * 16 : c * 16 + 16, :] = part[:, c * LANES : c * LANES + LANES]
        bed = part[:, 2 * LANES :]
        out[n, 32:40, :] = jnp.where(upper, turn(bed[8:16], 32), bed[0:8])


def close_kernel(
    place, got, modes, to_eigen, from_eigen, eigenvalues, out, flat, held, built, sems
):
    parts = [(c, g) for c in range(2) for g in range(4)]
    bed = [jnp.sum(got[nx * 8 : nx * 8 + 8, 32:40, :], axis=0) for nx in range(4)]
    bed = [cross(value) for value in swap(bed, (16, 8))]
    for c, g in parts:
        rows = swap([got[:, c * 16 + k, :] for k in modes_of(g)], (64, 32))
        for y in range(4):
            flat[c * 4 + g, pl.ds(y, 32, stride=4), :] = rows[y]
    for p in range(BED):
        flat[:, p, :] = flat[:, p, :] + bed[p]
    for c, g in parts:
        back = flat[c * 4 + g].T
        for i, k in enumerate(modes_of(g)):
            at = (c * 16 + k) * 32
            held[at : at + 32, :] = back[i * 32 : i * 32 + 32] + modes[c, k]
    across = (((1,), (1,)), ((), ()))
    forth, back = halves(from_eigen[...]), halves(to_eigen[...])
    sent = []
    for i in range(4):
        rows = slice(i * 256, i * 256 + 256)
        part = mul(halves(held[rows]), forth, across)
        row = lax.broadcasted_iota(jnp.int32, (256, LANES), 0) + i * 256
        wave_x = ((place[0] * 16 + ((row >> 5) & 15) + 1) >> 1).astype(f32)
        wave_z = ((place[1] * 32 + (row & 31) + 1) >> 1).astype(f32)
        divisor = 1.0 + viscous * (wave_x * wave_x + wave_z * wave_z + eigenvalues[...])
        result = mul(halves(part / divisor), back, across)
        built[i] = result.reshape(8, 32, LANES)
        block = out.at[i // 2, pl.ds(8 * (i % 2), 8)]
        sent += start([pltpu.make_async_copy(built.at[i], block, sems.at[i])])
    finish(sent)


def call(body, shape, *operands, scalars=0, scratch=(), sems=0, out_far=False):
    spaces = [pltpu.SMEM] * scalars + [pltpu.VMEM] * (len(operands) - scalars)
    out_space = pl.BlockSpec(memory_space=pltpu.HBM if out_far else pltpu.VMEM)
    several = isinstance(shape, list)
    outs = [jax.ShapeDtypeStruct(one, f32) for one in (shape if several else [shape])]
    held = [pltpu.VMEM(one, f32) for one in scratch]
    bytes_moved = sum(4 * math.prod(one.shape) for one in list(operands) + outs)
    result = pl.pallas_call(
        body,
        out_shape=outs,
        in_specs=[pl.BlockSpec(memory_space=space) for space in spaces],
        out_specs=[out_space] * len(outs),
        scratch_shapes=held + ([pltpu.SemaphoreType.DMA((sems,))] if sems else []),
        compiler_params=pltpu.CompilerParams(vmem_limit_bytes=20 << 20),
        cost_estimate=pl.CostEstimate(
            flops=2_000_000_000, bytes_accessed=bytes_moved, transcendentals=0
        ),
        name=body.__name__,
    )(*operands)
    return result if several else result[0]


def exchange(value, axis, groups=None):
    return lax.all_to_all(value, axis, 0, 0, axis_index_groups=groups, tiled=True)


def shards(
    modes,
    to_eigen,
    from_eigen,
    eigenvalues,
    bins_owned,
    bed_planes,
    particle_position,
    particle_velocity,
    particle_size,
):
    points, basis, slope = tables()
    narrow_at = lax.axis_index("narrow")
    wide_at = lax.axis_index("wide")
    groups = [[nz + 8 * nx for nx in range(4)] for nz in range(8)]

    counts = bins_owned[0]
    rank = jnp.arange(32, dtype=jnp.int32)
    firsts = jnp.sum(jnp.where(rank[None, :] < rank[:, None], counts[None, :], 0), axis=1)
    first_bin = jnp.sum(jnp.where(rank < narrow_at, counts, 0))
    owned_count = jnp.sum(jnp.where(rank == narrow_at, counts, 0))
    row_low = first_bin // ZB
    row_high = jnp.minimum(row_low + 1, 5)
    nz_at = narrow_at % 8
    group_low = jnp.sum(
        jnp.where(rank.reshape(4, 8) % 8 == nz_at, firsts.reshape(4, 8), 0), axis=1
    ) // ZB
    blocks = jnp.stack([group_low, jnp.minimum(group_low + 1, 5)])
    planes = bed_planes.reshape(6, ZB)
    planes = jnp.stack(
        [
            lax.dynamic_index_in_dim(planes, row_low, 0, keepdims=False),
            lax.dynamic_index_in_dim(planes, row_high, 0, keepdims=False),
        ],
        axis=1,
    )
    inside = jnp.arange(BED, dtype=jnp.int32)[None, None, :] < planes[:, :, None]
    share = jnp.where(inside, 1.0 / planes.astype(f32)[:, :, None], 0.0)
    share = jnp.broadcast_to(share[:, None, :, :, None], (ZB, 2, 2, BED, BIN)).reshape(ZB, LANES)

    where = jnp.stack([first_bin - row_low * ZB, owned_count, narrow_at // 8])

    sent = call(open_kernel, (32, 40, LANES), modes, scratch=[(8, LANES, LANES)])
    got = exchange(sent, "narrow")
    bed = exchange(call(spread_bed_kernel, (16, 24, LANES), got, points), "wide")
    sent = call(spread_kernel, (16, 96, LANES), got, points)
    sent, bed, blocks, where, share = lax.optimization_barrier((sent, bed, blocks, where, share))
    grid = exchange(sent, "wide")

    block = (LANES, LANES)
    sent = call(pick_kernel, [block] * 3, blocks, where, bed, scalars=2)
    got = []
    for k in range(1, 4):
        hops = [(x * 8 + z, (x + k) % 4 * 8 + z) for x in range(4) for z in range(8)]
        got.append(lax.ppermute(sent[k - 1], "narrow", hops))

    slots, pairs = particle_size.shape[2:], particle_velocity.shape[2:]
    sent, lifted, particle_push = call(
        bed_kernel,
        [(4,) + block, slots, pairs],
        blocks,
        where,
        bed,
        *got,
        share,
        points,
        basis,
        particle_position[0, 0],
        particle_velocity[0, 0],
        particle_size[0, 0],
        scalars=2,
        scratch=[
            (KZ, LANES),
            (ZB, BIN, LANES),
            (ZB, BIN, LANES),
            (2 * LANES, LANES),
            (4,) + block,
            slots,
            pairs,
        ],
        sems=6,
        out_far=True,
    )
    got = exchange(sent, "narrow", groups)
    inner = call(product_kernel, (16, 96, LANES), grid, basis, slope, scratch=[(384, KZ)])
    sent = call(place_kernel, (16, 120, LANES), blocks, got, inner, scalars=1)

    got = exchange(sent, "wide")
    sent = call(gather_kernel, (32, 40, LANES), got, basis)
    got = exchange(sent, "narrow")
    new_modes = call(
        close_kernel,
        modes.shape,
        jnp.stack([narrow_at, wide_at]),
        got,
        modes,
        to_eigen,
        from_eigen,
        eigenvalues[None],
        scalars=1,
        scratch=[(8, LANES, LANES), (1024, LANES), (4, 8, 32, LANES)],
        sems=4,
        out_far=True,
    )
    return (new_modes, lifted[None, None], particle_push[None, None])


def solution(mesh):
    in_specs = (
        P(None, "narrow", "wide", None),
        P(),
        P(),
        P(),
        P("wide", None),
        P("wide"),
        P("wide", "narrow", None, None, None),
        P("wide", "narrow", None, None, None),
        P("wide", "narrow", None, None),
    )
    out_specs = (
        P(None, "narrow", "wide", None),
        P("wide", "narrow", None, None),
        P("wide", "narrow", None, None, None),
    )
    return jax.shard_map(shards, mesh=mesh, in_specs=in_specs, out_specs=out_specs, check_vma=False)
```

```python
import math

import jax
import jax.numpy as jnp
import ml_dtypes
import numpy as np
from jax import lax
from jax.experimental import pallas as pl
from jax.experimental.pallas import tpu as pltpu
from jax.sharding import PartitionSpec as P

NX = 768
NZ = 768
KX = 512
KZ = 512
BED = 4
BIN = 8
COL = 48
ZB = NZ // BIN
LANES = 128

time_step = 0.003
viscous = 0.0001
reaction = 0.25
f32 = jnp.float32
bf16 = jnp.bfloat16


def basis_np(mode_count, points):
    m = np.arange(mode_count)[:, None]
    j = np.arange(points)[None, :]
    k = (m + 1) // 2
    angle = (k * j % points) * (2.0 * math.pi / points)
    table = math.sqrt(2.0 / points) * np.where(m % 2 == 1, np.cos(angle), np.sin(angle))
    return np.where(m == 0, 1.0 / math.sqrt(points), table)


def slope_np(points, mode_count):
    j = np.arange(points)[:, None]
    m = np.arange(mode_count)[None, :]
    k = (m + 1) // 2
    angle = (k * j % points) * (2.0 * math.pi / points)
    return k * math.sqrt(2.0 / points) * np.where(m % 2 == 1, np.sin(angle), -np.cos(angle))


def split_np(table):
    table = np.ascontiguousarray(table).astype(np.float32)
    high = table.astype(ml_dtypes.bfloat16)
    low = (table - high.astype(np.float32)).astype(ml_dtypes.bfloat16)
    return np.stack([high, low])


def tables():
    basis = basis_np(KX, NX)
    return split_np(basis.T), split_np(basis), split_np(-time_step * slope_np(NZ, KZ))


def halves(value):
    high = value.astype(bf16)
    return high, (value - high.astype(f32)).astype(bf16)


def mul(a, b, dims=(((1,), (0,)), ((), ()))):
    def one(p, q):
        return lax.dot_general(p, q, dims, preferred_element_type=f32)

    return one(a[0], b[0]) + (one(a[0], b[1]) + one(a[1], b[0]))


def start(copies):
    for copy in copies:
        copy.start()
    return copies


def finish(copies):
    for copy in copies:
        copy.wait()


def lane_bit(shape, bit):
    return (lax.broadcasted_iota(jnp.int32, shape, len(shape) - 1) & bit) != 0


def turn(value, shift):
    return pltpu.roll(value, shift % LANES, value.ndim - 1)


def swap(rows, bits):
    rows = list(rows)
    step = len(rows) // 2
    for bit in bits:
        upper = lane_bit(rows[0].shape, bit)
        for i in range(len(rows)):
            if i & step:
                continue
            a, b = rows[i], rows[i + step]
            rows[i] = jnp.where(upper, turn(b, bit), a)
            rows[i + step] = jnp.where(upper, b, turn(a, -bit))
        step //= 2
    return rows


def cross(value):
    row = lax.broadcasted_iota(jnp.int32, value.shape, 0)
    for sub, bit in ((4, 64), (2, 32)):
        below, right = (row & sub) != 0, lane_bit(value.shape, bit)
        down = turn(pltpu.roll(value, sub, 0), -bit)
        up = turn(pltpu.roll(value, 8 - sub, 0), bit)
        value = jnp.where(below == right, value, jnp.where(below, down, up))
    return value


def modes_of(g):
    return [(g // 2) * 8 + g % 2 + 2 * k for k in range(4)]


def open_kernel(modes, out, flat):
    for c in range(2):
        for g in range(4):
            at = c * 4 + g
            flat[at] = jnp.concatenate([modes[c, k] for k in modes_of(g)], axis=0).T
            rows = [flat[at, pl.ds(y, 32, stride=4), :] for y in range(4)]
            for k, row in zip(modes_of(g), swap(rows, (64, 32))):
                out[:, c * 16 + k, :] = row
    bed = swap([cross(flat[:, p, :]) for p in range(BED)], (16, 8))
    for nx in range(4):
        out[nx * 8 : nx * 8 + 8, 32:40, :] = jnp.broadcast_to(bed[nx][None], (8, 8, LANES))


def spread_bed_kernel(got, table, out):
    block = got[:, 32:40, :]
    block = jnp.concatenate([block, turn(block, -32)], axis=1).reshape(KX, LANES)
    bed = mul((table[0], table[1]), halves(block))
    upper = lane_bit((24, LANES), 32)
    for w in range(16):
        first = bed[w * COL : w * COL + 24]
        second = bed[w * COL + 24 : w * COL + COL]
        out[w] = jnp.where(upper, turn(second, 32), first)


def spread_kernel(got, table, out):
    block = jnp.concatenate(
        [got[:, c * 16 : c * 16 + 16, :].reshape(KX, LANES) for c in range(2)], axis=1
    )
    grid = mul((table[0], table[1]), halves(block))
    for w in range(16):
        for c in range(2):
            out[w, c * COL : c * COL + COL, :] = grid[
                w * COL : w * COL + COL, c * LANES : c * LANES + LANES
            ]


def pick(blocks, o, got):
    low, high = blocks[0, o], blocks[1, o]
    a = got[:, pl.ds(pl.multiple_of(8 * lax.rem(low, 3), 8), 8), :].reshape(LANES, LANES)
    b = got[:, pl.ds(pl.multiple_of(8 * lax.rem(high, 3), 8), 8), :].reshape(LANES, LANES)
    a = jnp.where(low >= 3, turn(a, -32), a)
    b = jnp.where(high >= 3, b, turn(b, 32))
    return jnp.where(lane_bit((LANES, LANES), 32), b, a)


def pick_kernel(blocks, where, got, out1, out2, out3):
    for k, out in enumerate((out1, out2, out3)):
        out[...] = pick(blocks, (where[2] + k + 1) & 3, got)


def product_kernel(got, basis, slope, out, held):
    for wh in range(4):
        rows = swap([got[4 * wh + wl] for wl in range(4)], (64, 32))
        for y in range(4):
            held[y * 96 : y * 96 + 96, wh * LANES : wh * LANES + LANES] = rows[y]
    speed = mul(halves(held[...]), (basis[0], basis[1])).reshape(4, 2, COL, NZ)
    product = (speed[:, 1:2] * speed).reshape(384, NZ)
    inner = mul(halves(product), (slope[0], slope[1]))
    for wh in range(4):
        part = inner[:, wh * LANES : wh * LANES + LANES]
        rows = swap([part[y * 96 : y * 96 + 96] for y in range(4)], (64, 32))
        for wl in range(4):
            out[4 * wh + wl, 0:96, :] = rows[wl]
    out[:, 96:120, :] = jnp.zeros((16, 24, LANES), f32)


def bed_kernel(
    blocks, where, own, got1, got2, got3, share, basis, basis_back, position, velocity, size,
    out, lifted, push,
    held, near, force, grid, built, lifted_held, push_held, sems,
):
    for k, got in enumerate((None, got1, got2, got3)):
        nx = (where[2] - k) & 3
        flat = (pick(blocks, nx, own) if k == 0 else got[...]).T
        rows = swap([flat[q * 8 : q * 8 + 8] for q in range(16)], (64, 32, 16, 8))
        for w in range(16):
            held[pl.ds(pl.multiple_of(w * 32 + nx * 8, 8), 8), :] = rows[w]
    speed = mul((basis[0], basis[1]), halves(held[...])).reshape(ZB, BIN, LANES)
    speed = speed * share[...][:, None, :]
    speed = speed + turn(speed, -8)
    near[...] = speed + turn(speed, -16)
    force[...] = jnp.zeros(force.shape, f32)

    offset, owned = where[0], where[1]
    lane = lax.broadcasted_iota(jnp.int32, (BIN, LANES), 1)
    slots = position.shape[1]
    bases = (0, 16, 32, slots - 16)
    spots = []
    for i, base in enumerate(bases):
        for s in range(16):
            index = offset + (base + s)
            row = (index >= ZB).astype(jnp.int32)
            spots.append((index - ZB * row, row))
            cells = near[index - ZB * row]
            for c in range(2):
                cell = pltpu.roll(cells, (s * 8 - c * 64 - row * 32) & (LANES - 1), 1)
                at = s * 16 + c * 8
                grid[i, at : at + 8, :] = jnp.where(lane >> 3 == s, cell, 0.0)

    centre = lax.broadcasted_iota(jnp.int32, (16, BIN, LANES), 1).astype(f32) + 0.5
    spans = [slice(base, base + 16) for base in bases]
    weight_x = [jnp.exp(-0.5 * (position[0, span][:, None, :] - centre) ** 2) for span in spans]
    weight_z = [jnp.exp(-0.5 * (position[1, span][:, None, :] - centre) ** 2) for span in spans]
    flat_x = [halves(weight.reshape(LANES, LANES)) for weight in weight_x]
    part = [mul(halves(grid[i]), flat_x[i]).reshape(16, 2, BIN, LANES) for i in range(4)]
    pulls = []
    for i, span in enumerate(spans):
        totals = jnp.sum(weight_x[i], axis=1) * jnp.sum(weight_z[i], axis=1)
        felt = [jnp.sum(part[i][:, c] * weight_z[i], axis=1) / totals for c in range(2)]
        relative = [felt[c] - velocity[c, span] for c in range(2)]
        magnitude = jnp.sqrt(relative[0] * relative[0] + relative[1] * relative[1] + 0.1)
        diameter = size[span]
        squared = diameter * diameter
        lift = 0.5 * squared * (felt[0] * felt[0] + felt[1] * felt[1])
        active = lax.broadcasted_iota(jnp.int32, (16, LANES), 0) + bases[i] < owned
        chance = jnp.where(
            active, jax.nn.sigmoid((lift - 0.5 * squared * diameter) / 0.25), 0.0
        )
        lifted_held[span, 0, :] = chance
        pull = []
        for c in range(2):
            pushed = jnp.where(
                active, 0.5 * squared * relative[c] * magnitude * (1.0 + chance), 0.0
            )
            push_held[span, c, :] = pushed
            pull.append((-reaction * pushed / totals)[:, None, :] * weight_z[i])
        pulls.append(halves(jnp.stack(pull, axis=1).reshape(2 * LANES, LANES)))
    sent = start(
        [
            pltpu.make_async_copy(lifted_held, lifted, sems.at[0]),
            pltpu.make_async_copy(push_held, push, sems.at[1]),
        ]
    )

    shape = (2 * LANES, LANES)
    mine = lax.broadcasted_iota(jnp.int32, shape, 1) >> 3 == (
        lax.broadcasted_iota(jnp.int32, shape, 0) >> 4
    )
    for i in range(4):
        cells = mul(pulls[i], flat_x[i], (((1,), (1,)), ((), ())))
        cells = jnp.where(mine, cells, 0.0)
        for bit in (8, 16, 32, 64):
            cells = cells + turn(cells, bit)
        for s in range(16):
            spot, row = spots[i * 16 + s]
            value = jnp.where(
                lane_bit((BIN, LANES), 64),
                cells[s * 16 + 8 : s * 16 + 16],
                cells[s * 16 : s * 16 + 8],
            )
            value = jnp.where((lane >> 5) & 1 == row, value, 0.0)
            force[spot] = value * share[pl.ds(spot, 1), :]

    inner = mul((basis_back[0], basis_back[1]), halves(force[...].reshape(NZ, LANES)))
    for nx in range(4):
        rows = [inner[w * 32 + nx * 8 : w * 32 + nx * 8 + 8] for w in range(16)]
        built[nx] = jnp.concatenate(swap(rows, (64, 32, 16, 8)), axis=0).T
        sent += start([pltpu.make_async_copy(built.at[nx], out.at[nx], sems.at[2 + nx])])
    finish(sent)


def place_kernel(blocks, got, main, out):
    upper = lane_bit((LANES, LANES), 32)
    for o in range(4):
        low, high = blocks[0, o], blocks[1, o]
        value = got[o]
        a = jnp.where(upper, 0.0, value)
        b = jnp.where(upper, value, 0.0)
        a = jnp.where(low >= 3, turn(a, 32), a).reshape(16, 8, LANES)
        b = jnp.where(high >= 3, b, turn(b, -32)).reshape(16, 8, LANES)
        rows = pl.ds(pl.multiple_of(96 + 8 * lax.rem(low, 3), 8), 8)
        out[:, rows, :] = out[:, rows, :] + a
        rows = pl.ds(pl.multiple_of(96 + 8 * lax.rem(high, 3), 8), 8)
        out[:, rows, :] = out[:, rows, :] + b


def gather_kernel(got, table, out):
    block = [got[:, c * COL : c * COL + COL, :].reshape(NX, LANES) for c in range(2)]
    bed = got[:, 96:120, :]
    block.append(jnp.concatenate([bed, turn(bed, -32)], axis=1).reshape(NX, LANES))
    terms = mul((table[0], table[1]), halves(jnp.concatenate(block, axis=1)))
    upper = lane_bit((8, LANES), 32)
    for n in range(32):
        part = terms[n * 16 : n * 16 + 16]
        for c in range(2):
            out[n, c * 16 : c * 16 + 16, :] = part[:, c * LANES : c * LANES + LANES]
        bed = part[:, 2 * LANES :]
        out[n, 32:40, :] = jnp.where(upper, turn(bed[8:16], 32), bed[0:8])


def close_kernel(
    where, got, modes, to_eigen, from_eigen, eigenvalues, out, flat, held, built, sems
):
    parts = [(c, g) for c in range(2) for g in range(4)]
    bed = [jnp.sum(got[nx * 8 : nx * 8 + 8, 32:40, :], axis=0) for nx in range(4)]
    bed = [cross(value) for value in swap(bed, (16, 8))]
    for c, g in parts:
        rows = swap([got[:, c * 16 + k, :] for k in modes_of(g)], (64, 32))
        for y in range(4):
            flat[c * 4 + g, pl.ds(y, 32, stride=4), :] = rows[y]
    for p in range(BED):
        flat[:, p, :] = flat[:, p, :] + bed[p]
    for c, g in parts:
        back = flat[c * 4 + g].T
        for i, k in enumerate(modes_of(g)):
            at = (c * 16 + k) * 32
            held[at : at + 32, :] = back[i * 32 : i * 32 + 32] + modes[c, k]
    across = (((1,), (1,)), ((), ()))
    forth, back = halves(from_eigen[...]), halves(to_eigen[...])
    sent = []
    for i in range(4):
        rows = slice(i * 256, i * 256 + 256)
        part = mul(halves(held[rows]), forth, across)
        row = lax.broadcasted_iota(jnp.int32, (256, LANES), 0) + i * 256
        wave_x = ((where[3] * 16 + ((row >> 5) & 15) + 1) >> 1).astype(f32)
        wave_z = ((where[4] * 32 + (row & 31) + 1) >> 1).astype(f32)
        divisor = 1.0 + viscous * (wave_x * wave_x + wave_z * wave_z + eigenvalues[...])
        result = mul(halves(part / divisor), back, across)
        built[i] = result.reshape(8, 32, LANES)
        block = out.at[i // 2, pl.ds(8 * (i % 2), 8)]
        sent += start([pltpu.make_async_copy(built.at[i], block, sems.at[i])])
    finish(sent)


def call(body, shape, *operands, scalars=0, scratch=(), sems=0, out_far=False, alias={}):
    spaces = [pltpu.SMEM] * scalars + [pltpu.VMEM] * (len(operands) - scalars)
    out_space = pl.BlockSpec(memory_space=pltpu.HBM if out_far else pltpu.VMEM)
    several = isinstance(shape, list)
    outs = [jax.ShapeDtypeStruct(one, f32) for one in (shape if several else [shape])]
    held = [pltpu.VMEM(one, f32) for one in scratch]
    bytes_moved = sum(4 * math.prod(one.shape) for one in list(operands) + outs)
    result = pl.pallas_call(
        body,
        out_shape=outs,
        in_specs=[pl.BlockSpec(memory_space=space) for space in spaces],
        out_specs=[out_space] * len(outs),
        scratch_shapes=held + ([pltpu.SemaphoreType.DMA((sems,))] if sems else []),
        compiler_params=pltpu.CompilerParams(vmem_limit_bytes=16 << 20),
        cost_estimate=pl.CostEstimate(
            flops=100_000_000, bytes_accessed=bytes_moved, transcendentals=0
        ),
        input_output_aliases=alias,
        name=body.__name__,
    )(*operands)
    return result if several else result[0]


def exchange(value, axis, groups=None):
    return lax.all_to_all(value, axis, 0, 0, axis_index_groups=groups, tiled=True)


def shards(
    modes,
    to_eigen,
    from_eigen,
    eigenvalues,
    bins_owned,
    bed_planes,
    particle_position,
    particle_velocity,
    particle_size,
):
    points, basis, slope = tables()
    narrow_at = lax.axis_index("narrow")
    wide_at = lax.axis_index("wide")
    groups = [[nz + 8 * nx for nx in range(4)] for nz in range(8)]

    counts = bins_owned[0]
    rank = jnp.arange(32, dtype=jnp.int32)
    firsts = jnp.sum(jnp.where(rank[None, :] < rank[:, None], counts[None, :], 0), axis=1)
    first_bin = jnp.sum(jnp.where(rank < narrow_at, counts, 0))
    owned_count = jnp.sum(jnp.where(rank == narrow_at, counts, 0))
    row_low = first_bin // ZB
    row_high = jnp.minimum(row_low + 1, 5)
    nz_at = narrow_at % 8
    group_low = jnp.sum(
        jnp.where(rank.reshape(4, 8) % 8 == nz_at, firsts.reshape(4, 8), 0), axis=1
    ) // ZB
    blocks = jnp.stack([group_low, jnp.minimum(group_low + 1, 5)])
    planes = bed_planes.reshape(6, ZB)
    planes = jnp.stack(
        [
            lax.dynamic_index_in_dim(planes, row_low, 0, keepdims=False),
            lax.dynamic_index_in_dim(planes, row_high, 0, keepdims=False),
        ],
        axis=1,
    )
    inside = jnp.arange(BED, dtype=jnp.int32)[None, None, :] < planes[:, :, None]
    share = jnp.where(inside, 1.0 / planes.astype(f32)[:, :, None], 0.0)
    share = jnp.broadcast_to(share[:, None, :, :, None], (ZB, 2, 2, BED, BIN)).reshape(ZB, LANES)

    where = jnp.stack(
        [first_bin - row_low * ZB, owned_count, narrow_at // 8, narrow_at, wide_at]
    )

    sent = call(open_kernel, (32, 40, LANES), modes, scratch=[(8, LANES, LANES)])
    got = exchange(sent, "narrow")
    bed = exchange(call(spread_bed_kernel, (16, 24, LANES), got, points), "wide")
    sent = call(spread_kernel, (16, 96, LANES), got, points)
    sent, bed, blocks, where, share = lax.optimization_barrier((sent, bed, blocks, where, share))
    grid = exchange(sent, "wide")

    block = (LANES, LANES)
    sent = call(pick_kernel, [block] * 3, blocks, where, bed, scalars=2)
    got = []
    for k in range(1, 4):
        hops = [(x * 8 + z, (x + k) % 4 * 8 + z) for x in range(4) for z in range(8)]
        got.append(lax.ppermute(sent[k - 1], "narrow", hops))

    count = particle_size.shape[2]
    slots, pairs = (count, 1, LANES), (count, 2, LANES)
    sent, lifted, particle_push = call(
        bed_kernel,
        [(4,) + block, slots, pairs],
        blocks,
        where,
        bed,
        *got,
        share,
        points,
        basis,
        particle_position[0, 0],
        particle_velocity[0, 0],
        particle_size[0, 0],
        scalars=2,
        scratch=[
            (KZ, LANES),
            (ZB, BIN, LANES),
            (ZB, BIN, LANES),
            (4, 2 * LANES, LANES),
            (4,) + block,
            slots,
            pairs,
        ],
        sems=6,
        out_far=True,
    )
    got = exchange(sent, "narrow", groups)
    inner = call(product_kernel, (16, 120, LANES), grid, basis, slope, scratch=[(384, KZ)])
    sent = call(place_kernel, (16, 120, LANES), blocks, got, inner, scalars=1, alias={2: 0})

    got = exchange(sent, "wide")
    sent = call(gather_kernel, (32, 40, LANES), got, basis)
    got = exchange(sent, "narrow")
    new_modes = call(
        close_kernel,
        modes.shape,
        where,
        got,
        modes,
        to_eigen,
        from_eigen,
        eigenvalues[None],
        scalars=1,
        scratch=[(8, LANES, LANES), (1024, LANES), (4, 8, 32, LANES)],
        sems=4,
        out_far=True,
    )
    lifted = lifted.transpose(1, 0, 2)[None]
    return (new_modes, lifted, particle_push.transpose(1, 0, 2)[None, None])


def solution(mesh):
    in_specs = (
        P(None, "narrow", "wide", None),
        P(),
        P(),
        P(),
        P("wide", None),
        P("wide"),
        P("wide", "narrow", None, None, None),
        P("wide", "narrow", None, None, None),
        P("wide", "narrow", None, None),
    )
    out_specs = (
        P(None, "narrow", "wide", None),
        P("wide", "narrow", None, None),
        P("wide", "narrow", None, None, None),
    )
    return jax.shard_map(shards, mesh=mesh, in_specs=in_specs, out_specs=out_specs, check_vma=False)
```

```python
import math

import jax
import jax.numpy as jnp
import ml_dtypes
import numpy as np
from jax import lax
from jax.experimental import pallas as pl
from jax.experimental.pallas import tpu as pltpu
from jax.sharding import PartitionSpec as P

NX = 768
NZ = 768
KX = 512
KZ = 512
BED = 4
BIN = 8
COL = 48
ZB = NZ // BIN
LANES = 128

time_step = 0.003
viscous = 0.0001
reaction = 0.25
f32 = jnp.float32
bf16 = jnp.bfloat16


def basis_np(mode_count, points):
    m = np.arange(mode_count)[:, None]
    j = np.arange(points)[None, :]
    k = (m + 1) // 2
    angle = (k * j % points) * (2.0 * math.pi / points)
    table = math.sqrt(2.0 / points) * np.where(m % 2 == 1, np.cos(angle), np.sin(angle))
    return np.where(m == 0, 1.0 / math.sqrt(points), table)


def slope_np(points, mode_count):
    j = np.arange(points)[:, None]
    m = np.arange(mode_count)[None, :]
    k = (m + 1) // 2
    angle = (k * j % points) * (2.0 * math.pi / points)
    return k * math.sqrt(2.0 / points) * np.where(m % 2 == 1, np.sin(angle), -np.cos(angle))


def split_np(table):
    table = np.ascontiguousarray(table).astype(np.float32)
    high = table.astype(ml_dtypes.bfloat16)
    low = (table - high.astype(np.float32)).astype(ml_dtypes.bfloat16)
    return np.stack([high, low])


def tables():
    basis = basis_np(KX, NX)
    return split_np(basis.T), split_np(basis), split_np(-time_step * slope_np(NZ, KZ))


def halves(value):
    high = value.astype(bf16)
    return high, (value - high.astype(f32)).astype(bf16)


def mul(a, b, dims=(((1,), (0,)), ((), ()))):
    def one(p, q):
        return lax.dot_general(p, q, dims, preferred_element_type=f32)

    return one(a[0], b[0]) + (one(a[0], b[1]) + one(a[1], b[0]))


def start(copies):
    for copy in copies:
        copy.start()
    return copies


def finish(copies):
    for copy in copies:
        copy.wait()


def lane_bit(shape, bit):
    return (lax.broadcasted_iota(jnp.int32, shape, len(shape) - 1) & bit) != 0


def turn(value, shift):
    return pltpu.roll(value, shift % LANES, value.ndim - 1)


def swap(rows, bits):
    rows = list(rows)
    step = len(rows) // 2
    for bit in bits:
        upper = lane_bit(rows[0].shape, bit)
        for i in range(len(rows)):
            if i & step:
                continue
            a, b = rows[i], rows[i + step]
            rows[i] = jnp.where(upper, turn(b, bit), a)
            rows[i + step] = jnp.where(upper, b, turn(a, -bit))
        step //= 2
    return rows


def cross(value):
    row = lax.broadcasted_iota(jnp.int32, value.shape, 0)
    for sub, bit in ((4, 64), (2, 32)):
        below, right = (row & sub) != 0, lane_bit(value.shape, bit)
        down = turn(pltpu.roll(value, sub, 0), -bit)
        up = turn(pltpu.roll(value, 8 - sub, 0), bit)
        value = jnp.where(below == right, value, jnp.where(below, down, up))
    return value


def modes_of(g):
    return [(g // 2) * 8 + g % 2 + 2 * k for k in range(4)]


def open_kernel(modes, out, flat):
    for c in range(2):
        for g in range(4):
            at = c * 4 + g
            flat[at] = jnp.concatenate([modes[c, k] for k in modes_of(g)], axis=0).T
            rows = [flat[at, pl.ds(y, 32, stride=4), :] for y in range(4)]
            for k, row in zip(modes_of(g), swap(rows, (64, 32))):
                out[:, c * 16 + k, :] = row
    bed = swap([cross(flat[:, p, :]) for p in range(BED)], (16, 8))
    for nx in range(4):
        out[nx * 8 : nx * 8 + 8, 32:40, :] = jnp.broadcast_to(bed[nx][None], (8, 8, LANES))


def spread_bed_kernel(got, table, out):
    block = got[:, 32:40, :]
    block = jnp.concatenate([block, turn(block, -32)], axis=1).reshape(KX, LANES)
    bed = mul((table[0], table[1]), halves(block))
    upper = lane_bit((24, LANES), 32)
    for w in range(16):
        first = bed[w * COL : w * COL + 24]
        second = bed[w * COL + 24 : w * COL + COL]
        out[w] = jnp.where(upper, turn(second, 32), first)


def spread_kernel(got, table, out):
    block = jnp.concatenate(
        [got[:, c * 16 : c * 16 + 16, :].reshape(KX, LANES) for c in range(2)], axis=1
    )
    grid = mul((table[0], table[1]), halves(block))
    for w in range(16):
        for c in range(2):
            out[w, c * COL : c * COL + COL, :] = grid[
                w * COL : w * COL + COL, c * LANES : c * LANES + LANES
            ]


def pick(blocks, o, got):
    low, high = blocks[0, o], blocks[1, o]
    a = got[:, pl.ds(pl.multiple_of(8 * lax.rem(low, 3), 8), 8), :].reshape(LANES, LANES)
    b = got[:, pl.ds(pl.multiple_of(8 * lax.rem(high, 3), 8), 8), :].reshape(LANES, LANES)
    a = jnp.where(low >= 3, turn(a, -32), a)
    b = jnp.where(high >= 3, b, turn(b, 32))
    return jnp.where(lane_bit((LANES, LANES), 32), b, a)


def pick_kernel(blocks, where, got, out1, out2, out3):
    for k, out in enumerate((out1, out2, out3)):
        out[...] = pick(blocks, (where[2] + k + 1) & 3, got)


def product_kernel(got, basis, slope, out, held):
    for wh in range(4):
        rows = swap([got[4 * wh + wl] for wl in range(4)], (64, 32))
        for y in range(4):
            held[y * 96 : y * 96 + 96, wh * LANES : wh * LANES + LANES] = rows[y]
    speed = mul(halves(held[...]), (basis[0], basis[1])).reshape(4, 2, COL, NZ)
    product = (speed[:, 1:2] * speed).reshape(384, NZ)
    inner = mul(halves(product), (slope[0], slope[1]))
    for wh in range(4):
        part = inner[:, wh * LANES : wh * LANES + LANES]
        rows = swap([part[y * 96 : y * 96 + 96] for y in range(4)], (64, 32))
        for wl in range(4):
            out[4 * wh + wl, 0:96, :] = rows[wl]
    out[:, 96:120, :] = jnp.zeros((16, 24, LANES), f32)


def bed_kernel(
    blocks, where, own, got1, got2, got3, share, across, basis, position, velocity, size,
    out, lifted, push,
    step, near, force, grid, built, lifted_held, push_held, sems,
):
    for k, got in enumerate((None, got1, got2, got3)):
        nx = (where[2] - k) & 3
        block = pick(blocks, nx, own) if k == 0 else got[...]
        rows = swap([block[w * 8 : w * 8 + 8] for w in range(16)], (16, 8, 64, 32))
        step[nx] = jnp.concatenate(rows, axis=0)
    lines = jnp.concatenate(swap([step[nx] for nx in range(4)], (16, 8)), axis=1)
    speed = mul(halves(lines), (basis[0], basis[1]))
    means = []
    for q in range(4):
        parts = [
            speed[(p * 4 + q) * 8 : (p * 4 + q) * 8 + 8] * across[pl.ds(p * 2 + q % 2, 1), :]
            for p in range(BED)
        ]
        means.append((parts[0] + parts[1]) + (parts[2] + parts[3]))
    means = jnp.concatenate(means * 4, axis=0)
    for t in range(6):
        near[t * 16 : t * 16 + 16] = means[:, t * LANES : t * LANES + LANES].T.reshape(
            16, BIN, LANES
        )
    force[...] = jnp.zeros(force.shape, f32)

    offset, owned = where[0], where[1]
    lane = lax.broadcasted_iota(jnp.int32, (BIN, LANES), 1)
    slots = position.shape[1]
    bases = (0, 16, 32, slots - 16)
    spots = []
    for i, base in enumerate(bases):
        for s in range(16):
            index = offset + (base + s)
            row = (index >= ZB).astype(jnp.int32)
            spots.append((index - ZB * row, row))
            cells = near[index - ZB * row]
            for c in range(2):
                cell = pltpu.roll(cells, (s * 8 - c * 16 - row * 8) & (LANES - 1), 1)
                at = s * 16 + c * 8
                grid[i, at : at + 8, :] = jnp.where(lane >> 3 == s, cell, 0.0)

    centre = lax.broadcasted_iota(jnp.int32, (16, BIN, LANES), 1).astype(f32) + 0.5
    spans = [slice(base, base + 16) for base in bases]
    weight_x = [jnp.exp(-0.5 * (position[0, span][:, None, :] - centre) ** 2) for span in spans]
    weight_z = [jnp.exp(-0.5 * (position[1, span][:, None, :] - centre) ** 2) for span in spans]
    flat_x = [halves(weight.reshape(LANES, LANES)) for weight in weight_x]
    part = [mul(halves(grid[i]), flat_x[i]).reshape(16, 2, BIN, LANES) for i in range(4)]
    pulls = []
    for i, span in enumerate(spans):
        totals = jnp.sum(weight_x[i], axis=1) * jnp.sum(weight_z[i], axis=1)
        felt = [jnp.sum(part[i][:, c] * weight_z[i], axis=1) / totals for c in range(2)]
        relative = [felt[c] - velocity[c, span] for c in range(2)]
        magnitude = jnp.sqrt(relative[0] * relative[0] + relative[1] * relative[1] + 0.1)
        diameter = size[span]
        squared = diameter * diameter
        lift = 0.5 * squared * (felt[0] * felt[0] + felt[1] * felt[1])
        active = lax.broadcasted_iota(jnp.int32, (16, LANES), 0) + bases[i] < owned
        chance = jnp.where(
            active, jax.nn.sigmoid((lift - 0.5 * squared * diameter) / 0.25), 0.0
        )
        lifted_held[span, 0, :] = chance
        pull = []
        for c in range(2):
            pushed = jnp.where(
                active, 0.5 * squared * relative[c] * magnitude * (1.0 + chance), 0.0
            )
            push_held[span, c, :] = pushed
            pull.append((-reaction * pushed / totals)[:, None, :] * weight_z[i])
        pulls.append(halves(jnp.stack(pull, axis=1).reshape(2 * LANES, LANES)))
    sent = start(
        [
            pltpu.make_async_copy(lifted_held, lifted, sems.at[0]),
            pltpu.make_async_copy(push_held, push, sems.at[1]),
        ]
    )

    shape = (2 * LANES, LANES)
    mine = lax.broadcasted_iota(jnp.int32, shape, 1) >> 3 == (
        lax.broadcasted_iota(jnp.int32, shape, 0) >> 4
    )
    for i in range(4):
        cells = mul(pulls[i], flat_x[i], (((1,), (1,)), ((), ())))
        cells = jnp.where(mine, cells, 0.0)
        for bit in (8, 16, 32, 64):
            cells = cells + turn(cells, bit)
        for s in range(16):
            spot, row = spots[i * 16 + s]
            value = jnp.where(
                lane_bit((BIN, LANES), 64),
                cells[s * 16 + 8 : s * 16 + 16],
                cells[s * 16 : s * 16 + 8],
            )
            value = jnp.where((lane >> 5) & 1 == row, value, 0.0)
            force[spot] = value * share[pl.ds(spot, 1), :]

    inner = mul((basis[0], basis[1]), halves(force[...].reshape(NZ, LANES)))
    for nx in range(4):
        rows = [inner[w * 32 + nx * 8 : w * 32 + nx * 8 + 8] for w in range(16)]
        built[nx] = jnp.concatenate(swap(rows, (64, 32, 16, 8)), axis=0).T
        sent += start([pltpu.make_async_copy(built.at[nx], out.at[nx], sems.at[2 + nx])])
    finish(sent)


def place_kernel(blocks, got, main, out):
    upper = lane_bit((LANES, LANES), 32)
    for o in range(4):
        low, high = blocks[0, o], blocks[1, o]
        value = got[o]
        a = jnp.where(upper, 0.0, value)
        b = jnp.where(upper, value, 0.0)
        a = jnp.where(low >= 3, turn(a, 32), a).reshape(16, 8, LANES)
        b = jnp.where(high >= 3, b, turn(b, -32)).reshape(16, 8, LANES)
        rows = pl.ds(pl.multiple_of(96 + 8 * lax.rem(low, 3), 8), 8)
        out[:, rows, :] = out[:, rows, :] + a
        rows = pl.ds(pl.multiple_of(96 + 8 * lax.rem(high, 3), 8), 8)
        out[:, rows, :] = out[:, rows, :] + b


def gather_kernel(got, table, out):
    block = [got[:, c * COL : c * COL + COL, :].reshape(NX, LANES) for c in range(2)]
    bed = got[:, 96:120, :]
    block.append(jnp.concatenate([bed, turn(bed, -32)], axis=1).reshape(NX, LANES))
    terms = mul((table[0], table[1]), halves(jnp.concatenate(block, axis=1)))
    upper = lane_bit((8, LANES), 32)
    for n in range(32):
        part = terms[n * 16 : n * 16 + 16]
        for c in range(2):
            out[n, c * 16 : c * 16 + 16, :] = part[:, c * LANES : c * LANES + LANES]
        bed = part[:, 2 * LANES :]
        out[n, 32:40, :] = jnp.where(upper, turn(bed[8:16], 32), bed[0:8])


def close_kernel(
    where, got, modes, to_eigen, from_eigen, eigenvalues, out, flat, held, built, sems
):
    parts = [(c, g) for c in range(2) for g in range(4)]
    bed = [jnp.sum(got[nx * 8 : nx * 8 + 8, 32:40, :], axis=0) for nx in range(4)]
    bed = [cross(value) for value in swap(bed, (16, 8))]
    for c, g in parts:
        rows = swap([got[:, c * 16 + k, :] for k in modes_of(g)], (64, 32))
        for y in range(4):
            flat[c * 4 + g, pl.ds(y, 32, stride=4), :] = rows[y]
    for p in range(BED):
        flat[:, p, :] = flat[:, p, :] + bed[p]
    for c, g in parts:
        back = flat[c * 4 + g].T
        for i, k in enumerate(modes_of(g)):
            at = (c * 16 + k) * 32
            held[at : at + 32, :] = back[i * 32 : i * 32 + 32] + modes[c, k]
    across = (((1,), (1,)), ((), ()))
    forth, back = halves(from_eigen[...]), halves(to_eigen[...])
    sent = []
    for i in range(4):
        rows = slice(i * 256, i * 256 + 256)
        part = mul(halves(held[rows]), forth, across)
        row = lax.broadcasted_iota(jnp.int32, (256, LANES), 0) + i * 256
        wave_x = ((where[3] * 16 + ((row >> 5) & 15) + 1) >> 1).astype(f32)
        wave_z = ((where[4] * 32 + (row & 31) + 1) >> 1).astype(f32)
        divisor = 1.0 + viscous * (wave_x * wave_x + wave_z * wave_z + eigenvalues[...])
        result = mul(halves(part / divisor), back, across)
        built[i] = result.reshape(8, 32, LANES)
        block = out.at[i // 2, pl.ds(8 * (i % 2), 8)]
        sent += start([pltpu.make_async_copy(built.at[i], block, sems.at[i])])
    finish(sent)


def call(body, shape, *operands, scalars=0, scratch=(), sems=0, out_far=False, alias={}):
    spaces = [pltpu.SMEM] * scalars + [pltpu.VMEM] * (len(operands) - scalars)
    out_space = pl.BlockSpec(memory_space=pltpu.HBM if out_far else pltpu.VMEM)
    several = isinstance(shape, list)
    outs = [jax.ShapeDtypeStruct(one, f32) for one in (shape if several else [shape])]
    held = [pltpu.VMEM(one, f32) for one in scratch]
    bytes_moved = sum(4 * math.prod(one.shape) for one in list(operands) + outs)
    result = pl.pallas_call(
        body,
        out_shape=outs,
        in_specs=[pl.BlockSpec(memory_space=space) for space in spaces],
        out_specs=[out_space] * len(outs),
        scratch_shapes=held + ([pltpu.SemaphoreType.DMA((sems,))] if sems else []),
        compiler_params=pltpu.CompilerParams(vmem_limit_bytes=16 << 20),
        cost_estimate=pl.CostEstimate(
            flops=700_000_000, bytes_accessed=bytes_moved, transcendentals=0
        ),
        input_output_aliases=alias,
        name=body.__name__,
    )(*operands)
    return result if several else result[0]


def exchange(value, axis, groups=None):
    return lax.all_to_all(value, axis, 0, 0, axis_index_groups=groups, tiled=True)


def shards(
    modes,
    to_eigen,
    from_eigen,
    eigenvalues,
    bins_owned,
    bed_planes,
    particle_position,
    particle_velocity,
    particle_size,
):
    points, basis, slope = tables()
    narrow_at = lax.axis_index("narrow")
    wide_at = lax.axis_index("wide")
    groups = [[nz + 8 * nx for nx in range(4)] for nz in range(8)]

    counts = bins_owned[0]
    rank = jnp.arange(32, dtype=jnp.int32)
    firsts = jnp.sum(jnp.where(rank[None, :] < rank[:, None], counts[None, :], 0), axis=1)
    first_bin = jnp.sum(jnp.where(rank < narrow_at, counts, 0))
    owned_count = jnp.sum(jnp.where(rank == narrow_at, counts, 0))
    row_low = first_bin // ZB
    row_high = jnp.minimum(row_low + 1, 5)
    nz_at = narrow_at % 8
    group_low = jnp.sum(
        jnp.where(rank.reshape(4, 8) % 8 == nz_at, firsts.reshape(4, 8), 0), axis=1
    ) // ZB
    blocks = jnp.stack([group_low, jnp.minimum(group_low + 1, 5)])
    planes = bed_planes.reshape(6, ZB)
    planes = jnp.stack(
        [
            lax.dynamic_index_in_dim(planes, row_low, 0, keepdims=False),
            lax.dynamic_index_in_dim(planes, row_high, 0, keepdims=False),
        ],
        axis=1,
    )
    inside = jnp.arange(BED, dtype=jnp.int32)[None, None, :] < planes[:, :, None]
    share = jnp.where(inside, 1.0 / planes.astype(f32)[:, :, None], 0.0)
    across = jnp.repeat(share.transpose(2, 1, 0).reshape(8, ZB), BIN, axis=1)
    share = jnp.broadcast_to(share[:, None, :, :, None], (ZB, 2, 2, BED, BIN)).reshape(ZB, LANES)

    where = jnp.stack(
        [first_bin - row_low * ZB, owned_count, narrow_at // 8, narrow_at, wide_at]
    )

    sent = call(open_kernel, (32, 40, LANES), modes, scratch=[(8, LANES, LANES)])
    got = exchange(sent, "narrow")
    bed = exchange(call(spread_bed_kernel, (16, 24, LANES), got, points), "wide")
    sent = call(spread_kernel, (16, 96, LANES), got, points)
    sent, bed, blocks, where, share, across = lax.optimization_barrier(
        (sent, bed, blocks, where, share, across)
    )
    grid = exchange(sent, "wide")

    block = (LANES, LANES)
    sent = call(pick_kernel, [block] * 3, blocks, where, bed, scalars=2)
    got = []
    for k in range(1, 4):
        hops = [(x * 8 + z, (x + k) % 4 * 8 + z) for x in range(4) for z in range(8)]
        got.append(lax.ppermute(sent[k - 1], "narrow", hops))

    count = particle_size.shape[2]
    slots, pairs = (count, 1, LANES), (count, 2, LANES)
    sent, lifted, particle_push = call(
        bed_kernel,
        [(4,) + block, slots, pairs],
        blocks,
        where,
        bed,
        *got,
        share,
        across,
        basis,
        particle_position[0, 0],
        particle_velocity[0, 0],
        particle_size[0, 0],
        scalars=2,
        scratch=[
            (4,) + block,
            (ZB, BIN, LANES),
            (ZB, BIN, LANES),
            (4, 2 * LANES, LANES),
            (4,) + block,
            slots,
            pairs,
        ],
        sems=6,
        out_far=True,
    )
    got = exchange(sent, "narrow", groups)
    inner = call(product_kernel, (16, 120, LANES), grid, basis, slope, scratch=[(384, KZ)])
    sent = call(place_kernel, (16, 120, LANES), blocks, got, inner, scalars=1, alias={2: 0})

    got = exchange(sent, "wide")
    sent = call(gather_kernel, (32, 40, LANES), got, basis)
    got = exchange(sent, "narrow")
    new_modes = call(
        close_kernel,
        modes.shape,
        where,
        got,
        modes,
        to_eigen,
        from_eigen,
        eigenvalues[None],
        scalars=1,
        scratch=[(8, LANES, LANES), (1024, LANES), (4, 8, 32, LANES)],
        sems=4,
        out_far=True,
    )
    lifted = lifted.transpose(1, 0, 2)[None]
    return (new_modes, lifted, particle_push.transpose(1, 0, 2)[None, None])


def solution(mesh):
    in_specs = (
        P(None, "narrow", "wide", None),
        P(),
        P(),
        P(),
        P("wide", None),
        P("wide"),
        P("wide", "narrow", None, None, None),
        P("wide", "narrow", None, None, None),
        P("wide", "narrow", None, None),
    )
    out_specs = (
        P(None, "narrow", "wide", None),
        P("wide", "narrow", None, None),
        P("wide", "narrow", None, None, None),
    )
    return jax.shard_map(shards, mesh=mesh, in_specs=in_specs, out_specs=out_specs, check_vma=False)
```

```python
import math

import jax
import jax.numpy as jnp
import ml_dtypes
import numpy as np
from jax import lax
from jax.experimental import pallas as pl
from jax.experimental.pallas import tpu as pltpu
from jax.sharding import PartitionSpec as P

NX = 768
NZ = 768
KX = 512
KZ = 512
BED = 4
BIN = 8
COL = 48
ZB = NZ // BIN
LANES = 128

time_step = 0.003
viscous = 0.0001
reaction = 0.25
f32 = jnp.float32
bf16 = jnp.bfloat16


def basis_np(mode_count, points):
    m = np.arange(mode_count)[:, None]
    j = np.arange(points)[None, :]
    k = (m + 1) // 2
    angle = (k * j % points) * (2.0 * math.pi / points)
    table = math.sqrt(2.0 / points) * np.where(m % 2 == 1, np.cos(angle), np.sin(angle))
    return np.where(m == 0, 1.0 / math.sqrt(points), table)


def slope_np(points, mode_count):
    j = np.arange(points)[:, None]
    m = np.arange(mode_count)[None, :]
    k = (m + 1) // 2
    angle = (k * j % points) * (2.0 * math.pi / points)
    return k * math.sqrt(2.0 / points) * np.where(m % 2 == 1, np.sin(angle), -np.cos(angle))


def split_np(table):
    table = np.ascontiguousarray(table).astype(np.float32)
    high = table.astype(ml_dtypes.bfloat16)
    low = (table - high.astype(np.float32)).astype(ml_dtypes.bfloat16)
    return np.stack([high, low])


def tables():
    basis = basis_np(KX, NX)
    return split_np(basis.T), split_np(basis), split_np(-time_step * slope_np(NZ, KZ))


def halves(value):
    high = value.astype(bf16)
    return high, (value - high.astype(f32)).astype(bf16)


def mul(a, b):
    def one(p, q):
        return jnp.dot(p, q, preferred_element_type=f32)

    return one(a[0], b[0]) + (one(a[0], b[1]) + one(a[1], b[0]))


def mul_narrow(a, b):
    wide = jnp.dot(a[0], jnp.concatenate(b, axis=1), preferred_element_type=f32)
    rest = jnp.dot(a[1], b[0], preferred_element_type=f32)
    return wide[:, :LANES] + (wide[:, LANES:] + rest)


def mul_small(a, b, across=False):
    zero = jnp.zeros((LANES, LANES), bf16)
    order = [[b[0], b[0]], [b[1], zero]] if across else [[b[0], b[1]], [b[0], zero]]
    both = jnp.concatenate([jnp.concatenate(row, axis=1) for row in order], axis=0)
    dims = (((1,), (1 if across else 0,)), ((), ()))
    wide = lax.dot_general(jnp.concatenate(a, axis=1), both, dims, preferred_element_type=f32)
    return wide[:, :LANES] + wide[:, LANES:]


def start(copies):
    for copy in copies:
        copy.start()
    return copies


def finish(copies):
    for copy in copies:
        copy.wait()


def lane_bit(shape, bit):
    return (lax.broadcasted_iota(jnp.int32, shape, len(shape) - 1) & bit) != 0


def turn(value, shift):
    return pltpu.roll(value, shift % LANES, value.ndim - 1)


def swap(rows, bits):
    rows = list(rows)
    step = len(rows) // 2
    for bit in bits:
        upper = lane_bit(rows[0].shape, bit)
        for i in range(len(rows)):
            if i & step:
                continue
            a, b = rows[i], rows[i + step]
            rows[i] = jnp.where(upper, turn(b, bit), a)
            rows[i + step] = jnp.where(upper, b, turn(a, -bit))
        step //= 2
    return rows


def cross(value):
    row = lax.broadcasted_iota(jnp.int32, value.shape, 0)
    for sub, bit in ((4, 64), (2, 32)):
        below, right = (row & sub) != 0, lane_bit(value.shape, bit)
        down = turn(pltpu.roll(value, sub, 0), -bit)
        up = turn(pltpu.roll(value, 8 - sub, 0), bit)
        value = jnp.where(below == right, value, jnp.where(below, down, up))
    return value


def modes_of(g):
    return [(g // 2) * 8 + g % 2 + 2 * k for k in range(4)]


def open_kernel(modes, out, flat, built, sems):
    for c in range(2):
        for g in range(4):
            flat[c * 4 + g] = jnp.concatenate([modes[c, k] for k in modes_of(g)], axis=0).T
    bed = swap([cross(flat[:, p, :]) for p in range(BED)], (16, 8))
    sent = []
    for nx in range(4):
        for c in range(2):
            for g in range(4):
                rows = [flat[c * 4 + g, pl.ds(nx * 32 + y, 8, stride=4), :] for y in range(4)]
                for k, row in zip(modes_of(g), swap(rows, (64, 32))):
                    built[nx * 8 : nx * 8 + 8, c * 16 + k, :] = row
        built[nx * 8 : nx * 8 + 8, 32:40, :] = jnp.broadcast_to(bed[nx][None], (8, 8, LANES))
        peers = pl.ds(nx * 8, 8)
        sent += start([pltpu.make_async_copy(built.at[peers], out.at[peers], sems.at[nx])])
    finish(sent)


def spread_bed_kernel(got, table, out):
    block = got[:, 32:40, :]
    block = jnp.concatenate([block, turn(block, -32)], axis=1).reshape(KX, LANES)
    bed = mul_narrow((table[0], table[1]), halves(block))
    upper = lane_bit((24, LANES), 32)
    for w in range(16):
        first = bed[w * COL : w * COL + 24]
        second = bed[w * COL + 24 : w * COL + COL]
        out[w] = jnp.where(upper, turn(second, 32), first)


def spread_kernel(got, table, out):
    block = jnp.concatenate(
        [got[:, c * 16 : c * 16 + 16, :].reshape(KX, LANES) for c in range(2)], axis=1
    )
    grid = mul((table[0], table[1]), halves(block))
    for w in range(16):
        for c in range(2):
            out[w, c * COL : c * COL + COL, :] = grid[
                w * COL : w * COL + COL, c * LANES : c * LANES + LANES
            ]


def pick(blocks, o, got):
    low, high = blocks[0, o], blocks[1, o]
    a = got[:, pl.ds(pl.multiple_of(8 * lax.rem(low, 3), 8), 8), :].reshape(LANES, LANES)
    b = got[:, pl.ds(pl.multiple_of(8 * lax.rem(high, 3), 8), 8), :].reshape(LANES, LANES)
    a = jnp.where(low >= 3, turn(a, -32), a)
    b = jnp.where(high >= 3, b, turn(b, 32))
    return jnp.where(lane_bit((LANES, LANES), 32), b, a)


def pick_kernel(blocks, where, got, out1, out2, out3):
    for k, out in enumerate((out1, out2, out3)):
        out[...] = pick(blocks, (where[2] + k + 1) & 3, got)


def product_kernel(got, basis, slope, out, held):
    for wh in range(4):
        rows = swap([got[4 * wh + wl] for wl in range(4)], (64, 32))
        for y in range(4):
            held[y * 96 : y * 96 + 96, wh * LANES : wh * LANES + LANES] = rows[y]
    speed = mul(halves(held[...]), (basis[0], basis[1])).reshape(4, 2, COL, NZ)
    product = (speed[:, 1:2] * speed).reshape(384, NZ)
    inner = mul(halves(product), (slope[0], slope[1]))
    for wh in range(4):
        part = inner[:, wh * LANES : wh * LANES + LANES]
        rows = swap([part[y * 96 : y * 96 + 96] for y in range(4)], (64, 32))
        for wl in range(4):
            out[4 * wh + wl, 0:96, :] = rows[wl]
    out[:, 96:120, :] = jnp.zeros((16, 24, LANES), f32)


def bed_kernel(
    blocks, where, own, got1, got2, got3, share, across, basis, position, velocity, size,
    out, lifted, push,
    step, near, force, grid, built, lifted_held, push_held, sems,
):
    for k, got in enumerate((None, got1, got2, got3)):
        nx = (where[2] - k) & 3
        block = pick(blocks, nx, own) if k == 0 else got[...]
        rows = swap([block[w * 8 : w * 8 + 8] for w in range(16)], (16, 8, 64, 32))
        step[nx] = jnp.concatenate(rows, axis=0)
    lines = jnp.concatenate(swap([step[nx] for nx in range(4)], (16, 8)), axis=1)
    speed = mul(halves(lines), (basis[0], basis[1]))
    means = []
    for q in range(4):
        parts = [
            speed[(p * 4 + q) * 8 : (p * 4 + q) * 8 + 8] * across[pl.ds(p * 2 + q % 2, 1), :]
            for p in range(BED)
        ]
        means.append((parts[0] + parts[1]) + (parts[2] + parts[3]))
    means = jnp.concatenate(means * 4, axis=0)
    for t in range(6):
        near[t * 16 : t * 16 + 16] = means[:, t * LANES : t * LANES + LANES].T.reshape(
            16, BIN, LANES
        )
    force[...] = jnp.zeros(force.shape, f32)

    offset, owned = where[0], where[1]
    lane = lax.broadcasted_iota(jnp.int32, (BIN, LANES), 1)
    slots = position.shape[1]
    bases = (0, 16, 32, slots - 16)
    spots = []
    for i, base in enumerate(bases):
        for s in range(16):
            index = offset + (base + s)
            row = (index >= ZB).astype(jnp.int32)
            spots.append((index - ZB * row, row))
            cells = near[index - ZB * row]
            for c in range(2):
                cell = pltpu.roll(cells, (s * 8 - c * 16 - row * 8) & (LANES - 1), 1)
                at = s * 16 + c * 8
                grid[i, at : at + 8, :] = jnp.where(lane >> 3 == s, cell, 0.0)

    centre = lax.broadcasted_iota(jnp.int32, (16, BIN, LANES), 1).astype(f32) + 0.5
    spans = [slice(base, base + 16) for base in bases]
    weight_x = [jnp.exp(-0.5 * (position[0, span][:, None, :] - centre) ** 2) for span in spans]
    weight_z = [jnp.exp(-0.5 * (position[1, span][:, None, :] - centre) ** 2) for span in spans]
    flat_x = [halves(weight.reshape(LANES, LANES)) for weight in weight_x]
    part = [mul_small(halves(grid[i]), flat_x[i]).reshape(16, 2, BIN, LANES) for i in range(4)]
    pulls = []
    for i, span in enumerate(spans):
        totals = jnp.sum(weight_x[i], axis=1) * jnp.sum(weight_z[i], axis=1)
        felt = [jnp.sum(part[i][:, c] * weight_z[i], axis=1) / totals for c in range(2)]
        relative = [felt[c] - velocity[c, span] for c in range(2)]
        magnitude = jnp.sqrt(relative[0] * relative[0] + relative[1] * relative[1] + 0.1)
        diameter = size[span]
        squared = diameter * diameter
        lift = 0.5 * squared * (felt[0] * felt[0] + felt[1] * felt[1])
        active = lax.broadcasted_iota(jnp.int32, (16, LANES), 0) + bases[i] < owned
        chance = jnp.where(
            active, jax.nn.sigmoid((lift - 0.5 * squared * diameter) / 0.25), 0.0
        )
        lifted_held[span, 0, :] = chance
        pull = []
        for c in range(2):
            pushed = jnp.where(
                active, 0.5 * squared * relative[c] * magnitude * (1.0 + chance), 0.0
            )
            push_held[span, c, :] = pushed
            pull.append((-reaction * pushed / totals)[:, None, :] * weight_z[i])
        pulls.append(halves(jnp.stack(pull, axis=1).reshape(2 * LANES, LANES)))
    sent = start(
        [
            pltpu.make_async_copy(lifted_held, lifted, sems.at[0]),
            pltpu.make_async_copy(push_held, push, sems.at[1]),
        ]
    )

    shape = (2 * LANES, LANES)
    mine = lax.broadcasted_iota(jnp.int32, shape, 1) >> 3 == (
        lax.broadcasted_iota(jnp.int32, shape, 0) >> 4
    )
    for i in range(4):
        cells = mul_small(pulls[i], flat_x[i], True)
        cells = jnp.where(mine, cells, 0.0)
        for bit in (8, 16, 32, 64):
            cells = cells + turn(cells, bit)
        for s in range(16):
            spot, row = spots[i * 16 + s]
            value = jnp.where(
                lane_bit((BIN, LANES), 64),
                cells[s * 16 + 8 : s * 16 + 16],
                cells[s * 16 : s * 16 + 8],
            )
            value = jnp.where((lane >> 5) & 1 == row, value, 0.0)
            force[spot] = value * share[pl.ds(spot, 1), :]

    inner = mul_narrow((basis[0], basis[1]), halves(force[...].reshape(NZ, LANES)))
    for nx in range(4):
        rows = [inner[w * 32 + nx * 8 : w * 32 + nx * 8 + 8] for w in range(16)]
        built[nx] = jnp.concatenate(swap(rows, (64, 32, 16, 8)), axis=0).T
        sent += start([pltpu.make_async_copy(built.at[nx], out.at[nx], sems.at[2 + nx])])
    finish(sent)


def place_kernel(blocks, got, main, out):
    upper = lane_bit((LANES, LANES), 32)
    for o in range(4):
        low, high = blocks[0, o], blocks[1, o]
        value = got[o]
        a = jnp.where(upper, 0.0, value)
        b = jnp.where(upper, value, 0.0)
        a = jnp.where(low >= 3, turn(a, 32), a).reshape(16, 8, LANES)
        b = jnp.where(high >= 3, b, turn(b, -32)).reshape(16, 8, LANES)
        rows = pl.ds(pl.multiple_of(96 + 8 * lax.rem(low, 3), 8), 8)
        out[:, rows, :] = out[:, rows, :] + a
        rows = pl.ds(pl.multiple_of(96 + 8 * lax.rem(high, 3), 8), 8)
        out[:, rows, :] = out[:, rows, :] + b


def gather_kernel(got, table, out):
    block = [got[:, c * COL : c * COL + COL, :].reshape(NX, LANES) for c in range(2)]
    block = halves(jnp.concatenate(block, axis=1))
    bed = got[:, 96:120, :]
    bed = halves(jnp.concatenate([bed, turn(bed, -32)], axis=1).reshape(NX, LANES))
    first = jnp.dot(
        table[0], jnp.concatenate([block[0], *bed], axis=1), preferred_element_type=f32
    )
    second = jnp.dot(
        table[1], jnp.concatenate([block[0], bed[0]], axis=1), preferred_element_type=f32
    )
    third = jnp.dot(table[0], block[1], preferred_element_type=f32)
    main = first[:, : 2 * LANES] + (second[:, : 2 * LANES] + third)
    beds = first[:, 2 * LANES : 3 * LANES] + (first[:, 3 * LANES :] + second[:, 2 * LANES :])
    upper = lane_bit((8, LANES), 32)
    for n in range(32):
        part = main[n * 16 : n * 16 + 16]
        for c in range(2):
            out[n, c * 16 : c * 16 + 16, :] = part[:, c * LANES : c * LANES + LANES]
        bed = beds[n * 16 : n * 16 + 16]
        out[n, 32:40, :] = jnp.where(upper, turn(bed[8:16], 32), bed[0:8])


def close_kernel(
    where, got, modes, to_eigen, from_eigen, eigenvalues, out, flat, held, built, sems
):
    parts = [(c, g) for c in range(2) for g in range(4)]
    bed = [jnp.sum(got[nx * 8 : nx * 8 + 8, 32:40, :], axis=0) for nx in range(4)]
    bed = [cross(value) for value in swap(bed, (16, 8))]
    for c, g in parts:
        rows = swap([got[:, c * 16 + k, :] for k in modes_of(g)], (64, 32))
        for y in range(4):
            flat[c * 4 + g, pl.ds(y, 32, stride=4), :] = rows[y]
    for p in range(BED):
        flat[:, p, :] = flat[:, p, :] + bed[p]
    for c, g in parts:
        back = flat[c * 4 + g].T
        for i, k in enumerate(modes_of(g)):
            at = (c * 16 + k) * 32
            held[at : at + 32, :] = back[i * 32 : i * 32 + 32] + modes[c, k]
    forth, back = halves(from_eigen[...]), halves(to_eigen[...])
    sent = []
    for i in range(4):
        rows = slice(i * 256, i * 256 + 256)
        part = mul_small(halves(held[rows]), forth, True)
        row = lax.broadcasted_iota(jnp.int32, (256, LANES), 0) + i * 256
        wave_x = ((where[3] * 16 + ((row >> 5) & 15) + 1) >> 1).astype(f32)
        wave_z = ((where[4] * 32 + (row & 31) + 1) >> 1).astype(f32)
        divisor = 1.0 + viscous * (wave_x * wave_x + wave_z * wave_z + eigenvalues[...])
        result = mul_small(halves(part / divisor), back, True)
        built[i] = result.reshape(8, 32, LANES)
        block = out.at[i // 2, pl.ds(8 * (i % 2), 8)]
        sent += start([pltpu.make_async_copy(built.at[i], block, sems.at[i])])
    finish(sent)


def call(body, shape, *operands, scalars=0, scratch=(), sems=0, out_far=False, alias={}):
    spaces = [pltpu.SMEM] * scalars + [pltpu.VMEM] * (len(operands) - scalars)
    out_space = pl.BlockSpec(memory_space=pltpu.HBM if out_far else pltpu.VMEM)
    several = isinstance(shape, list)
    outs = [jax.ShapeDtypeStruct(one, f32) for one in (shape if several else [shape])]
    held = [pltpu.VMEM(one, f32) for one in scratch]
    bytes_moved = sum(4 * math.prod(one.shape) for one in list(operands) + outs)
    result = pl.pallas_call(
        body,
        out_shape=outs,
        in_specs=[pl.BlockSpec(memory_space=space) for space in spaces],
        out_specs=[out_space] * len(outs),
        scratch_shapes=held + ([pltpu.SemaphoreType.DMA((sems,))] if sems else []),
        compiler_params=pltpu.CompilerParams(vmem_limit_bytes=16 << 20),
        cost_estimate=pl.CostEstimate(
            flops=700_000_000, bytes_accessed=bytes_moved, transcendentals=0
        ),
        input_output_aliases=alias,
        name=body.__name__,
    )(*operands)
    return result if several else result[0]


def exchange(value, axis, groups=None):
    return lax.all_to_all(value, axis, 0, 0, axis_index_groups=groups, tiled=True)


def shards(
    modes,
    to_eigen,
    from_eigen,
    eigenvalues,
    bins_owned,
    bed_planes,
    particle_position,
    particle_velocity,
    particle_size,
):
    points, basis, slope = tables()
    narrow_at = lax.axis_index("narrow")
    wide_at = lax.axis_index("wide")
    groups = [[nz + 8 * nx for nx in range(4)] for nz in range(8)]

    counts = bins_owned[0]
    rank = jnp.arange(32, dtype=jnp.int32)
    firsts = jnp.sum(jnp.where(rank[None, :] < rank[:, None], counts[None, :], 0), axis=1)
    first_bin = jnp.sum(jnp.where(rank < narrow_at, counts, 0))
    owned_count = jnp.sum(jnp.where(rank == narrow_at, counts, 0))
    row_low = first_bin // ZB
    row_high = jnp.minimum(row_low + 1, 5)
    nz_at = narrow_at % 8
    group_low = jnp.sum(
        jnp.where(rank.reshape(4, 8) % 8 == nz_at, firsts.reshape(4, 8), 0), axis=1
    ) // ZB
    blocks = jnp.stack([group_low, jnp.minimum(group_low + 1, 5)])
    planes = bed_planes.reshape(6, ZB)
    planes = jnp.stack(
        [
            lax.dynamic_index_in_dim(planes, row_low, 0, keepdims=False),
            lax.dynamic_index_in_dim(planes, row_high, 0, keepdims=False),
        ],
        axis=1,
    )
    inside = jnp.arange(BED, dtype=jnp.int32)[None, None, :] < planes[:, :, None]
    share = jnp.where(inside, 1.0 / planes.astype(f32)[:, :, None], 0.0)
    across = jnp.repeat(share.transpose(2, 1, 0).reshape(8, ZB), BIN, axis=1)
    share = jnp.broadcast_to(share[:, None, :, :, None], (ZB, 2, 2, BED, BIN)).reshape(ZB, LANES)

    where = jnp.stack(
        [first_bin - row_low * ZB, owned_count, narrow_at // 8, narrow_at, wide_at]
    )

    sent = call(
        open_kernel,
        (32, 40, LANES),
        modes,
        scratch=[(8, LANES, LANES), (32, 40, LANES)],
        sems=4,
        out_far=True,
    )
    got = exchange(sent, "narrow")
    bed = exchange(call(spread_bed_kernel, (16, 24, LANES), got, points), "wide")
    sent = call(spread_kernel, (16, 96, LANES), got, points)
    sent, bed, blocks, where, share, across = lax.optimization_barrier(
        (sent, bed, blocks, where, share, across)
    )
    grid = exchange(sent, "wide")

    block = (LANES, LANES)
    sent = call(pick_kernel, [block] * 3, blocks, where, bed, scalars=2)
    got = []
    for k in range(1, 4):
        hops = [(x * 8 + z, (x + k) % 4 * 8 + z) for x in range(4) for z in range(8)]
        got.append(lax.ppermute(sent[k - 1], "narrow", hops))

    count = particle_size.shape[2]
    slots, pairs = (count, 1, LANES), (count, 2, LANES)
    sent, lifted, particle_push = call(
        bed_kernel,
        [(4,) + block, slots, pairs],
        blocks,
        where,
        bed,
        *got,
        share,
        across,
        basis,
        particle_position[0, 0],
        particle_velocity[0, 0],
        particle_size[0, 0],
        scalars=2,
        scratch=[
            (4,) + block,
            (ZB, BIN, LANES),
            (ZB, BIN, LANES),
            (4, 2 * LANES, LANES),
            (4,) + block,
            slots,
            pairs,
        ],
        sems=6,
        out_far=True,
    )
    got = exchange(sent, "narrow", groups)
    inner = call(product_kernel, (16, 120, LANES), grid, basis, slope, scratch=[(384, KZ)])
    sent = call(place_kernel, (16, 120, LANES), blocks, got, inner, scalars=1, alias={2: 0})

    got = exchange(sent, "wide")
    sent = call(gather_kernel, (32, 40, LANES), got, basis)
    got = exchange(sent, "narrow")
    new_modes = call(
        close_kernel,
        modes.shape,
        where,
        got,
        modes,
        to_eigen,
        from_eigen,
        eigenvalues[None],
        scalars=1,
        scratch=[(8, LANES, LANES), (1024, LANES), (4, 8, 32, LANES)],
        sems=4,
        out_far=True,
    )
    lifted = lifted.transpose(1, 0, 2)[None]
    return (new_modes, lifted, particle_push.transpose(1, 0, 2)[None, None])


def solution(mesh):
    in_specs = (
        P(None, "narrow", "wide", None),
        P(),
        P(),
        P(),
        P("wide", None),
        P("wide"),
        P("wide", "narrow", None, None, None),
        P("wide", "narrow", None, None, None),
        P("wide", "narrow", None, None),
    )
    out_specs = (
        P(None, "narrow", "wide", None),
        P("wide", "narrow", None, None),
        P("wide", "narrow", None, None, None),
    )
    return jax.shard_map(shards, mesh=mesh, in_specs=in_specs, out_specs=out_specs, check_vma=False)
```

```python
import math

import jax
import jax.numpy as jnp
import ml_dtypes
import numpy as np
from jax import lax
from jax.experimental import pallas as pl
from jax.experimental.pallas import tpu as pltpu
from jax.sharding import PartitionSpec as P

NX = 768
NZ = 768
KX = 512
KZ = 512
BED = 4
BIN = 8
COL = 48
ZB = NZ // BIN
LANES = 128

time_step = 0.003
viscous = 0.0001
reaction = 0.25
f32 = jnp.float32
bf16 = jnp.bfloat16


def basis_np(mode_count, points):
    m = np.arange(mode_count)[:, None]
    j = np.arange(points)[None, :]
    k = (m + 1) // 2
    angle = (k * j % points) * (2.0 * math.pi / points)
    table = math.sqrt(2.0 / points) * np.where(m % 2 == 1, np.cos(angle), np.sin(angle))
    return np.where(m == 0, 1.0 / math.sqrt(points), table)


def slope_np(points, mode_count):
    j = np.arange(points)[:, None]
    m = np.arange(mode_count)[None, :]
    k = (m + 1) // 2
    angle = (k * j % points) * (2.0 * math.pi / points)
    return k * math.sqrt(2.0 / points) * np.where(m % 2 == 1, np.sin(angle), -np.cos(angle))


def split_np(table):
    table = np.ascontiguousarray(table).astype(np.float32)
    high = table.astype(ml_dtypes.bfloat16)
    low = (table - high.astype(np.float32)).astype(ml_dtypes.bfloat16)
    return np.stack([high, low])


def tables():
    basis = basis_np(KX, NX)
    return split_np(basis.T), split_np(basis), split_np(-time_step * slope_np(NZ, KZ))


def halves(value):
    high = value.astype(bf16)
    return high, (value - high.astype(f32)).astype(bf16)


def mul(a, b):
    def one(p, q):
        return jnp.dot(p, q, preferred_element_type=f32)

    return one(a[0], b[0]) + (one(a[0], b[1]) + one(a[1], b[0]))


def mul_narrow(a, b):
    wide = jnp.dot(a[0], jnp.concatenate(b, axis=1), preferred_element_type=f32)
    rest = jnp.dot(a[1], b[0], preferred_element_type=f32)
    return wide[:, :LANES] + (wide[:, LANES:] + rest)


def mul_small(a, b, across=False):
    zero = jnp.zeros((LANES, LANES), bf16)
    order = [[b[0], b[0]], [b[1], zero]] if across else [[b[0], b[1]], [b[0], zero]]
    both = jnp.concatenate([jnp.concatenate(row, axis=1) for row in order], axis=0)
    dims = (((1,), (1 if across else 0,)), ((), ()))
    wide = lax.dot_general(jnp.concatenate(a, axis=1), both, dims, preferred_element_type=f32)
    return wide[:, :LANES] + wide[:, LANES:]


def start(copies):
    for copy in copies:
        copy.start()
    return copies


def finish(copies):
    for copy in copies:
        copy.wait()


def lane_bit(shape, bit):
    return (lax.broadcasted_iota(jnp.int32, shape, len(shape) - 1) & bit) != 0


def turn(value, shift):
    return pltpu.roll(value, shift % LANES, value.ndim - 1)


def swap(rows, bits):
    rows = list(rows)
    step = len(rows) // 2
    for bit in bits:
        upper = lane_bit(rows[0].shape, bit)
        for i in range(len(rows)):
            if i & step:
                continue
            a, b = rows[i], rows[i + step]
            rows[i] = jnp.where(upper, turn(b, bit), a)
            rows[i + step] = jnp.where(upper, b, turn(a, -bit))
        step //= 2
    return rows


def cross(value):
    row = lax.broadcasted_iota(jnp.int32, value.shape, 0)
    for sub, bit in ((4, 64), (2, 32)):
        below, right = (row & sub) != 0, lane_bit(value.shape, bit)
        down = turn(pltpu.roll(value, sub, 0), -bit)
        up = turn(pltpu.roll(value, 8 - sub, 0), bit)
        value = jnp.where(below == right, value, jnp.where(below, down, up))
    return value


def modes_of(g):
    return [(g // 2) * 8 + g % 2 + 2 * k for k in range(4)]


def open_kernel(modes, out, flat):
    for c in range(2):
        for g in range(4):
            at = c * 4 + g
            flat[at] = jnp.concatenate([modes[c, k] for k in modes_of(g)], axis=0).T
            rows = [flat[at, pl.ds(y, 32, stride=4), :] for y in range(4)]
            for k, row in zip(modes_of(g), swap(rows, (64, 32))):
                out[:, c * 16 + k, :] = row
    bed = swap([cross(flat[:, p, :]) for p in range(BED)], (16, 8))
    for nx in range(4):
        out[nx * 8 : nx * 8 + 8, 32:40, :] = jnp.broadcast_to(bed[nx][None], (8, 8, LANES))


def spread_bed_kernel(got, table, out):
    block = got[:, 32:40, :]
    block = jnp.concatenate([block, turn(block, -32)], axis=1).reshape(KX, LANES)
    bed = mul_narrow((table[0], table[1]), halves(block))
    upper = lane_bit((24, LANES), 32)
    for w in range(16):
        first = bed[w * COL : w * COL + 24]
        second = bed[w * COL + 24 : w * COL + COL]
        out[w] = jnp.where(upper, turn(second, 32), first)


def spread_kernel(got, table, out):
    block = jnp.concatenate(
        [got[:, c * 16 : c * 16 + 16, :].reshape(KX, LANES) for c in range(2)], axis=1
    )
    grid = mul((table[0], table[1]), halves(block))
    for w in range(16):
        for c in range(2):
            out[w, c * COL : c * COL + COL, :] = grid[
                w * COL : w * COL + COL, c * LANES : c * LANES + LANES
            ]


def pick(blocks, o, got):
    low, high = blocks[0, o], blocks[1, o]
    a = got[:, pl.ds(pl.multiple_of(8 * lax.rem(low, 3), 8), 8), :].reshape(LANES, LANES)
    b = got[:, pl.ds(pl.multiple_of(8 * lax.rem(high, 3), 8), 8), :].reshape(LANES, LANES)
    a = jnp.where(low >= 3, turn(a, -32), a)
    b = jnp.where(high >= 3, b, turn(b, 32))
    return jnp.where(lane_bit((LANES, LANES), 32), b, a)


def pick_kernel(blocks, where, got, out1, out2, out3):
    for k, out in enumerate((out1, out2, out3)):
        out[...] = pick(blocks, (where[2] + k + 1) & 3, got)


def product_kernel(got, basis, slope, out, held):
    for wh in range(4):
        rows = swap([got[4 * wh + wl] for wl in range(4)], (64, 32))
        for y in range(4):
            held[y * 96 : y * 96 + 96, wh * LANES : wh * LANES + LANES] = rows[y]
    speed = mul(halves(held[...]), (basis[0], basis[1])).reshape(4, 2, COL, NZ)
    product = (speed[:, 1:2] * speed).reshape(384, NZ)
    inner = mul(halves(product), (slope[0], slope[1]))
    for wh in range(4):
        part = inner[:, wh * LANES : wh * LANES + LANES]
        rows = swap([part[y * 96 : y * 96 + 96] for y in range(4)], (64, 32))
        for wl in range(4):
            out[4 * wh + wl, 0:96, :] = rows[wl]
    out[:, 96:120, :] = jnp.zeros((16, 24, LANES), f32)


def bed_kernel(
    blocks, where, own, got1, got2, got3, share, across, basis, position, velocity, size,
    out, lifted, push,
    step, near, force, grid, built, lifted_held, push_held, sems,
):
    for k, got in enumerate((None, got1, got2, got3)):
        nx = (where[2] - k) & 3
        block = pick(blocks, nx, own) if k == 0 else got[...]
        rows = swap([block[w * 8 : w * 8 + 8] for w in range(16)], (16, 8, 64, 32))
        step[nx] = jnp.concatenate(rows, axis=0)
    lines = jnp.concatenate(swap([step[nx] for nx in range(4)], (16, 8)), axis=1)
    speed = mul(halves(lines), (basis[0], basis[1]))
    means = []
    for q in range(4):
        parts = [
            speed[(p * 4 + q) * 8 : (p * 4 + q) * 8 + 8] * across[pl.ds(p * 2 + q % 2, 1), :]
            for p in range(BED)
        ]
        means.append((parts[0] + parts[1]) + (parts[2] + parts[3]))
    means = jnp.concatenate(means * 4, axis=0)
    for t in range(6):
        near[t * 16 : t * 16 + 16] = means[:, t * LANES : t * LANES + LANES].T.reshape(
            16, BIN, LANES
        )
    force[...] = jnp.zeros(force.shape, f32)

    offset, owned = where[0], where[1]
    lane = lax.broadcasted_iota(jnp.int32, (BIN, LANES), 1)
    slots = position.shape[1]
    bases = (0, 16, 32, slots - 16)
    spots = []
    for i, base in enumerate(bases):
        for s in range(16):
            index = offset + (base + s)
            row = (index >= ZB).astype(jnp.int32)
            spots.append((index - ZB * row, row))
            cells = near[index - ZB * row]
            for c in range(2):
                cell = pltpu.roll(cells, (s * 8 - c * 16 - row * 8) & (LANES - 1), 1)
                at = s * 16 + c * 8
                grid[i, at : at + 8, :] = jnp.where(lane >> 3 == s, cell, 0.0)

    centre = lax.broadcasted_iota(jnp.int32, (16, BIN, LANES), 1).astype(f32) + 0.5
    spans = [slice(base, base + 16) for base in bases]
    weight_x = [jnp.exp(-0.5 * (position[0, span][:, None, :] - centre) ** 2) for span in spans]
    weight_z = [jnp.exp(-0.5 * (position[1, span][:, None, :] - centre) ** 2) for span in spans]
    flat_x = [halves(weight.reshape(LANES, LANES)) for weight in weight_x]
    part = [mul_small(halves(grid[i]), flat_x[i]).reshape(16, 2, BIN, LANES) for i in range(4)]
    pulls = []
    for i, span in enumerate(spans):
        totals = jnp.sum(weight_x[i], axis=1) * jnp.sum(weight_z[i], axis=1)
        felt = [jnp.sum(part[i][:, c] * weight_z[i], axis=1) / totals for c in range(2)]
        relative = [felt[c] - velocity[c, span] for c in range(2)]
        magnitude = jnp.sqrt(relative[0] * relative[0] + relative[1] * relative[1] + 0.1)
        diameter = size[span]
        squared = diameter * diameter
        lift = 0.5 * squared * (felt[0] * felt[0] + felt[1] * felt[1])
        active = lax.broadcasted_iota(jnp.int32, (16, LANES), 0) + bases[i] < owned
        chance = jnp.where(
            active, jax.nn.sigmoid((lift - 0.5 * squared * diameter) / 0.25), 0.0
        )
        lifted_held[span, 0, :] = chance
        pull = []
        for c in range(2):
            pushed = jnp.where(
                active, 0.5 * squared * relative[c] * magnitude * (1.0 + chance), 0.0
            )
            push_held[span, c, :] = pushed
            pull.append((-reaction * pushed / totals)[:, None, :] * weight_z[i])
        pulls.append(halves(jnp.stack(pull, axis=1).reshape(2 * LANES, LANES)))
    sent = start(
        [
            pltpu.make_async_copy(lifted_held, lifted, sems.at[0]),
            pltpu.make_async_copy(push_held, push, sems.at[1]),
        ]
    )

    shape = (2 * LANES, LANES)
    mine = lax.broadcasted_iota(jnp.int32, shape, 1) >> 3 == (
        lax.broadcasted_iota(jnp.int32, shape, 0) >> 4
    )
    for i in range(4):
        cells = mul_small(pulls[i], flat_x[i], True)
        cells = jnp.where(mine, cells, 0.0)
        for bit in (8, 16, 32, 64):
            cells = cells + turn(cells, bit)
        for s in range(16):
            spot, row = spots[i * 16 + s]
            value = jnp.where(
                lane_bit((BIN, LANES), 64),
                cells[s * 16 + 8 : s * 16 + 16],
                cells[s * 16 : s * 16 + 8],
            )
            value = jnp.where((lane >> 5) & 1 == row, value, 0.0)
            force[spot] = value * share[pl.ds(spot, 1), :]

    inner = mul_narrow((basis[0], basis[1]), halves(force[...].reshape(NZ, LANES)))
    for nx in range(4):
        rows = [inner[w * 32 + nx * 8 : w * 32 + nx * 8 + 8] for w in range(16)]
        built[nx] = jnp.concatenate(swap(rows, (64, 32, 16, 8)), axis=0).T
        sent += start([pltpu.make_async_copy(built.at[nx], out.at[nx], sems.at[2 + nx])])
    finish(sent)


def place_kernel(blocks, got, main, out):
    upper = lane_bit((LANES, LANES), 32)
    for o in range(4):
        low, high = blocks[0, o], blocks[1, o]
        value = got[o]
        a = jnp.where(upper, 0.0, value)
        b = jnp.where(upper, value, 0.0)
        a = jnp.where(low >= 3, turn(a, 32), a).reshape(16, 8, LANES)
        b = jnp.where(high >= 3, b, turn(b, -32)).reshape(16, 8, LANES)
        rows = pl.ds(pl.multiple_of(96 + 8 * lax.rem(low, 3), 8), 8)
        out[:, rows, :] = out[:, rows, :] + a
        rows = pl.ds(pl.multiple_of(96 + 8 * lax.rem(high, 3), 8), 8)
        out[:, rows, :] = out[:, rows, :] + b


def gather_kernel(got, table, out):
    block = [got[:, c * COL : c * COL + COL, :].reshape(NX, LANES) for c in range(2)]
    block = halves(jnp.concatenate(block, axis=1))
    bed = got[:, 96:120, :]
    bed = halves(jnp.concatenate([bed, turn(bed, -32)], axis=1).reshape(NX, LANES))
    first = jnp.dot(
        table[0], jnp.concatenate([block[0], *bed], axis=1), preferred_element_type=f32
    )
    second = jnp.dot(
        table[1], jnp.concatenate([block[0], bed[0]], axis=1), preferred_element_type=f32
    )
    third = jnp.dot(table[0], block[1], preferred_element_type=f32)
    main = first[:, : 2 * LANES] + (second[:, : 2 * LANES] + third)
    beds = first[:, 2 * LANES : 3 * LANES] + (first[:, 3 * LANES :] + second[:, 2 * LANES :])
    upper = lane_bit((8, LANES), 32)
    for n in range(32):
        part = main[n * 16 : n * 16 + 16]
        for c in range(2):
            out[n, c * 16 : c * 16 + 16, :] = part[:, c * LANES : c * LANES + LANES]
        bed = beds[n * 16 : n * 16 + 16]
        out[n, 32:40, :] = jnp.where(upper, turn(bed[8:16], 32), bed[0:8])


def close_kernel(
    where, got, modes, to_eigen, from_eigen, eigenvalues, out, flat, held, built, sems
):
    parts = [(c, g) for c in range(2) for g in range(4)]
    bed = [jnp.sum(got[nx * 8 : nx * 8 + 8, 32:40, :], axis=0) for nx in range(4)]
    bed = [cross(value) for value in swap(bed, (16, 8))]
    for c, g in parts:
        rows = swap([got[:, c * 16 + k, :] for k in modes_of(g)], (64, 32))
        for y in range(4):
            flat[c * 4 + g, pl.ds(y, 32, stride=4), :] = rows[y]
    for p in range(BED):
        flat[:, p, :] = flat[:, p, :] + bed[p]
    for c, g in parts:
        back = flat[c * 4 + g].T
        for i, k in enumerate(modes_of(g)):
            at = (c * 16 + k) * 32
            held[at : at + 32, :] = back[i * 32 : i * 32 + 32] + modes[c, k]
    forth, back = halves(from_eigen[...]), halves(to_eigen[...])
    sent = []
    for i in range(4):
        rows = slice(i * 256, i * 256 + 256)
        part = mul_small(halves(held[rows]), forth, True)
        row = lax.broadcasted_iota(jnp.int32, (256, LANES), 0) + i * 256
        wave_x = ((where[3] * 16 + ((row >> 5) & 15) + 1) >> 1).astype(f32)
        wave_z = ((where[4] * 32 + (row & 31) + 1) >> 1).astype(f32)
        divisor = 1.0 + viscous * (wave_x * wave_x + wave_z * wave_z + eigenvalues[...])
        result = mul_small(halves(part / divisor), back, True)
        built[i] = result.reshape(8, 32, LANES)
        block = out.at[i // 2, pl.ds(8 * (i % 2), 8)]
        sent += start([pltpu.make_async_copy(built.at[i], block, sems.at[i])])
    finish(sent)


def call(body, shape, *operands, scalars=0, scratch=(), sems=0, out_far=False, alias={}):
    spaces = [pltpu.SMEM] * scalars + [pltpu.VMEM] * (len(operands) - scalars)
    out_space = pl.BlockSpec(memory_space=pltpu.HBM if out_far else pltpu.VMEM)
    several = isinstance(shape, list)
    outs = [jax.ShapeDtypeStruct(one, f32) for one in (shape if several else [shape])]
    held = [pltpu.VMEM(one, f32) for one in scratch]
    bytes_moved = sum(4 * math.prod(one.shape) for one in list(operands) + outs)
    result = pl.pallas_call(
        body,
        out_shape=outs,
        in_specs=[pl.BlockSpec(memory_space=space) for space in spaces],
        out_specs=[out_space] * len(outs),
        scratch_shapes=held + ([pltpu.SemaphoreType.DMA((sems,))] if sems else []),
        compiler_params=pltpu.CompilerParams(vmem_limit_bytes=16 << 20),
        cost_estimate=pl.CostEstimate(
            flops=700_000_000, bytes_accessed=bytes_moved, transcendentals=0
        ),
        input_output_aliases=alias,
        name=body.__name__,
    )(*operands)
    return result if several else result[0]


def exchange(value, axis, groups=None):
    return lax.all_to_all(value, axis, 0, 0, axis_index_groups=groups, tiled=True)


def shards(
    modes,
    to_eigen,
    from_eigen,
    eigenvalues,
    bins_owned,
    bed_planes,
    particle_position,
    particle_velocity,
    particle_size,
):
    points, basis, slope = tables()
    narrow_at = lax.axis_index("narrow")
    wide_at = lax.axis_index("wide")
    groups = [[nz + 8 * nx for nx in range(4)] for nz in range(8)]

    counts = bins_owned[0]
    rank = jnp.arange(32, dtype=jnp.int32)
    firsts = jnp.sum(jnp.where(rank[None, :] < rank[:, None], counts[None, :], 0), axis=1)
    first_bin = jnp.sum(jnp.where(rank < narrow_at, counts, 0))
    owned_count = jnp.sum(jnp.where(rank == narrow_at, counts, 0))
    row_low = first_bin // ZB
    row_high = jnp.minimum(row_low + 1, 5)
    nz_at = narrow_at % 8
    group_low = jnp.sum(
        jnp.where(rank.reshape(4, 8) % 8 == nz_at, firsts.reshape(4, 8), 0), axis=1
    ) // ZB
    blocks = jnp.stack([group_low, jnp.minimum(group_low + 1, 5)])
    planes = bed_planes.reshape(6, ZB)
    planes = jnp.stack(
        [
            lax.dynamic_index_in_dim(planes, row_low, 0, keepdims=False),
            lax.dynamic_index_in_dim(planes, row_high, 0, keepdims=False),
        ],
        axis=1,
    )
    inside = jnp.arange(BED, dtype=jnp.int32)[None, None, :] < planes[:, :, None]
    share = jnp.where(inside, 1.0 / planes.astype(f32)[:, :, None], 0.0)
    across = jnp.repeat(share.transpose(2, 1, 0).reshape(8, ZB), BIN, axis=1)
    share = jnp.broadcast_to(share[:, None, :, :, None], (ZB, 2, 2, BED, BIN)).reshape(ZB, LANES)

    where = jnp.stack(
        [first_bin - row_low * ZB, owned_count, narrow_at // 8, narrow_at, wide_at]
    )

    sent = call(open_kernel, (32, 40, LANES), modes, scratch=[(8, LANES, LANES)])
    got = exchange(sent, "narrow")
    bed = exchange(call(spread_bed_kernel, (16, 24, LANES), got, points), "wide")
    sent = call(spread_kernel, (16, 96, LANES), got, points)
    sent, bed, blocks, where, share, across = lax.optimization_barrier(
        (sent, bed, blocks, where, share, across)
    )
    grid = exchange(sent, "wide")

    block = (LANES, LANES)
    sent = call(pick_kernel, [block] * 3, blocks, where, bed, scalars=2)
    got = []
    for k in range(1, 4):
        hops = [(x * 8 + z, (x + k) % 4 * 8 + z) for x in range(4) for z in range(8)]
        got.append(lax.ppermute(sent[k - 1], "narrow", hops))

    count = particle_size.shape[2]
    slots, pairs = (count, 1, LANES), (count, 2, LANES)
    sent, lifted, particle_push = call(
        bed_kernel,
        [(4,) + block, slots, pairs],
        blocks,
        where,
        bed,
        *got,
        share,
        across,
        basis,
        particle_position[0, 0],
        particle_velocity[0, 0],
        particle_size[0, 0],
        scalars=2,
        scratch=[
            (4,) + block,
            (ZB, BIN, LANES),
            (ZB, BIN, LANES),
            (4, 2 * LANES, LANES),
            (4,) + block,
            slots,
            pairs,
        ],
        sems=6,
        out_far=True,
    )
    got = exchange(sent, "narrow", groups)
    inner = call(product_kernel, (16, 120, LANES), grid, basis, slope, scratch=[(384, KZ)])
    sent = call(place_kernel, (16, 120, LANES), blocks, got, inner, scalars=1, alias={2: 0})

    got = exchange(sent, "wide")
    sent = call(gather_kernel, (32, 40, LANES), got, basis)
    got = exchange(sent, "narrow")
    new_modes = call(
        close_kernel,
        modes.shape,
        where,
        got,
        modes,
        to_eigen,
        from_eigen,
        eigenvalues[None],
        scalars=1,
        scratch=[(8, LANES, LANES), (1024, LANES), (4, 8, 32, LANES)],
        sems=4,
        out_far=True,
    )
    lifted = lifted.transpose(1, 0, 2)[None]
    return (new_modes, lifted, particle_push.transpose(1, 0, 2)[None, None])


def solution(mesh):
    in_specs = (
        P(None, "narrow", "wide", None),
        P(),
        P(),
        P(),
        P("wide", None),
        P("wide"),
        P("wide", "narrow", None, None, None),
        P("wide", "narrow", None, None, None),
        P("wide", "narrow", None, None),
    )
    out_specs = (
        P(None, "narrow", "wide", None),
        P("wide", "narrow", None, None),
        P("wide", "narrow", None, None, None),
    )
    return jax.shard_map(shards, mesh=mesh, in_specs=in_specs, out_specs=out_specs, check_vma=False)
```

```python
import math

import jax
import jax.numpy as jnp
import ml_dtypes
import numpy as np
from jax import lax
from jax.experimental import pallas as pl
from jax.experimental.pallas import tpu as pltpu
from jax.sharding import PartitionSpec as P

NX = 768
NZ = 768
KX = 512
KZ = 512
BED = 4
BIN = 8
COL = 48
ZB = NZ // BIN
LANES = 128

time_step = 0.003
viscous = 0.0001
reaction = 0.25
f32 = jnp.float32
bf16 = jnp.bfloat16


def basis_np(mode_count, points):
    m = np.arange(mode_count)[:, None]
    j = np.arange(points)[None, :]
    k = (m + 1) // 2
    angle = (k * j % points) * (2.0 * math.pi / points)
    table = math.sqrt(2.0 / points) * np.where(m % 2 == 1, np.cos(angle), np.sin(angle))
    return np.where(m == 0, 1.0 / math.sqrt(points), table)


def slope_np(points, mode_count):
    j = np.arange(points)[:, None]
    m = np.arange(mode_count)[None, :]
    k = (m + 1) // 2
    angle = (k * j % points) * (2.0 * math.pi / points)
    return k * math.sqrt(2.0 / points) * np.where(m % 2 == 1, np.sin(angle), -np.cos(angle))


def split_np(table):
    table = np.ascontiguousarray(table).astype(np.float32)
    high = table.astype(ml_dtypes.bfloat16)
    low = (table - high.astype(np.float32)).astype(ml_dtypes.bfloat16)
    return np.stack([high, low])


def tables():
    basis = basis_np(KX, NX)
    return split_np(basis.T), split_np(basis), split_np(-time_step * slope_np(NZ, KZ))


def halves(value):
    high = value.astype(bf16)
    return high, (value - high.astype(f32)).astype(bf16)


def mul(a, b):
    def one(p, q):
        return jnp.dot(p, q, preferred_element_type=f32)

    return one(a[0], b[0]) + (one(a[0], b[1]) + one(a[1], b[0]))


def mul_narrow(a, b):
    wide = jnp.dot(a[0], jnp.concatenate(b, axis=1), preferred_element_type=f32)
    rest = jnp.dot(a[1], b[0], preferred_element_type=f32)
    return wide[:, :LANES] + (wide[:, LANES:] + rest)


def mul_small(a, b, across=False):
    zero = jnp.zeros((LANES, LANES), bf16)
    order = [[b[0], b[0]], [b[1], zero]] if across else [[b[0], b[1]], [b[0], zero]]
    both = jnp.concatenate([jnp.concatenate(row, axis=1) for row in order], axis=0)
    dims = (((1,), (1 if across else 0,)), ((), ()))
    wide = lax.dot_general(jnp.concatenate(a, axis=1), both, dims, preferred_element_type=f32)
    return wide[:, :LANES] + wide[:, LANES:]


def start(copies):
    for copy in copies:
        copy.start()
    return copies


def finish(copies):
    for copy in copies:
        copy.wait()


def lane_bit(shape, bit):
    return (lax.broadcasted_iota(jnp.int32, shape, len(shape) - 1) & bit) != 0


def turn(value, shift):
    return pltpu.roll(value, shift % LANES, value.ndim - 1)


def swap(rows, bits):
    rows = list(rows)
    step = len(rows) // 2
    for bit in bits:
        upper = lane_bit(rows[0].shape, bit)
        for i in range(len(rows)):
            if i & step:
                continue
            a, b = rows[i], rows[i + step]
            rows[i] = jnp.where(upper, turn(b, bit), a)
            rows[i + step] = jnp.where(upper, b, turn(a, -bit))
        step //= 2
    return rows


def cross(value):
    row = lax.broadcasted_iota(jnp.int32, value.shape, 0)
    for sub, bit in ((4, 64), (2, 32)):
        below, right = (row & sub) != 0, lane_bit(value.shape, bit)
        down = turn(pltpu.roll(value, sub, 0), -bit)
        up = turn(pltpu.roll(value, 8 - sub, 0), bit)
        value = jnp.where(below == right, value, jnp.where(below, down, up))
    return value


def modes_of(g):
    return [(g // 2) * 8 + g % 2 + 2 * k for k in range(4)]


def open_kernel(modes, out, flat):
    for c in range(2):
        for g in range(4):
            at = c * 4 + g
            flat[at] = jnp.concatenate([modes[c, k] for k in modes_of(g)], axis=0).T
            rows = [flat[at, pl.ds(y, 32, stride=4), :] for y in range(4)]
            for k, row in zip(modes_of(g), swap(rows, (64, 32))):
                out[:, c * 16 + k, :] = row
    bed = swap([cross(flat[:, p, :]) for p in range(BED)], (16, 8))
    for nx in range(4):
        out[nx * 8 : nx * 8 + 8, 32:40, :] = jnp.broadcast_to(bed[nx][None], (8, 8, LANES))


def spread_bed_kernel(got, table, out):
    block = got[:, 32:40, :]
    block = jnp.concatenate([block, turn(block, -32)], axis=1).reshape(KX, LANES)
    bed = mul_narrow((table[0], table[1]), halves(block))
    upper = lane_bit((24, LANES), 32)
    for w in range(16):
        first = bed[w * COL : w * COL + 24]
        second = bed[w * COL + 24 : w * COL + COL]
        out[w] = jnp.where(upper, turn(second, 32), first)


def spread_kernel(got, table, out):
    block = jnp.concatenate(
        [got[:, c * 16 : c * 16 + 16, :].reshape(KX, LANES) for c in range(2)], axis=1
    )
    grid = mul((table[0], table[1]), halves(block))
    for w in range(16):
        for c in range(2):
            out[w, c * COL : c * COL + COL, :] = grid[
                w * COL : w * COL + COL, c * LANES : c * LANES + LANES
            ]


def map_kernel(place, bins_owned, bed_planes, blocks, where, share, across, firsts, planes):
    total = jnp.int32(0)
    for n in range(32):
        firsts[n] = total
        total = total + bins_owned[0, n]
    narrow_at = place[0]
    first = firsts[narrow_at]
    low = lax.div(first, ZB)
    high = jnp.minimum(low + 1, 5)
    where[0] = first - ZB * low
    where[1] = bins_owned[0, narrow_at]
    where[2] = lax.div(narrow_at, 8)
    where[3] = narrow_at
    where[4] = place[1]
    for nx in range(4):
        row = lax.div(firsts[nx * 8 + (narrow_at & 7)], ZB)
        blocks[0, nx] = row
        blocks[1, nx] = jnp.minimum(row + 1, 5)

    planes[...] = jnp.zeros((LANES, LANES), f32)
    planes[0:6, 0:ZB] = bed_planes[...].astype(f32)
    table = planes[...].astype(bf16)

    def row_of(odd):
        return jnp.where(odd, high, low)

    shape = (LANES, LANES)
    index, lane = (lax.broadcasted_iota(jnp.int32, shape, i) for i in (0, 1))
    chosen = (index == row_of(lane_bit(shape, 32))).astype(f32).astype(bf16)
    count = jnp.dot(planes[...].T.astype(bf16), chosen, preferred_element_type=f32)[:ZB]
    plane = ((lane >> 3) & 3)[:ZB].astype(f32)
    share[...] = jnp.where(plane < count, 1.0 / jnp.maximum(count, 1.0), 0.0)

    chosen = (lane == row_of((index & 1) != 0)).astype(f32).astype(bf16)
    count = jnp.dot(chosen, table, preferred_element_type=f32).astype(bf16)
    wide = (LANES, NZ)
    spread = lax.broadcasted_iota(jnp.int32, wide, 1) >> 3 == lax.broadcasted_iota(jnp.int32, wide, 0)
    count = jnp.dot(count, spread.astype(f32).astype(bf16), preferred_element_type=f32)[:8]
    plane = (lax.broadcasted_iota(jnp.int32, (8, NZ), 0) >> 1).astype(f32)
    across[...] = jnp.where(plane < count, 1.0 / jnp.maximum(count, 1.0), 0.0)


def pick(blocks, o, got):
    low, high = blocks[0, o], blocks[1, o]
    a = got[:, pl.ds(pl.multiple_of(8 * lax.rem(low, 3), 8), 8), :].reshape(LANES, LANES)
    b = got[:, pl.ds(pl.multiple_of(8 * lax.rem(high, 3), 8), 8), :].reshape(LANES, LANES)
    a = jnp.where(low >= 3, turn(a, -32), a)
    b = jnp.where(high >= 3, b, turn(b, 32))
    return jnp.where(lane_bit((LANES, LANES), 32), b, a)


def pick_kernel(blocks, where, got, out1, out2, out3):
    for k, out in enumerate((out1, out2, out3)):
        out[...] = pick(blocks, (where[2] + k + 1) & 3, got)


def product_kernel(got, basis, slope, out, held):
    for wh in range(4):
        rows = swap([got[4 * wh + wl] for wl in range(4)], (64, 32))
        for y in range(4):
            held[y * 96 : y * 96 + 96, wh * LANES : wh * LANES + LANES] = rows[y]
    speed = mul(halves(held[...]), (basis[0], basis[1])).reshape(4, 2, COL, NZ)
    product = (speed[:, 1:2] * speed).reshape(384, NZ)
    inner = mul(halves(product), (slope[0], slope[1]))
    for wh in range(4):
        part = inner[:, wh * LANES : wh * LANES + LANES]
        rows = swap([part[y * 96 : y * 96 + 96] for y in range(4)], (64, 32))
        for wl in range(4):
            out[4 * wh + wl, 0:96, :] = rows[wl]
    out[:, 96:120, :] = jnp.zeros((16, 24, LANES), f32)


def bed_kernel(
    blocks, where, own, got1, got2, got3, share, across, basis, position, velocity, size,
    out, lifted, push,
    step, near, force, grid, built, lifted_held, push_held, sems,
):
    for k, got in enumerate((None, got1, got2, got3)):
        nx = (where[2] - k) & 3
        block = pick(blocks, nx, own) if k == 0 else got[...]
        rows = swap([block[w * 8 : w * 8 + 8] for w in range(16)], (16, 8, 64, 32))
        step[nx] = jnp.concatenate(rows, axis=0)
    lines = jnp.concatenate(swap([step[nx] for nx in range(4)], (16, 8)), axis=1)
    speed = mul(halves(lines), (basis[0], basis[1]))
    means = []
    for q in range(4):
        parts = [
            speed[(p * 4 + q) * 8 : (p * 4 + q) * 8 + 8] * across[pl.ds(p * 2 + q % 2, 1), :]
            for p in range(BED)
        ]
        means.append((parts[0] + parts[1]) + (parts[2] + parts[3]))
    means = jnp.concatenate(means * 4, axis=0)
    for t in range(6):
        near[t * 16 : t * 16 + 16] = means[:, t * LANES : t * LANES + LANES].T.reshape(
            16, BIN, LANES
        )
    force[...] = jnp.zeros(force.shape, f32)

    offset, owned = where[0], where[1]
    lane = lax.broadcasted_iota(jnp.int32, (BIN, LANES), 1)
    slots = position.shape[1]
    bases = (0, 16, 32, slots - 16)
    spots = []
    for i, base in enumerate(bases):
        for s in range(16):
            index = offset + (base + s)
            row = (index >= ZB).astype(jnp.int32)
            spots.append((index - ZB * row, row))
            cells = near[index - ZB * row]
            for c in range(2):
                cell = pltpu.roll(cells, (s * 8 - c * 16 - row * 8) & (LANES - 1), 1)
                at = s * 16 + c * 8
                grid[i, at : at + 8, :] = jnp.where(lane >> 3 == s, cell, 0.0)

    centre = lax.broadcasted_iota(jnp.int32, (16, BIN, LANES), 1).astype(f32) + 0.5
    spans = [slice(base, base + 16) for base in bases]
    weight_x = [jnp.exp(-0.5 * (position[0, span][:, None, :] - centre) ** 2) for span in spans]
    weight_z = [jnp.exp(-0.5 * (position[1, span][:, None, :] - centre) ** 2) for span in spans]
    flat_x = [halves(weight.reshape(LANES, LANES)) for weight in weight_x]
    part = [mul_small(halves(grid[i]), flat_x[i]).reshape(16, 2, BIN, LANES) for i in range(4)]
    pulls = []
    for i, span in enumerate(spans):
        totals = jnp.sum(weight_x[i], axis=1) * jnp.sum(weight_z[i], axis=1)
        felt = [jnp.sum(part[i][:, c] * weight_z[i], axis=1) / totals for c in range(2)]
        relative = [felt[c] - velocity[c, span] for c in range(2)]
        magnitude = jnp.sqrt(relative[0] * relative[0] + relative[1] * relative[1] + 0.1)
        diameter = size[span]
        squared = diameter * diameter
        lift = 0.5 * squared * (felt[0] * felt[0] + felt[1] * felt[1])
        active = lax.broadcasted_iota(jnp.int32, (16, LANES), 0) + bases[i] < owned
        chance = jnp.where(
            active, jax.nn.sigmoid((lift - 0.5 * squared * diameter) / 0.25), 0.0
        )
        lifted_held[span, 0, :] = chance
        pull = []
        for c in range(2):
            pushed = jnp.where(
                active, 0.5 * squared * relative[c] * magnitude * (1.0 + chance), 0.0
            )
            push_held[span, c, :] = pushed
            pull.append((-reaction * pushed / totals)[:, None, :] * weight_z[i])
        pulls.append(halves(jnp.stack(pull, axis=1).reshape(2 * LANES, LANES)))
    sent = start(
        [
            pltpu.make_async_copy(lifted_held, lifted, sems.at[0]),
            pltpu.make_async_copy(push_held, push, sems.at[1]),
        ]
    )

    shape = (2 * LANES, LANES)
    mine = lax.broadcasted_iota(jnp.int32, shape, 1) >> 3 == (
        lax.broadcasted_iota(jnp.int32, shape, 0) >> 4
    )
    for i in range(4):
        cells = mul_small(pulls[i], flat_x[i], True)
        cells = jnp.where(mine, cells, 0.0)
        for bit in (8, 16, 32, 64):
            cells = cells + turn(cells, bit)
        for s in range(16):
            spot, row = spots[i * 16 + s]
            value = jnp.where(
                lane_bit((BIN, LANES), 64),
                cells[s * 16 + 8 : s * 16 + 16],
                cells[s * 16 : s * 16 + 8],
            )
            value = jnp.where((lane >> 5) & 1 == row, value, 0.0)
            force[spot] = value * share[pl.ds(spot, 1), :]

    inner = mul_narrow((basis[0], basis[1]), halves(force[...].reshape(NZ, LANES)))
    for nx in range(4):
        rows = [inner[w * 32 + nx * 8 : w * 32 + nx * 8 + 8] for w in range(16)]
        built[nx] = jnp.concatenate(swap(rows, (64, 32, 16, 8)), axis=0).T
        sent += start([pltpu.make_async_copy(built.at[nx], out.at[nx], sems.at[2 + nx])])
    finish(sent)


def place_kernel(blocks, got, main, out):
    upper = lane_bit((LANES, LANES), 32)
    for o in range(4):
        low, high = blocks[0, o], blocks[1, o]
        value = got[o]
        a = jnp.where(upper, 0.0, value)
        b = jnp.where(upper, value, 0.0)
        a = jnp.where(low >= 3, turn(a, 32), a).reshape(16, 8, LANES)
        b = jnp.where(high >= 3, b, turn(b, -32)).reshape(16, 8, LANES)
        rows = pl.ds(pl.multiple_of(96 + 8 * lax.rem(low, 3), 8), 8)
        out[:, rows, :] = out[:, rows, :] + a
        rows = pl.ds(pl.multiple_of(96 + 8 * lax.rem(high, 3), 8), 8)
        out[:, rows, :] = out[:, rows, :] + b


def gather_kernel(got, table, out):
    block = [got[:, c * COL : c * COL + COL, :].reshape(NX, LANES) for c in range(2)]
    block = halves(jnp.concatenate(block, axis=1))
    bed = got[:, 96:120, :]
    bed = halves(jnp.concatenate([bed, turn(bed, -32)], axis=1).reshape(NX, LANES))
    first = jnp.dot(
        table[0], jnp.concatenate([block[0], *bed], axis=1), preferred_element_type=f32
    )
    second = jnp.dot(
        table[1], jnp.concatenate([block[0], bed[0]], axis=1), preferred_element_type=f32
    )
    third = jnp.dot(table[0], block[1], preferred_element_type=f32)
    main = first[:, : 2 * LANES] + (second[:, : 2 * LANES] + third)
    beds = first[:, 2 * LANES : 3 * LANES] + (first[:, 3 * LANES :] + second[:, 2 * LANES :])
    upper = lane_bit((8, LANES), 32)
    for n in range(32):
        part = main[n * 16 : n * 16 + 16]
        for c in range(2):
            out[n, c * 16 : c * 16 + 16, :] = part[:, c * LANES : c * LANES + LANES]
        bed = beds[n * 16 : n * 16 + 16]
        out[n, 32:40, :] = jnp.where(upper, turn(bed[8:16], 32), bed[0:8])


def close_kernel(
    where, got, modes, to_eigen, from_eigen, eigenvalues, out, flat, held, built, sems
):
    parts = [(c, g) for c in range(2) for g in range(4)]
    bed = [jnp.sum(got[nx * 8 : nx * 8 + 8, 32:40, :], axis=0) for nx in range(4)]
    bed = [cross(value) for value in swap(bed, (16, 8))]
    for c, g in parts:
        rows = swap([got[:, c * 16 + k, :] for k in modes_of(g)], (64, 32))
        for y in range(4):
            flat[c * 4 + g, pl.ds(y, 32, stride=4), :] = rows[y]
    for p in range(BED):
        flat[:, p, :] = flat[:, p, :] + bed[p]
    for c, g in parts:
        back = flat[c * 4 + g].T
        for i, k in enumerate(modes_of(g)):
            at = (c * 16 + k) * 32
            held[at : at + 32, :] = back[i * 32 : i * 32 + 32] + modes[c, k]
    forth, back = halves(from_eigen[...]), halves(to_eigen[...])
    sent = []
    for i in range(4):
        rows = slice(i * 256, i * 256 + 256)
        part = mul_small(halves(held[rows]), forth, True)
        row = lax.broadcasted_iota(jnp.int32, (256, LANES), 0) + i * 256
        wave_x = ((where[3] * 16 + ((row >> 5) & 15) + 1) >> 1).astype(f32)
        wave_z = ((where[4] * 32 + (row & 31) + 1) >> 1).astype(f32)
        divisor = 1.0 + viscous * (wave_x * wave_x + wave_z * wave_z + eigenvalues[...])
        result = mul_small(halves(part / divisor), back, True)
        built[i] = result.reshape(8, 32, LANES)
        block = out.at[i // 2, pl.ds(8 * (i % 2), 8)]
        sent += start([pltpu.make_async_copy(built.at[i], block, sems.at[i])])
    finish(sent)


def call(body, shape, *operands, scalars=0, scratch=(), sems=0, out_far=False, alias={}):
    spaces = [pltpu.SMEM] * scalars + [pltpu.VMEM] * (len(operands) - scalars)
    out_space = pl.BlockSpec(memory_space=pltpu.HBM if out_far else pltpu.VMEM)
    several = isinstance(shape, list)
    outs = [jax.ShapeDtypeStruct(one, f32) for one in (shape if several else [shape])]
    held = [pltpu.VMEM(one, f32) for one in scratch]
    bytes_moved = sum(4 * math.prod(one.shape) for one in list(operands) + outs)
    result = pl.pallas_call(
        body,
        out_shape=outs,
        in_specs=[pl.BlockSpec(memory_space=space) for space in spaces],
        out_specs=[out_space] * len(outs),
        scratch_shapes=held + ([pltpu.SemaphoreType.DMA((sems,))] if sems else []),
        compiler_params=pltpu.CompilerParams(vmem_limit_bytes=16 << 20),
        cost_estimate=pl.CostEstimate(
            flops=700_000_000, bytes_accessed=bytes_moved, transcendentals=0
        ),
        input_output_aliases=alias,
        name=body.__name__,
    )(*operands)
    return result if several else result[0]


def map_call(place, bins_owned, bed_planes):
    smem, vmem = pl.BlockSpec(memory_space=pltpu.SMEM), pl.BlockSpec(memory_space=pltpu.VMEM)
    return pl.pallas_call(
        map_kernel,
        out_shape=[
            jax.ShapeDtypeStruct((2, 4), jnp.int32),
            jax.ShapeDtypeStruct((5,), jnp.int32),
            jax.ShapeDtypeStruct((ZB, LANES), f32),
            jax.ShapeDtypeStruct((8, NZ), f32),
        ],
        in_specs=[smem, smem, vmem],
        out_specs=[smem, smem, vmem, vmem],
        scratch_shapes=[pltpu.SMEM((32,), jnp.int32), pltpu.VMEM((LANES, LANES), f32)],
        compiler_params=pltpu.CompilerParams(vmem_limit_bytes=16 << 20),
        name="map_kernel",
    )(place, bins_owned, bed_planes)


def exchange(value, axis, groups=None):
    return lax.all_to_all(value, axis, 0, 0, axis_index_groups=groups, tiled=True)


def shards(
    modes,
    to_eigen,
    from_eigen,
    eigenvalues,
    bins_owned,
    bed_planes,
    particle_position,
    particle_velocity,
    particle_size,
):
    points, basis, slope = tables()
    narrow_at = lax.axis_index("narrow")
    wide_at = lax.axis_index("wide")
    groups = [[nz + 8 * nx for nx in range(4)] for nz in range(8)]

    sent = call(open_kernel, (32, 40, LANES), modes, scratch=[(8, LANES, LANES)])
    got = exchange(sent, "narrow")
    bed = exchange(call(spread_bed_kernel, (16, 24, LANES), got, points), "wide")
    sent = call(spread_kernel, (16, 96, LANES), got, points)
    sent, bed, bins_owned, bed_planes = lax.optimization_barrier(
        (sent, bed, bins_owned, bed_planes)
    )
    grid = exchange(sent, "wide")

    blocks, where, share, across = map_call(
        jnp.stack([narrow_at, wide_at]), bins_owned, bed_planes.reshape(6, ZB)
    )

    block = (LANES, LANES)
    sent = call(pick_kernel, [block] * 3, blocks, where, bed, scalars=2)
    got = []
    for k in range(1, 4):
        hops = [(x * 8 + z, (x + k) % 4 * 8 + z) for x in range(4) for z in range(8)]
        got.append(lax.ppermute(sent[k - 1], "narrow", hops))

    count = particle_size.shape[2]
    slots, pairs = (count, 1, LANES), (count, 2, LANES)
    sent, lifted, particle_push = call(
        bed_kernel,
        [(4,) + block, slots, pairs],
        blocks,
        where,
        bed,
        *got,
        share,
        across,
        basis,
        particle_position[0, 0],
        particle_velocity[0, 0],
        particle_size[0, 0],
        scalars=2,
        scratch=[
            (4,) + block,
            (ZB, BIN, LANES),
            (ZB, BIN, LANES),
            (4, 2 * LANES, LANES),
            (4,) + block,
            slots,
            pairs,
        ],
        sems=6,
        out_far=True,
    )
    got = exchange(sent, "narrow", groups)
    inner = call(product_kernel, (16, 120, LANES), grid, basis, slope, scratch=[(384, KZ)])
    sent = call(place_kernel, (16, 120, LANES), blocks, got, inner, scalars=1, alias={2: 0})

    got = exchange(sent, "wide")
    sent = call(gather_kernel, (32, 40, LANES), got, basis)
    got = exchange(sent, "narrow")
    new_modes = call(
        close_kernel,
        modes.shape,
        where,
        got,
        modes,
        to_eigen,
        from_eigen,
        eigenvalues[None],
        scalars=1,
        scratch=[(8, LANES, LANES), (1024, LANES), (4, 8, 32, LANES)],
        sems=4,
        out_far=True,
    )
    lifted = lifted.transpose(1, 0, 2)[None]
    return (new_modes, lifted, particle_push.transpose(1, 0, 2)[None, None])


def solution(mesh):
    in_specs = (
        P(None, "narrow", "wide", None),
        P(),
        P(),
        P(),
        P("wide", None),
        P("wide"),
        P("wide", "narrow", None, None, None),
        P("wide", "narrow", None, None, None),
        P("wide", "narrow", None, None),
    )
    out_specs = (
        P(None, "narrow", "wide", None),
        P("wide", "narrow", None, None),
        P("wide", "narrow", None, None, None),
    )
    return jax.shard_map(shards, mesh=mesh, in_specs=in_specs, out_specs=out_specs, check_vma=False)
```

```python
import math

import jax
import jax.numpy as jnp
import ml_dtypes
import numpy as np
from jax import lax
from jax.experimental import pallas as pl
from jax.experimental.pallas import tpu as pltpu
from jax.sharding import PartitionSpec as P

NX = 768
NZ = 768
KX = 512
KZ = 512
BED = 4
BIN = 8
COL = 48
ZB = NZ // BIN
LANES = 128

time_step = 0.003
viscous = 0.0001
reaction = 0.25
f32 = jnp.float32
bf16 = jnp.bfloat16


def basis_np(mode_count, points):
    m = np.arange(mode_count)[:, None]
    j = np.arange(points)[None, :]
    k = (m + 1) // 2
    angle = (k * j % points) * (2.0 * math.pi / points)
    table = math.sqrt(2.0 / points) * np.where(m % 2 == 1, np.cos(angle), np.sin(angle))
    return np.where(m == 0, 1.0 / math.sqrt(points), table)


def slope_np(points, mode_count):
    j = np.arange(points)[:, None]
    m = np.arange(mode_count)[None, :]
    k = (m + 1) // 2
    angle = (k * j % points) * (2.0 * math.pi / points)
    return k * math.sqrt(2.0 / points) * np.where(m % 2 == 1, np.sin(angle), -np.cos(angle))


def split_np(table):
    table = np.ascontiguousarray(table).astype(np.float32)
    high = table.astype(ml_dtypes.bfloat16)
    low = (table - high.astype(np.float32)).astype(ml_dtypes.bfloat16)
    return np.stack([high, low])


def tables():
    basis = basis_np(KX, NX)
    return split_np(basis.T), split_np(basis), split_np(-time_step * slope_np(NZ, KZ))


def halves(value):
    high = value.astype(bf16)
    return high, (value - high.astype(f32)).astype(bf16)


def mul(a, b):
    def one(p, q):
        return jnp.dot(p, q, preferred_element_type=f32)

    return one(a[0], b[0]) + (one(a[0], b[1]) + one(a[1], b[0]))


def mul_narrow(a, b):
    wide = jnp.dot(a[0], jnp.concatenate(b, axis=1), preferred_element_type=f32)
    rest = jnp.dot(a[1], b[0], preferred_element_type=f32)
    return wide[:, :LANES] + (wide[:, LANES:] + rest)


def mul_small(a, b, across=False):
    zero = jnp.zeros((LANES, LANES), bf16)
    order = [[b[0], b[0]], [b[1], zero]] if across else [[b[0], b[1]], [b[0], zero]]
    both = jnp.concatenate([jnp.concatenate(row, axis=1) for row in order], axis=0)
    dims = (((1,), (1 if across else 0,)), ((), ()))
    wide = lax.dot_general(jnp.concatenate(a, axis=1), both, dims, preferred_element_type=f32)
    return wide[:, :LANES] + wide[:, LANES:]


def start(copies):
    for copy in copies:
        copy.start()
    return copies


def finish(copies):
    for copy in copies:
        copy.wait()


def lane_bit(shape, bit):
    return (lax.broadcasted_iota(jnp.int32, shape, len(shape) - 1) & bit) != 0


def turn(value, shift):
    return pltpu.roll(value, shift % LANES, value.ndim - 1)


def swap(rows, bits):
    rows = list(rows)
    step = len(rows) // 2
    for bit in bits:
        upper = lane_bit(rows[0].shape, bit)
        for i in range(len(rows)):
            if i & step:
                continue
            a, b = rows[i], rows[i + step]
            rows[i] = jnp.where(upper, turn(b, bit), a)
            rows[i + step] = jnp.where(upper, b, turn(a, -bit))
        step //= 2
    return rows


def cross(value):
    row = lax.broadcasted_iota(jnp.int32, value.shape, 0)
    for sub, bit in ((4, 64), (2, 32)):
        below, right = (row & sub) != 0, lane_bit(value.shape, bit)
        down = turn(pltpu.roll(value, sub, 0), -bit)
        up = turn(pltpu.roll(value, 8 - sub, 0), bit)
        value = jnp.where(below == right, value, jnp.where(below, down, up))
    return value


def modes_of(g):
    return [(g // 2) * 8 + g % 2 + 2 * k for k in range(4)]


def open_kernel(modes, out, flat):
    for c in range(2):
        for g in range(4):
            at = c * 4 + g
            flat[at] = jnp.concatenate([modes[c, k] for k in modes_of(g)], axis=0).T
            rows = [flat[at, pl.ds(y, 32, stride=4), :] for y in range(4)]
            for k, row in zip(modes_of(g), swap(rows, (64, 32))):
                out[:, c * 16 + k, :] = row
    bed = swap([cross(flat[:, p, :]) for p in range(BED)], (16, 8))
    for nx in range(4):
        out[nx * 8 : nx * 8 + 8, 32:40, :] = jnp.broadcast_to(bed[nx][None], (8, 8, LANES))


def spread_kernel(got, table, out):
    block = jnp.concatenate(
        [got[:, c * 16 : c * 16 + 16, :].reshape(KX, LANES) for c in range(2)], axis=1
    )
    grid = mul((table[0], table[1]), halves(block))
    for w in range(16):
        for c in range(2):
            out[w, c * COL : c * COL + COL, :] = grid[
                w * COL : w * COL + COL, c * LANES : c * LANES + LANES
            ]
    block = got[:, 32:40, :]
    block = jnp.concatenate([block, turn(block, -32)], axis=1).reshape(KX, LANES)
    bed = mul_narrow((table[0], table[1]), halves(block))
    upper = lane_bit((24, LANES), 32)
    for w in range(16):
        first = bed[w * COL : w * COL + 24]
        second = bed[w * COL + 24 : w * COL + COL]
        out[w, 96:120, :] = jnp.where(upper, turn(second, 32), first)


def map_kernel(place, bins_owned, bed_planes, blocks, where, share, across, firsts, planes):
    total = jnp.int32(0)
    for n in range(32):
        firsts[n] = total
        total = total + bins_owned[0, n]
    narrow_at = place[0]
    first = firsts[narrow_at]
    low = lax.div(first, ZB)
    high = jnp.minimum(low + 1, 5)
    where[0] = first - ZB * low
    where[1] = bins_owned[0, narrow_at]
    where[2] = lax.div(narrow_at, 8)
    where[3] = narrow_at
    where[4] = place[1]
    for nx in range(4):
        row = lax.div(firsts[nx * 8 + (narrow_at & 7)], ZB)
        blocks[0, nx] = row
        blocks[1, nx] = jnp.minimum(row + 1, 5)

    planes[...] = jnp.zeros((LANES, LANES), f32)
    planes[0:6, 0:ZB] = bed_planes[...].astype(f32)
    table = planes[...].astype(bf16)

    def row_of(odd):
        return jnp.where(odd, high, low)

    shape = (LANES, LANES)
    index, lane = (lax.broadcasted_iota(jnp.int32, shape, i) for i in (0, 1))
    chosen = (index == row_of(lane_bit(shape, 32))).astype(f32).astype(bf16)
    count = jnp.dot(planes[...].T.astype(bf16), chosen, preferred_element_type=f32)[:ZB]
    plane = ((lane >> 3) & 3)[:ZB].astype(f32)
    share[...] = jnp.where(plane < count, 1.0 / jnp.maximum(count, 1.0), 0.0)

    chosen = (lane == row_of((index & 1) != 0)).astype(f32).astype(bf16)
    count = jnp.dot(chosen, table, preferred_element_type=f32).astype(bf16)
    wide = (LANES, NZ)
    spread = lax.broadcasted_iota(jnp.int32, wide, 1) >> 3 == lax.broadcasted_iota(jnp.int32, wide, 0)
    count = jnp.dot(count, spread.astype(f32).astype(bf16), preferred_element_type=f32)[:8]
    plane = (lax.broadcasted_iota(jnp.int32, (8, NZ), 0) >> 1).astype(f32)
    across[...] = jnp.where(plane < count, 1.0 / jnp.maximum(count, 1.0), 0.0)


def pick(blocks, o, got):
    low, high = blocks[0, o], blocks[1, o]
    a = got[:, pl.ds(pl.multiple_of(96 + 8 * lax.rem(low, 3), 8), 8), :].reshape(LANES, LANES)
    b = got[:, pl.ds(pl.multiple_of(96 + 8 * lax.rem(high, 3), 8), 8), :].reshape(LANES, LANES)
    a = jnp.where(low >= 3, turn(a, -32), a)
    b = jnp.where(high >= 3, b, turn(b, 32))
    return jnp.where(lane_bit((LANES, LANES), 32), b, a)


def pick_kernel(blocks, got, out):
    for o in range(4):
        out[o] = pick(blocks, o, got)


def product_kernel(got, basis, slope, out, held):
    for wh in range(4):
        rows = swap([got[4 * wh + wl, 0:96, :] for wl in range(4)], (64, 32))
        for y in range(4):
            held[y * 96 : y * 96 + 96, wh * LANES : wh * LANES + LANES] = rows[y]
    speed = mul(halves(held[...]), (basis[0], basis[1])).reshape(4, 2, COL, NZ)
    product = (speed[:, 1:2] * speed).reshape(384, NZ)
    inner = mul(halves(product), (slope[0], slope[1]))
    for wh in range(4):
        part = inner[:, wh * LANES : wh * LANES + LANES]
        rows = swap([part[y * 96 : y * 96 + 96] for y in range(4)], (64, 32))
        for wl in range(4):
            out[4 * wh + wl] = rows[wl]


def bed_kernel(
    where, got, share, across, basis, position, velocity, size,
    out0, out1, out2, out3, lifted, push,
    step, near, force, grid, built, lifted_held, push_held, sems,
):
    for nx in range(4):
        block = got[nx]
        rows = swap([block[w * 8 : w * 8 + 8] for w in range(16)], (16, 8, 64, 32))
        step[nx] = jnp.concatenate(rows, axis=0)
    lines = jnp.concatenate(swap([step[nx] for nx in range(4)], (16, 8)), axis=1)
    speed = mul(halves(lines), (basis[0], basis[1]))
    means = []
    for q in range(4):
        parts = [
            speed[(p * 4 + q) * 8 : (p * 4 + q) * 8 + 8] * across[pl.ds(p * 2 + q % 2, 1), :]
            for p in range(BED)
        ]
        means.append((parts[0] + parts[1]) + (parts[2] + parts[3]))
    means = jnp.concatenate(means * 4, axis=0)
    for t in range(6):
        near[t * 16 : t * 16 + 16] = means[:, t * LANES : t * LANES + LANES].T.reshape(
            16, BIN, LANES
        )
    force[...] = jnp.zeros(force.shape, f32)

    offset, owned = where[0], where[1]
    lane = lax.broadcasted_iota(jnp.int32, (BIN, LANES), 1)
    slots = position.shape[1]
    bases = (0, 16, 32, slots - 16)
    spots = []
    for i, base in enumerate(bases):
        for s in range(16):
            index = offset + (base + s)
            row = (index >= ZB).astype(jnp.int32)
            spots.append((index - ZB * row, row))
            cells = near[index - ZB * row]
            for c in range(2):
                cell = pltpu.roll(cells, (s * 8 - c * 16 - row * 8) & (LANES - 1), 1)
                at = s * 16 + c * 8
                grid[i, at : at + 8, :] = jnp.where(lane >> 3 == s, cell, 0.0)

    centre = lax.broadcasted_iota(jnp.int32, (16, BIN, LANES), 1).astype(f32) + 0.5
    spans = [slice(base, base + 16) for base in bases]
    weight_x = [jnp.exp(-0.5 * (position[0, span][:, None, :] - centre) ** 2) for span in spans]
    weight_z = [jnp.exp(-0.5 * (position[1, span][:, None, :] - centre) ** 2) for span in spans]
    flat_x = [halves(weight.reshape(LANES, LANES)) for weight in weight_x]
    part = [mul_small(halves(grid[i]), flat_x[i]).reshape(16, 2, BIN, LANES) for i in range(4)]
    pulls = []
    for i, span in enumerate(spans):
        totals = jnp.sum(weight_x[i], axis=1) * jnp.sum(weight_z[i], axis=1)
        felt = [jnp.sum(part[i][:, c] * weight_z[i], axis=1) / totals for c in range(2)]
        relative = [felt[c] - velocity[c, span] for c in range(2)]
        magnitude = jnp.sqrt(relative[0] * relative[0] + relative[1] * relative[1] + 0.1)
        diameter = size[span]
        squared = diameter * diameter
        lift = 0.5 * squared * (felt[0] * felt[0] + felt[1] * felt[1])
        active = lax.broadcasted_iota(jnp.int32, (16, LANES), 0) + bases[i] < owned
        chance = jnp.where(
            active, jax.nn.sigmoid((lift - 0.5 * squared * diameter) / 0.25), 0.0
        )
        lifted_held[span, 0, :] = chance
        pull = []
        for c in range(2):
            pushed = jnp.where(
                active, 0.5 * squared * relative[c] * magnitude * (1.0 + chance), 0.0
            )
            push_held[span, c, :] = pushed
            pull.append((-reaction * pushed / totals)[:, None, :] * weight_z[i])
        pulls.append(halves(jnp.stack(pull, axis=1).reshape(2 * LANES, LANES)))
    sent = start(
        [
            pltpu.make_async_copy(lifted_held, lifted, sems.at[0]),
            pltpu.make_async_copy(push_held, push, sems.at[1]),
        ]
    )

    shape = (2 * LANES, LANES)
    mine = lax.broadcasted_iota(jnp.int32, shape, 1) >> 3 == (
        lax.broadcasted_iota(jnp.int32, shape, 0) >> 4
    )
    for i in range(4):
        cells = mul_small(pulls[i], flat_x[i], True)
        cells = jnp.where(mine, cells, 0.0)
        for bit in (8, 16, 32, 64):
            cells = cells + turn(cells, bit)
        for s in range(16):
            spot, row = spots[i * 16 + s]
            value = jnp.where(
                lane_bit((BIN, LANES), 64),
                cells[s * 16 + 8 : s * 16 + 16],
                cells[s * 16 : s * 16 + 8],
            )
            value = jnp.where((lane >> 5) & 1 == row, value, 0.0)
            force[spot] = value * share[pl.ds(spot, 1), :]

    inner = mul_narrow((basis[0], basis[1]), halves(force[...].reshape(NZ, LANES)))
    for nx in range(4):
        rows = [inner[w * 32 + nx * 8 : w * 32 + nx * 8 + 8] for w in range(16)]
        built[(nx - where[2]) & 3] = jnp.concatenate(swap(rows, (64, 32, 16, 8)), axis=0).T
    for k, out in enumerate((out0, out1, out2, out3)):
        sent += start([pltpu.make_async_copy(built.at[k], out, sems.at[2 + k])])
    finish(sent)


def place_kernel(blocks, where, got0, got1, got2, got3, out):
    out[...] = jnp.zeros(out.shape, f32)
    upper = lane_bit((LANES, LANES), 32)
    for k, got in enumerate((got0, got1, got2, got3)):
        o = (where[2] - k) & 3
        low, high = blocks[0, o], blocks[1, o]
        value = got[...]
        a = jnp.where(upper, 0.0, value)
        b = jnp.where(upper, value, 0.0)
        a = jnp.where(low >= 3, turn(a, 32), a).reshape(16, 8, LANES)
        b = jnp.where(high >= 3, b, turn(b, -32)).reshape(16, 8, LANES)
        rows = pl.ds(pl.multiple_of(8 * lax.rem(low, 3), 8), 8)
        out[:, rows, :] = out[:, rows, :] + a
        rows = pl.ds(pl.multiple_of(8 * lax.rem(high, 3), 8), 8)
        out[:, rows, :] = out[:, rows, :] + b


def gather_kernel(got, table, out):
    block = jnp.concatenate(
        [got[:, c * COL : c * COL + COL, :].reshape(NX, LANES) for c in range(2)], axis=1
    )
    terms = mul((table[0], table[1]), halves(block))
    for n in range(32):
        for c in range(2):
            out[n, c * 16 : c * 16 + 16, :] = terms[
                n * 16 : n * 16 + 16, c * LANES : c * LANES + LANES
            ]


def join_kernel(main, got, table, out):
    out[:, 0:32, :] = main[...]
    bed = got[...]
    bed = jnp.concatenate([bed, turn(bed, -32)], axis=1).reshape(NX, LANES)
    bed = mul_narrow((table[0], table[1]), halves(bed))
    upper = lane_bit((8, LANES), 32)
    for n in range(32):
        part = bed[n * 16 : n * 16 + 16]
        out[n, 32:40, :] = jnp.where(upper, turn(part[8:16], 32), part[0:8])


def close_kernel(
    where, got, modes, to_eigen, from_eigen, eigenvalues, out, flat, held, built, sems
):
    parts = [(c, g) for c in range(2) for g in range(4)]
    bed = [jnp.sum(got[nx * 8 : nx * 8 + 8, 32:40, :], axis=0) for nx in range(4)]
    bed = [cross(value) for value in swap(bed, (16, 8))]
    for c, g in parts:
        rows = swap([got[:, c * 16 + k, :] for k in modes_of(g)], (64, 32))
        for y in range(4):
            flat[c * 4 + g, pl.ds(y, 32, stride=4), :] = rows[y]
    for p in range(BED):
        flat[:, p, :] = flat[:, p, :] + bed[p]
    for c, g in parts:
        back = flat[c * 4 + g].T
        for i, k in enumerate(modes_of(g)):
            at = (c * 16 + k) * 32
            held[at : at + 32, :] = back[i * 32 : i * 32 + 32] + modes[c, k]
    forth, back = halves(from_eigen[...]), halves(to_eigen[...])
    sent = []
    for i in range(4):
        rows = slice(i * 256, i * 256 + 256)
        part = mul_small(halves(held[rows]), forth, True)
        row = lax.broadcasted_iota(jnp.int32, (256, LANES), 0) + i * 256
        wave_x = ((where[3] * 16 + ((row >> 5) & 15) + 1) >> 1).astype(f32)
        wave_z = ((where[4] * 32 + (row & 31) + 1) >> 1).astype(f32)
        divisor = 1.0 + viscous * (wave_x * wave_x + wave_z * wave_z + eigenvalues[...])
        result = mul_small(halves(part / divisor), back, True)
        built[i] = result.reshape(8, 32, LANES)
        block = out.at[i // 2, pl.ds(8 * (i % 2), 8)]
        sent += start([pltpu.make_async_copy(built.at[i], block, sems.at[i])])
    finish(sent)


def call(body, shape, *operands, scalars=0, scratch=(), sems=0, out_far=False, alias={}):
    spaces = [pltpu.SMEM] * scalars + [pltpu.VMEM] * (len(operands) - scalars)
    out_space = pl.BlockSpec(memory_space=pltpu.HBM if out_far else pltpu.VMEM)
    several = isinstance(shape, list)
    outs = [jax.ShapeDtypeStruct(one, f32) for one in (shape if several else [shape])]
    held = [pltpu.VMEM(one, f32) for one in scratch]
    bytes_moved = sum(4 * math.prod(one.shape) for one in list(operands) + outs)
    result = pl.pallas_call(
        body,
        out_shape=outs,
        in_specs=[pl.BlockSpec(memory_space=space) for space in spaces],
        out_specs=[out_space] * len(outs),
        scratch_shapes=held + ([pltpu.SemaphoreType.DMA((sems,))] if sems else []),
        compiler_params=pltpu.CompilerParams(vmem_limit_bytes=16 << 20),
        cost_estimate=pl.CostEstimate(
            flops=700_000_000, bytes_accessed=bytes_moved, transcendentals=0
        ),
        input_output_aliases=alias,
        name=body.__name__,
    )(*operands)
    return result if several else result[0]


def map_call(place, bins_owned, bed_planes):
    smem, vmem = pl.BlockSpec(memory_space=pltpu.SMEM), pl.BlockSpec(memory_space=pltpu.VMEM)
    return pl.pallas_call(
        map_kernel,
        out_shape=[
            jax.ShapeDtypeStruct((2, 4), jnp.int32),
            jax.ShapeDtypeStruct((5,), jnp.int32),
            jax.ShapeDtypeStruct((ZB, LANES), f32),
            jax.ShapeDtypeStruct((8, NZ), f32),
        ],
        in_specs=[smem, smem, vmem],
        out_specs=[smem, smem, vmem, vmem],
        scratch_shapes=[pltpu.SMEM((32,), jnp.int32), pltpu.VMEM((LANES, LANES), f32)],
        compiler_params=pltpu.CompilerParams(vmem_limit_bytes=16 << 20),
        name="map_kernel",
    )(place, bins_owned, bed_planes)


def exchange(value, axis, groups=None):
    return lax.all_to_all(value, axis, 0, 0, axis_index_groups=groups, tiled=True)


def shards(
    modes,
    to_eigen,
    from_eigen,
    eigenvalues,
    bins_owned,
    bed_planes,
    particle_position,
    particle_velocity,
    particle_size,
):
    points, basis, slope = tables()
    narrow_at = lax.axis_index("narrow")
    wide_at = lax.axis_index("wide")
    groups = [[nz + 8 * nx for nx in range(4)] for nz in range(8)]

    sent = call(open_kernel, (32, 40, LANES), modes, scratch=[(8, LANES, LANES)])
    got = exchange(sent, "narrow")
    sent = call(spread_kernel, (16, 120, LANES), got, points)
    sent, bins_owned, bed_planes = lax.optimization_barrier((sent, bins_owned, bed_planes))
    grid = exchange(sent, "wide")

    blocks, where, share, across = map_call(
        jnp.stack([narrow_at, wide_at]), bins_owned, bed_planes.reshape(6, ZB)
    )

    block = (LANES, LANES)
    sent = call(pick_kernel, (4,) + block, blocks, grid, scalars=1)
    got = exchange(sent, "narrow", groups)
    inner = call(product_kernel, (16, 96, LANES), grid, basis, slope, scratch=[(384, KZ)])
    main = exchange(inner, "wide")

    count = particle_size.shape[2]
    slots, pairs = (count, 1, LANES), (count, 2, LANES)
    *sent, lifted, particle_push = call(
        bed_kernel,
        [block] * 4 + [slots, pairs],
        where,
        got,
        share,
        across,
        basis,
        particle_position[0, 0],
        particle_velocity[0, 0],
        particle_size[0, 0],
        scalars=1,
        scratch=[
            (4,) + block,
            (ZB, BIN, LANES),
            (ZB, BIN, LANES),
            (4, 2 * LANES, LANES),
            (4,) + block,
            slots,
            pairs,
        ],
        sems=6,
        out_far=True,
    )
    got = [sent[0]]
    for k in range(1, 4):
        hops = [(x * 8 + z, (x + k) % 4 * 8 + z) for x in range(4) for z in range(8)]
        got.append(lax.ppermute(sent[k], "narrow", hops))
    sent = call(place_kernel, (16, 24, LANES), blocks, where, *got, scalars=2)
    bed = exchange(sent, "wide")

    terms = call(gather_kernel, (32, 32, LANES), main, basis)
    sent = call(join_kernel, (32, 40, LANES), terms, bed, basis)
    got = exchange(sent, "narrow")
    new_modes = call(
        close_kernel,
        modes.shape,
        where,
        got,
        modes,
        to_eigen,
        from_eigen,
        eigenvalues[None],
        scalars=1,
        scratch=[(8, LANES, LANES), (1024, LANES), (4, 8, 32, LANES)],
        sems=4,
        out_far=True,
    )
    lifted = lifted.transpose(1, 0, 2)[None]
    return (new_modes, lifted, particle_push.transpose(1, 0, 2)[None, None])


def solution(mesh):
    in_specs = (
        P(None, "narrow", "wide", None),
        P(),
        P(),
        P(),
        P("wide", None),
        P("wide"),
        P("wide", "narrow", None, None, None),
        P("wide", "narrow", None, None, None),
        P("wide", "narrow", None, None),
    )
    out_specs = (
        P(None, "narrow", "wide", None),
        P("wide", "narrow", None, None),
        P("wide", "narrow", None, None, None),
    )
    return jax.shard_map(shards, mesh=mesh, in_specs=in_specs, out_specs=out_specs, check_vma=False)
```

```python
import math

import jax
import jax.numpy as jnp
import ml_dtypes
import numpy as np
from jax import lax
from jax.experimental import pallas as pl
from jax.experimental.pallas import tpu as pltpu
from jax.sharding import PartitionSpec as P

NX = 768
NZ = 768
KX = 512
KZ = 512
BED = 4
BIN = 8
COL = 48
ZB = NZ // BIN
LANES = 128

time_step = 0.003
viscous = 0.0001
reaction = 0.25
f32 = jnp.float32
COST = {name: 700_000_000 for name in ("open_kernel", "spread_bed_kernel", "spread_kernel")}
bf16 = jnp.bfloat16


def basis_np(mode_count, points):
    m = np.arange(mode_count)[:, None]
    j = np.arange(points)[None, :]
    k = (m + 1) // 2
    angle = (k * j % points) * (2.0 * math.pi / points)
    table = math.sqrt(2.0 / points) * np.where(m % 2 == 1, np.cos(angle), np.sin(angle))
    return np.where(m == 0, 1.0 / math.sqrt(points), table)


def slope_np(points, mode_count):
    j = np.arange(points)[:, None]
    m = np.arange(mode_count)[None, :]
    k = (m + 1) // 2
    angle = (k * j % points) * (2.0 * math.pi / points)
    return k * math.sqrt(2.0 / points) * np.where(m % 2 == 1, np.sin(angle), -np.cos(angle))


def split_np(table):
    table = np.ascontiguousarray(table).astype(np.float32)
    high = table.astype(ml_dtypes.bfloat16)
    low = (table - high.astype(np.float32)).astype(ml_dtypes.bfloat16)
    return np.stack([high, low])


def tables():
    basis = basis_np(KX, NX)
    return split_np(basis.T), split_np(basis), split_np(-time_step * slope_np(NZ, KZ))


def halves(value):
    high = value.astype(bf16)
    return high, (value - high.astype(f32)).astype(bf16)


def mul(a, b):
    def one(p, q):
        return jnp.dot(p, q, preferred_element_type=f32)

    return one(a[0], b[0]) + (one(a[0], b[1]) + one(a[1], b[0]))


def mul_narrow(a, b):
    wide = jnp.dot(a[0], jnp.concatenate(b, axis=1), preferred_element_type=f32)
    rest = jnp.dot(a[1], b[0], preferred_element_type=f32)
    return wide[:, :LANES] + (wide[:, LANES:] + rest)


def mul_small(a, b, across=False):
    zero = jnp.zeros((LANES, LANES), bf16)
    order = [[b[0], b[0]], [b[1], zero]] if across else [[b[0], b[1]], [b[0], zero]]
    both = jnp.concatenate([jnp.concatenate(row, axis=1) for row in order], axis=0)
    dims = (((1,), (1 if across else 0,)), ((), ()))
    wide = lax.dot_general(jnp.concatenate(a, axis=1), both, dims, preferred_element_type=f32)
    return wide[:, :LANES] + wide[:, LANES:]


def start(copies):
    for copy in copies:
        copy.start()
    return copies


def finish(copies):
    for copy in copies:
        copy.wait()


def lane_bit(shape, bit):
    return (lax.broadcasted_iota(jnp.int32, shape, len(shape) - 1) & bit) != 0


def turn(value, shift):
    return pltpu.roll(value, shift % LANES, value.ndim - 1)


def swap(rows, bits):
    rows = list(rows)
    step = len(rows) // 2
    for bit in bits:
        upper = lane_bit(rows[0].shape, bit)
        for i in range(len(rows)):
            if i & step:
                continue
            a, b = rows[i], rows[i + step]
            rows[i] = jnp.where(upper, turn(b, bit), a)
            rows[i + step] = jnp.where(upper, b, turn(a, -bit))
        step //= 2
    return rows


def cross(value):
    row = lax.broadcasted_iota(jnp.int32, value.shape, 0)
    for sub, bit in ((4, 64), (2, 32)):
        below, right = (row & sub) != 0, lane_bit(value.shape, bit)
        down = turn(pltpu.roll(value, sub, 0), -bit)
        up = turn(pltpu.roll(value, 8 - sub, 0), bit)
        value = jnp.where(below == right, value, jnp.where(below, down, up))
    return value


def modes_of(g):
    return [(g // 2) * 8 + g % 2 + 2 * k for k in range(4)]


def open_kernel(modes, out, flat):
    for c in range(2):
        for g in range(4):
            at = c * 4 + g
            flat[at] = jnp.concatenate([modes[c, k] for k in modes_of(g)], axis=0).T
            rows = [flat[at, pl.ds(y, 32, stride=4), :] for y in range(4)]
            for k, row in zip(modes_of(g), swap(rows, (64, 32))):
                out[:, c * 16 + k, :] = row
    bed = swap([cross(flat[:, p, :]) for p in range(BED)], (16, 8))
    for nx in range(4):
        out[nx * 8 : nx * 8 + 8, 32:40, :] = jnp.broadcast_to(bed[nx][None], (8, 8, LANES))


def spread_bed_kernel(got, table, out):
    block = got[:, 32:40, :]
    block = jnp.concatenate([block, turn(block, -32)], axis=1).reshape(KX, LANES)
    bed = mul_narrow((table[0], table[1]), halves(block))
    upper = lane_bit((24, LANES), 32)
    for w in range(16):
        first = bed[w * COL : w * COL + 24]
        second = bed[w * COL + 24 : w * COL + COL]
        out[w] = jnp.where(upper, turn(second, 32), first)


def spread_kernel(got, table, out):
    block = jnp.concatenate(
        [got[:, c * 16 : c * 16 + 16, :].reshape(KX, LANES) for c in range(2)], axis=1
    )
    grid = mul((table[0], table[1]), halves(block))
    for w in range(16):
        for c in range(2):
            out[w, c * COL : c * COL + COL, :] = grid[
                w * COL : w * COL + COL, c * LANES : c * LANES + LANES
            ]


def map_kernel(place, bins_owned, bed_planes, blocks, where, share, across, firsts, planes):
    total = jnp.int32(0)
    for n in range(32):
        firsts[n] = total
        total = total + bins_owned[0, n]
    narrow_at = place[0]
    first = firsts[narrow_at]
    low = lax.div(first, ZB)
    high = jnp.minimum(low + 1, 5)
    where[0] = first - ZB * low
    where[1] = bins_owned[0, narrow_at]
    where[2] = lax.div(narrow_at, 8)
    where[3] = narrow_at
    where[4] = place[1]
    for nx in range(4):
        row = lax.div(firsts[nx * 8 + (narrow_at & 7)], ZB)
        blocks[0, nx] = row
        blocks[1, nx] = jnp.minimum(row + 1, 5)

    planes[...] = jnp.zeros((LANES, LANES), f32)
    planes[0:6, 0:ZB] = bed_planes[...].astype(f32)
    table = planes[...].astype(bf16)

    def row_of(odd):
        return jnp.where(odd, high, low)

    shape = (LANES, LANES)
    index, lane = (lax.broadcasted_iota(jnp.int32, shape, i) for i in (0, 1))
    chosen = (index == row_of(lane_bit(shape, 32))).astype(f32).astype(bf16)
    count = jnp.dot(planes[...].T.astype(bf16), chosen, preferred_element_type=f32)[:ZB]
    plane = ((lane >> 3) & 3)[:ZB].astype(f32)
    share[...] = jnp.where(plane < count, 1.0 / jnp.maximum(count, 1.0), 0.0)

    chosen = (lane == row_of((index & 1) != 0)).astype(f32).astype(bf16)
    count = jnp.dot(chosen, table, preferred_element_type=f32).astype(bf16)
    wide = (LANES, NZ)
    spread = lax.broadcasted_iota(jnp.int32, wide, 1) >> 3 == lax.broadcasted_iota(jnp.int32, wide, 0)
    count = jnp.dot(count, spread.astype(f32).astype(bf16), preferred_element_type=f32)[:8]
    plane = (lax.broadcasted_iota(jnp.int32, (8, NZ), 0) >> 1).astype(f32)
    across[...] = jnp.where(plane < count, 1.0 / jnp.maximum(count, 1.0), 0.0)


def pick(blocks, o, got):
    low, high = blocks[0, o], blocks[1, o]
    a = got[:, pl.ds(pl.multiple_of(8 * lax.rem(low, 3), 8), 8), :].reshape(LANES, LANES)
    b = got[:, pl.ds(pl.multiple_of(8 * lax.rem(high, 3), 8), 8), :].reshape(LANES, LANES)
    a = jnp.where(low >= 3, turn(a, -32), a)
    b = jnp.where(high >= 3, b, turn(b, 32))
    return jnp.where(lane_bit((LANES, LANES), 32), b, a)


def pick_kernel(blocks, where, got, out1, out2, out3):
    for k, out in enumerate((out1, out2, out3)):
        out[...] = pick(blocks, (where[2] + k + 1) & 3, got)


def product_kernel(got, basis, slope, out, held):
    for wh in range(4):
        rows = swap([got[4 * wh + wl] for wl in range(4)], (64, 32))
        for y in range(4):
            held[y * 96 : y * 96 + 96, wh * LANES : wh * LANES + LANES] = rows[y]
    speed = mul(halves(held[...]), (basis[0], basis[1])).reshape(4, 2, COL, NZ)
    product = (speed[:, 1:2] * speed).reshape(384, NZ)
    inner = mul(halves(product), (slope[0], slope[1]))
    for wh in range(4):
        part = inner[:, wh * LANES : wh * LANES + LANES]
        rows = swap([part[y * 96 : y * 96 + 96] for y in range(4)], (64, 32))
        for wl in range(4):
            out[4 * wh + wl, 0:96, :] = rows[wl]
    out[:, 96:120, :] = jnp.zeros((16, 24, LANES), f32)


def bed_kernel(
    blocks, where, own, got1, got2, got3, share, across, basis, position, velocity, size,
    out, lifted, push,
    step, near, force, grid, built, lifted_held, push_held, sems,
):
    for k, got in enumerate((None, got1, got2, got3)):
        nx = (where[2] - k) & 3
        block = pick(blocks, nx, own) if k == 0 else got[...]
        rows = swap([block[w * 8 : w * 8 + 8] for w in range(16)], (16, 8, 64, 32))
        step[nx] = jnp.concatenate(rows, axis=0)
    lines = jnp.concatenate(swap([step[nx] for nx in range(4)], (16, 8)), axis=1)
    speed = mul(halves(lines), (basis[0], basis[1]))
    means = []
    for q in range(4):
        parts = [
            speed[(p * 4 + q) * 8 : (p * 4 + q) * 8 + 8] * across[pl.ds(p * 2 + q % 2, 1), :]
            for p in range(BED)
        ]
        means.append((parts[0] + parts[1]) + (parts[2] + parts[3]))
    means = jnp.concatenate(means * 4, axis=0)
    for t in range(6):
        near[t * 16 : t * 16 + 16] = means[:, t * LANES : t * LANES + LANES].T.reshape(
            16, BIN, LANES
        )
    force[...] = jnp.zeros(force.shape, f32)

    offset, owned = where[0], where[1]
    lane = lax.broadcasted_iota(jnp.int32, (BIN, LANES), 1)
    slots = position.shape[1]
    bases = (0, 16, 32, slots - 16)
    spots = []
    for i, base in enumerate(bases):
        for s in range(16):
            index = offset + (base + s)
            row = (index >= ZB).astype(jnp.int32)
            spots.append((index - ZB * row, row))
            cells = near[index - ZB * row]
            for c in range(2):
                cell = pltpu.roll(cells, (s * 8 - c * 16 - row * 8) & (LANES - 1), 1)
                at = s * 16 + c * 8
                grid[i, at : at + 8, :] = jnp.where(lane >> 3 == s, cell, 0.0)

    centre = lax.broadcasted_iota(jnp.int32, (16, BIN, LANES), 1).astype(f32) + 0.5
    spans = [slice(base, base + 16) for base in bases]
    weight_x = [jnp.exp(-0.5 * (position[0, span][:, None, :] - centre) ** 2) for span in spans]
    weight_z = [jnp.exp(-0.5 * (position[1, span][:, None, :] - centre) ** 2) for span in spans]
    flat_x = [halves(weight.reshape(LANES, LANES)) for weight in weight_x]
    part = [mul_small(halves(grid[i]), flat_x[i]).reshape(16, 2, BIN, LANES) for i in range(4)]
    pulls = []
    for i, span in enumerate(spans):
        totals = jnp.sum(weight_x[i], axis=1) * jnp.sum(weight_z[i], axis=1)
        felt = [jnp.sum(part[i][:, c] * weight_z[i], axis=1) / totals for c in range(2)]
        relative = [felt[c] - velocity[c, span] for c in range(2)]
        magnitude = jnp.sqrt(relative[0] * relative[0] + relative[1] * relative[1] + 0.1)
        diameter = size[span]
        squared = diameter * diameter
        lift = 0.5 * squared * (felt[0] * felt[0] + felt[1] * felt[1])
        active = lax.broadcasted_iota(jnp.int32, (16, LANES), 0) + bases[i] < owned
        chance = jnp.where(
            active, jax.nn.sigmoid((lift - 0.5 * squared * diameter) / 0.25), 0.0
        )
        lifted_held[span, 0, :] = chance
        pull = []
        for c in range(2):
            pushed = jnp.where(
                active, 0.5 * squared * relative[c] * magnitude * (1.0 + chance), 0.0
            )
            push_held[span, c, :] = pushed
            pull.append((-reaction * pushed / totals)[:, None, :] * weight_z[i])
        pulls.append(halves(jnp.stack(pull, axis=1).reshape(2 * LANES, LANES)))
    sent = start(
        [
            pltpu.make_async_copy(lifted_held, lifted, sems.at[0]),
            pltpu.make_async_copy(push_held, push, sems.at[1]),
        ]
    )

    shape = (2 * LANES, LANES)
    mine = lax.broadcasted_iota(jnp.int32, shape, 1) >> 3 == (
        lax.broadcasted_iota(jnp.int32, shape, 0) >> 4
    )
    for i in range(4):
        cells = mul_small(pulls[i], flat_x[i], True)
        cells = jnp.where(mine, cells, 0.0)
        for bit in (8, 16, 32, 64):
            cells = cells + turn(cells, bit)
        for s in range(16):
            spot, row = spots[i * 16 + s]
            value = jnp.where(
                lane_bit((BIN, LANES), 64),
                cells[s * 16 + 8 : s * 16 + 16],
                cells[s * 16 : s * 16 + 8],
            )
            value = jnp.where((lane >> 5) & 1 == row, value, 0.0)
            force[spot] = value * share[pl.ds(spot, 1), :]

    inner = mul_narrow((basis[0], basis[1]), halves(force[...].reshape(NZ, LANES)))
    for nx in range(4):
        rows = [inner[w * 32 + nx * 8 : w * 32 + nx * 8 + 8] for w in range(16)]
        built[nx] = jnp.concatenate(swap(rows, (64, 32, 16, 8)), axis=0).T
        sent += start([pltpu.make_async_copy(built.at[nx], out.at[nx], sems.at[2 + nx])])
    finish(sent)


def place_kernel(blocks, got, main, out):
    upper = lane_bit((LANES, LANES), 32)
    for o in range(4):
        low, high = blocks[0, o], blocks[1, o]
        value = got[o]
        a = jnp.where(upper, 0.0, value)
        b = jnp.where(upper, value, 0.0)
        a = jnp.where(low >= 3, turn(a, 32), a).reshape(16, 8, LANES)
        b = jnp.where(high >= 3, b, turn(b, -32)).reshape(16, 8, LANES)
        rows = pl.ds(pl.multiple_of(96 + 8 * lax.rem(low, 3), 8), 8)
        out[:, rows, :] = out[:, rows, :] + a
        rows = pl.ds(pl.multiple_of(96 + 8 * lax.rem(high, 3), 8), 8)
        out[:, rows, :] = out[:, rows, :] + b


def gather_kernel(got, table, out):
    block = [got[:, c * COL : c * COL + COL, :].reshape(NX, LANES) for c in range(2)]
    block = halves(jnp.concatenate(block, axis=1))
    bed = got[:, 96:120, :]
    bed = halves(jnp.concatenate([bed, turn(bed, -32)], axis=1).reshape(NX, LANES))
    first = jnp.dot(
        table[0], jnp.concatenate([block[0], *bed], axis=1), preferred_element_type=f32
    )
    second = jnp.dot(
        table[1], jnp.concatenate([block[0], bed[0]], axis=1), preferred_element_type=f32
    )
    third = jnp.dot(table[0], block[1], preferred_element_type=f32)
    main = first[:, : 2 * LANES] + (second[:, : 2 * LANES] + third)
    beds = first[:, 2 * LANES : 3 * LANES] + (first[:, 3 * LANES :] + second[:, 2 * LANES :])
    upper = lane_bit((8, LANES), 32)
    for n in range(32):
        part = main[n * 16 : n * 16 + 16]
        for c in range(2):
            out[n, c * 16 : c * 16 + 16, :] = part[:, c * LANES : c * LANES + LANES]
        bed = beds[n * 16 : n * 16 + 16]
        out[n, 32:40, :] = jnp.where(upper, turn(bed[8:16], 32), bed[0:8])


def close_kernel(
    where, got, modes, to_eigen, from_eigen, eigenvalues, out, flat, held, built, sems
):
    parts = [(c, g) for c in range(2) for g in range(4)]
    bed = [jnp.sum(got[nx * 8 : nx * 8 + 8, 32:40, :], axis=0) for nx in range(4)]
    bed = [cross(value) for value in swap(bed, (16, 8))]
    for c, g in parts:
        rows = swap([got[:, c * 16 + k, :] for k in modes_of(g)], (64, 32))
        for y in range(4):
            flat[c * 4 + g, pl.ds(y, 32, stride=4), :] = rows[y]
    for p in range(BED):
        flat[:, p, :] = flat[:, p, :] + bed[p]
    for c, g in parts:
        back = flat[c * 4 + g].T
        for i, k in enumerate(modes_of(g)):
            at = (c * 16 + k) * 32
            held[at : at + 32, :] = back[i * 32 : i * 32 + 32] + modes[c, k]
    forth, back = halves(from_eigen[...]), halves(to_eigen[...])
    sent = []
    for i in range(4):
        rows = slice(i * 256, i * 256 + 256)
        part = mul_small(halves(held[rows]), forth, True)
        row = lax.broadcasted_iota(jnp.int32, (256, LANES), 0) + i * 256
        wave_x = ((where[3] * 16 + ((row >> 5) & 15) + 1) >> 1).astype(f32)
        wave_z = ((where[4] * 32 + (row & 31) + 1) >> 1).astype(f32)
        divisor = 1.0 + viscous * (wave_x * wave_x + wave_z * wave_z + eigenvalues[...])
        result = mul_small(halves(part / divisor), back, True)
        built[i] = result.reshape(8, 32, LANES)
        block = out.at[i // 2, pl.ds(8 * (i % 2), 8)]
        sent += start([pltpu.make_async_copy(built.at[i], block, sems.at[i])])
    finish(sent)


def call(body, shape, *operands, scalars=0, scratch=(), sems=0, out_far=False, alias={}):
    spaces = [pltpu.SMEM] * scalars + [pltpu.VMEM] * (len(operands) - scalars)
    out_space = pl.BlockSpec(memory_space=pltpu.HBM if out_far else pltpu.VMEM)
    several = isinstance(shape, list)
    outs = [jax.ShapeDtypeStruct(one, f32) for one in (shape if several else [shape])]
    held = [pltpu.VMEM(one, f32) for one in scratch]
    bytes_moved = sum(4 * math.prod(one.shape) for one in list(operands) + outs)
    result = pl.pallas_call(
        body,
        out_shape=outs,
        in_specs=[pl.BlockSpec(memory_space=space) for space in spaces],
        out_specs=[out_space] * len(outs),
        scratch_shapes=held + ([pltpu.SemaphoreType.DMA((sems,))] if sems else []),
        compiler_params=pltpu.CompilerParams(vmem_limit_bytes=16 << 20),
        cost_estimate=pl.CostEstimate(
            flops=COST.get(body.__name__, 2_000_000_000), bytes_accessed=bytes_moved, transcendentals=0
        ),
        input_output_aliases=alias,
        name=body.__name__,
    )(*operands)
    return result if several else result[0]


def map_call(place, bins_owned, bed_planes):
    smem, vmem = pl.BlockSpec(memory_space=pltpu.SMEM), pl.BlockSpec(memory_space=pltpu.VMEM)
    return pl.pallas_call(
        map_kernel,
        out_shape=[
            jax.ShapeDtypeStruct((2, 4), jnp.int32),
            jax.ShapeDtypeStruct((5,), jnp.int32),
            jax.ShapeDtypeStruct((ZB, LANES), f32),
            jax.ShapeDtypeStruct((8, NZ), f32),
        ],
        in_specs=[smem, smem, vmem],
        out_specs=[smem, smem, vmem, vmem],
        scratch_shapes=[pltpu.SMEM((32,), jnp.int32), pltpu.VMEM((LANES, LANES), f32)],
        compiler_params=pltpu.CompilerParams(vmem_limit_bytes=16 << 20),
        name="map_kernel",
    )(place, bins_owned, bed_planes)


def exchange(value, axis, groups=None):
    return lax.all_to_all(value, axis, 0, 0, axis_index_groups=groups, tiled=True)


def shards(
    modes,
    to_eigen,
    from_eigen,
    eigenvalues,
    bins_owned,
    bed_planes,
    particle_position,
    particle_velocity,
    particle_size,
):
    points, basis, slope = tables()
    narrow_at = lax.axis_index("narrow")
    wide_at = lax.axis_index("wide")
    groups = [[nz + 8 * nx for nx in range(4)] for nz in range(8)]

    sent = call(open_kernel, (32, 40, LANES), modes, scratch=[(8, LANES, LANES)])
    got = exchange(sent, "narrow")
    bed = exchange(call(spread_bed_kernel, (16, 24, LANES), got, points), "wide")
    sent = call(spread_kernel, (16, 96, LANES), got, points)
    sent, bed, bins_owned, bed_planes = lax.optimization_barrier(
        (sent, bed, bins_owned, bed_planes)
    )
    grid = exchange(sent, "wide")

    blocks, where, share, across = map_call(
        jnp.stack([narrow_at, wide_at]), bins_owned, bed_planes.reshape(6, ZB)
    )

    block = (LANES, LANES)
    sent = call(pick_kernel, [block] * 3, blocks, where, bed, scalars=2)
    got = []
    for k in range(1, 4):
        hops = [(x * 8 + z, (x + k) % 4 * 8 + z) for x in range(4) for z in range(8)]
        got.append(lax.ppermute(sent[k - 1], "narrow", hops))

    count = particle_size.shape[2]
    slots, pairs = (count, 1, LANES), (count, 2, LANES)
    sent, lifted, particle_push = call(
        bed_kernel,
        [(4,) + block, slots, pairs],
        blocks,
        where,
        bed,
        *got,
        share,
        across,
        basis,
        particle_position[0, 0],
        particle_velocity[0, 0],
        particle_size[0, 0],
        scalars=2,
        scratch=[
            (4,) + block,
            (ZB, BIN, LANES),
            (ZB, BIN, LANES),
            (4, 2 * LANES, LANES),
            (4,) + block,
            slots,
            pairs,
        ],
        sems=6,
        out_far=True,
    )
    got = exchange(sent, "narrow", groups)
    inner = call(product_kernel, (16, 120, LANES), grid, basis, slope, scratch=[(384, KZ)])
    sent = call(place_kernel, (16, 120, LANES), blocks, got, inner, scalars=1, alias={2: 0})

    got = exchange(sent, "wide")
    sent = call(gather_kernel, (32, 40, LANES), got, basis)
    got = exchange(sent, "narrow")
    new_modes = call(
        close_kernel,
        modes.shape,
        where,
        got,
        modes,
        to_eigen,
        from_eigen,
        eigenvalues[None],
        scalars=1,
        scratch=[(8, LANES, LANES), (1024, LANES), (4, 8, 32, LANES)],
        sems=4,
        out_far=True,
    )
    lifted = lifted.transpose(1, 0, 2)[None]
    return (new_modes, lifted, particle_push.transpose(1, 0, 2)[None, None])


def solution(mesh):
    in_specs = (
        P(None, "narrow", "wide", None),
        P(),
        P(),
        P(),
        P("wide", None),
        P("wide"),
        P("wide", "narrow", None, None, None),
        P("wide", "narrow", None, None, None),
        P("wide", "narrow", None, None),
    )
    out_specs = (
        P(None, "narrow", "wide", None),
        P("wide", "narrow", None, None),
        P("wide", "narrow", None, None, None),
    )
    return jax.shard_map(shards, mesh=mesh, in_specs=in_specs, out_specs=out_specs, check_vma=False)
```
